32 devices in a mesh: dp: 8 (over z, y), section: 4 (over x, core).
Axes of the slice: x: 2, y: 2, z: 4, core: 2. Of those that a mesh axis runs over, the one named last changes fastest.
Arguments:
- codes: int32 [128, 128], P('dp'), may hold values from 0 to 1023
- actions: int32 [128, 21], P('dp'), may hold values from 0 to 17
- frames: bfloat16 [128, 21, 512], P('dp', None, 'section'), may hold values from -6 to 6
- segment_ids: int32 [128, 128], P('dp'), may hold values from 0 to 21, as said below
- targets: int32 [128, 128], P('dp'), may hold values from 0 to 1023
- codebook: bfloat16 [1024, 512], replicated, may hold values from -6 to 6
- action_table: bfloat16 [18, 512], replicated, may hold values from -6 to 6
- slot_table: float32 [6, 512], replicated, may hold values from -3 to 3
- ln1_gain: float32 [2, 512], replicated, may hold values from 0.5 to 1.5
- ln1_bias: float32 [2, 512], replicated, may hold values from -2 to 2
- w_qkv: bfloat16 [2, 512, 1536], replicated, may hold values from -0.25 to 0.25
- w_out: bfloat16 [2, 512, 512], replicated, may hold values from -1.5 to 1.5
- b_out: float32 [2, 512], replicated, may hold values from -2 to 2
- ln2_gain: float32 [2, 512], replicated, may hold values from 0.5 to 1.5
- ln2_bias: float32 [2, 512], replicated, may hold values from -2 to 2
- w_up: bfloat16 [2, 512, 2048], replicated, may hold values from -0.25 to 0.25
- b_up: float32 [2, 2048], replicated, may hold values from -2 to 2
- w_down: bfloat16 [2, 2048, 512], replicated, may hold values from -0.25 to 0.25
- b_down: float32 [2, 512], replicated, may hold values from -2 to 2
- lnf_gain: float32 [512], replicated, may hold values from 0.5 to 1.5
- lnf_bias: float32 [512], replicated, may hold values from -2 to 2
- w_head: bfloat16 [512, 1024], replicated, may hold values from -0.5 to 0.5
- b_head: float32 [1024], replicated, may hold values from -3 to 3
Outputs:
- grad_codebook: float32 [1024, 512], replicated
- grad_action_table: float32 [18, 512], replicated
- grad_slot_table: float32 [6, 512], replicated
- grad_ln1_gain: float32 [2, 512], replicated
- grad_ln1_bias: float32 [2, 512], replicated
- grad_w_qkv: float32 [2, 512, 1536], replicated
- grad_w_out: float32 [2, 512, 512], replicated
- grad_b_out: float32 [2, 512], replicated
- grad_ln2_gain: float32 [2, 512], replicated
- grad_ln2_bias: float32 [2, 512], replicated
- grad_w_up: float32 [2, 512, 2048], replicated
- grad_b_up: float32 [2, 2048], replicated
- grad_w_down: float32 [2, 2048, 512], replicated
- grad_b_down: float32 [2, 512], replicated
- grad_lnf_gain: float32 [512], replicated
- grad_lnf_bias: float32 [512], replicated
- grad_w_head: float32 [512, 1024], replicated
- grad_b_head: float32 [1024], replicated
- grad_frames: float32 [128, 21, 512], P('dp', None, 'section')
The draws below stay inside these ranges and needn't reach their ends.
Inputs may be any that keep to these rules, and one draw needn't show every extreme that they name: `segment_ids`: within a row the ids start at 1 and never fall, all slots of a step share one id, a step's id exceeds the previous step's by 0 or 1, and the last 2 slots of every row hold 0 and are its only zeros; some row gives every step an id of its own.
All inputs are finite; a program needn't handle non-finite values.
Results may differ from the reference program's by a relative error of at most 0.02.
Values may be sent and summed in bfloat16 or wider, within the bound.
A program may use at most 320 MiB of HBM per device.

```python
import jax
import jax.numpy as jnp
from jax import lax

D = 512
HEADS = 8
HEAD_DIM = 64
FF = 2048
CODES = 1024
ACTIONS = 18
STEPS = 21
STEP_LEN = 6
LAYERS = 2
MICRO = 4
MB_ROWS = 4
SLOTS = 128
ROWS = 128
N_DP = 8


def draw_segment_ids(key, part):
    key = jax.random.fold_in(key, 7)
    starts = jax.random.randint(key, (ROWS, STEPS), 0, 4)
    first = jnp.arange(STEPS, dtype=jnp.int32)[None, :] == 0
    every_step = jnp.arange(ROWS, dtype=jnp.int32)[:, None] == 0
    fresh = jnp.where((starts == 0) | first | every_step, 1, 0).astype(jnp.int32)
    step_ids = jnp.cumsum(fresh, axis=1).astype(jnp.int32)
    per_slot = jnp.repeat(step_ids, STEP_LEN, axis=1)
    return jnp.concatenate([per_slot, jnp.zeros((ROWS, SLOTS - STEPS * STEP_LEN), jnp.int32)], 1)


def set_ends(values, stream_key, smallest, largest):
    index_at = [jax.random.randint(jax.random.fold_in(stream_key, axis), (), 0, length) for axis, length in enumerate(values.shape)]
    widest = values.shape.index(max(values.shape))
    next_to = index_at[:widest] + [(index_at[widest] + 1) % values.shape[widest]] + index_at[widest + 1:]
    return values.at[tuple(index_at)].set(smallest).at[tuple(next_to)].set(largest)


def level_of(stream_key, dims, cuts, smallest, largest):
    level, own = 1.0, jax.random.fold_in(stream_key, 6)
    for position, shards_of in cuts:
        heights = jnp.exp(jax.random.uniform(jax.random.fold_in(own, position), (shards_of,), jnp.float32, smallest / len(cuts), largest / len(cuts)))
        level = level * jnp.repeat(heights, dims[position] // shards_of).reshape([-1 if axis == position else 1 for axis in range(len(dims))])
    return level


def bell_draw(own_key, extent, scale, bound, pieces=(), kind=jnp.bfloat16):
    values = scale * jax.random.normal(own_key, extent, jnp.float32)
    if pieces:
        values = values * level_of(own_key, extent, pieces, -0.22, 0.18)
    return jnp.clip(values, -bound, bound).astype(kind)


def setup_inputs(seed: int = 0) -> dict:
    key_list = jax.random.split(jax.random.key(seed), 24)
    codes = set_ends(jax.random.randint(key_list[0], (ROWS, SLOTS), 0, CODES), jax.random.fold_in(key_list[0], 1), 0, CODES - 1).astype(jnp.int32)
    actions = set_ends(jax.random.randint(key_list[1], (ROWS, STEPS), 0, ACTIONS), jax.random.fold_in(key_list[1], 1), 0, ACTIONS - 1).astype(jnp.int32)
    frames = bell_draw(key_list[2], (ROWS, STEPS, D), 1.0, 6.0, ((0, 8), (2, 4)))
    segment_ids = draw_segment_ids(jax.random.fold_in(key_list[23], 71), 0)
    targets = set_ends(jax.random.randint(key_list[4], (ROWS, SLOTS), 0, CODES), jax.random.fold_in(key_list[4], 1), 0, CODES - 1).astype(jnp.int32)
    codebook = bell_draw(key_list[5], (CODES, D), 1.0, 6.0)
    action_table = bell_draw(key_list[6], (ACTIONS, D), 1.0, 6.0)
    slot_table = bell_draw(key_list[7], (STEP_LEN, D), 0.5, 3.0, (), jnp.float32)
    ln1_gain = jnp.clip(1.0 + 0.1 * jax.random.normal(key_list[8], (LAYERS, D), jnp.float32), 0.5, 1.5)
    ln1_bias = bell_draw(key_list[9], (LAYERS, D), 0.3, 2.0, (), jnp.float32)
    w_qkv = bell_draw(key_list[10], (LAYERS, D, 3 * D), D ** -0.5, 0.25)
    w_out = bell_draw(key_list[11], (LAYERS, D, D), (D // 32) ** -0.5, 1.5)
    b_out = bell_draw(key_list[12], (LAYERS, D), 0.3, 2.0, (), jnp.float32)
    ln2_gain = jnp.clip(1.0 + 0.1 * jax.random.normal(key_list[13], (LAYERS, D), jnp.float32), 0.5, 1.5)
    ln2_bias = bell_draw(key_list[14], (LAYERS, D), 0.3, 2.0, (), jnp.float32)
    w_up = bell_draw(key_list[15], (LAYERS, D, FF), D ** -0.5, 0.25)
    b_up = bell_draw(key_list[16], (LAYERS, FF), 0.3, 2.0, (), jnp.float32)
    w_down = bell_draw(key_list[17], (LAYERS, FF, D), (FF // 4) ** -0.5, 0.25)
    b_down = bell_draw(key_list[18], (LAYERS, D), 0.3, 2.0, (), jnp.float32)
    lnf_gain = jnp.clip(1.0 + 0.1 * jax.random.normal(key_list[19], (D,), jnp.float32), 0.5, 1.5)
    lnf_bias = bell_draw(key_list[20], (D,), 0.3, 2.0, (), jnp.float32)
    w_head = bell_draw(key_list[21], (D, CODES), (D // 4) ** -0.5, 0.5)
    b_head = bell_draw(key_list[22], (CODES,), 0.5, 3.0, (), jnp.float32)
    return {"codes": codes, "actions": actions, "frames": frames, "segment_ids": segment_ids, "targets": targets, "codebook": codebook, "action_table": action_table, "slot_table": slot_table, "ln1_gain": ln1_gain, "ln1_bias": ln1_bias, "w_qkv": w_qkv, "w_out": w_out, "b_out": b_out, "ln2_gain": ln2_gain, "ln2_bias": ln2_bias, "w_up": w_up, "b_up": b_up, "w_down": w_down, "b_down": b_down, "lnf_gain": lnf_gain, "lnf_bias": lnf_bias, "w_head": w_head, "b_head": b_head}


@jax.custom_vjp
def low(v):
    return lax.optimization_barrier(v.astype(jnp.bfloat16)).astype(jnp.float32)

@jax.custom_vjp
def low_back(v):
    return v

def low_keep(v):
    return (low(v), None)

def low_pass(kept, grad):
    return (grad,)

def back_keep(v):
    return (v, None)

def back_low(kept, grad):
    return (low(grad),)
low.defvjp(low_keep, low_pass)
low_back.defvjp(back_keep, back_low)
HIGH = lax.Precision.HIGHEST
GELU_C = 0.7978845608028654
EPS = 1e-05
NEG = -1e+30

def gelu_value(values):
    inner = GELU_C * (values + 0.044715 * values * values * values)
    return 0.5 * values * (1.0 + jnp.tanh(inner))

def layer_norm(values, gain_vec, bias_vec):
    centred = values - lax.optimization_barrier(jnp.mean(values, -1, keepdims=True))
    inverse = lax.rsqrt(lax.optimization_barrier(jnp.mean(centred * centred, -1, keepdims=True)) + EPS)
    return centred * inverse * gain_vec + bias_vec

def boundary(values):
    return low_back(low(values))

def block_mask(seg_rows):
    slots = seg_rows.shape[1]
    step_ids = jnp.arange(slots, dtype=jnp.int32) // STEP_LEN
    same = seg_rows[:, :, None] == seg_rows[:, None, :]
    causal = step_ids[None, :] <= step_ids[:, None]
    return (same & causal[None])[:, None]

def embed_apply(code_rows, action_rows, frame_rows, tables):
    codebook, action_table, slot_table = tables
    slots = code_rows.shape[1]
    slot_ids = jnp.arange(slots, dtype=jnp.int32)
    phase = slot_ids % STEP_LEN
    step_ids = jnp.minimum(slot_ids // STEP_LEN, STEPS - 1)
    real = slot_ids < STEPS * STEP_LEN
    is_code = (real & (phase >= 2))[None, :, None]
    is_action = (real & (phase == 0))[None, :, None]
    is_frame = (real & (phase == 1))[None, :, None]
    code_part = jnp.where(is_code, codebook[code_rows], 0.0)
    action_part = jnp.where(is_action, action_table[action_rows[:, step_ids]], 0.0)
    frame_part = jnp.where(is_frame, frame_rows[:, step_ids], 0.0)
    return code_part + action_part + frame_part + slot_table[phase][None]

def layer_apply(inputs, weights, allowed):
    gain_one, bias_one, w_qkv, w_out, b_out, gain_two, bias_two, w_up, b_up, w_down, b_down = weights
    rows, slots, width = inputs.shape
    normed = low(layer_norm(inputs, gain_one, bias_one))
    joined = jnp.einsum('rsd,de->rse', normed, w_qkv, precision=HIGH)
    heads = joined.reshape(rows, slots, 3, HEADS, width // HEADS)
    query = low_back(low(heads[:, :, 0]))
    keys = low_back(low(heads[:, :, 1]))
    values = low_back(low(heads[:, :, 2]))
    scores = low_back(jnp.einsum('rqhd,rkhd->rhqk', query, keys, precision=HIGH) * HEAD_DIM ** (-0.5))
    scores = jnp.where(allowed, scores, NEG)
    top = lax.optimization_barrier(jnp.max(scores, -1, keepdims=True))
    expo = jnp.exp(scores - top)
    probs = low(expo / lax.optimization_barrier(jnp.sum(expo, -1, keepdims=True)))
    mixed = jnp.einsum('rhqk,rkhd->rqhd', probs, values, precision=HIGH).reshape(rows, slots, width)
    mixed = low_back(low(mixed))
    attended = low_back(jnp.einsum('rsd,de->rse', mixed, w_out, precision=HIGH) + b_out)
    resid = inputs + attended
    second = low(layer_norm(resid, gain_two, bias_two))
    pre_act = low_back(jnp.einsum('rsd,df->rsf', second, w_up, precision=HIGH) + b_up)
    hidden = low(gelu_value(pre_act))
    return resid + jnp.einsum('rsf,fd->rsd', hidden, w_down, precision=HIGH) + b_down

def head_loss(inputs, target_rows, seg_rows, head_weights):
    gain_vec, bias_vec, w_head, b_head = head_weights
    slots = inputs.shape[1]
    normed = low(layer_norm(inputs, gain_vec, bias_vec))
    logits = low_back(jnp.einsum('rsd,dc->rsc', normed, w_head, precision=HIGH) + b_head)
    top = lax.optimization_barrier(jnp.max(logits, -1, keepdims=True))
    total = jnp.log(lax.optimization_barrier(jnp.sum(jnp.exp(logits - top), -1))) + top[..., 0]
    picked = jnp.take_along_axis(logits, target_rows[..., None], -1)[..., 0]
    phase = jnp.arange(slots, dtype=jnp.int32) % STEP_LEN
    chosen = (seg_rows != 0) & (phase >= 1)[None] & (phase <= 4)[None]
    weight = jnp.where(chosen, 1.0, 0.0) / (4 * STEPS)
    return jnp.sum(weight * (total - picked))

def reference(codes, actions, frames, segment_ids, targets, codebook, action_table, slot_table, ln1_gain, ln1_bias, w_qkv, w_out, b_out, ln2_gain, ln2_bias, w_up, b_up, w_down, b_down, lnf_gain, lnf_bias, w_head, b_head):
    floats = tuple((item.astype(jnp.float32) for item in (codebook, action_table, slot_table, ln1_gain, ln1_bias, w_qkv, w_out, b_out, ln2_gain, ln2_bias, w_up, b_up, w_down, b_down, lnf_gain, lnf_bias, w_head, b_head)))
    group_rows = MICRO * MB_ROWS

    def regroup(array):
        return array.reshape((N_DP, group_rows) + array.shape[1:])

    def total_loss(params, frame_values):
        tables = params[0:3]
        stacked = params[3:14]
        head_weights = params[14:18]

        def group_loss(carry, batch):
            code_rows, action_rows, frame_rows, seg_rows, target_rows = batch
            allowed = block_mask(seg_rows)
            hidden = boundary(embed_apply(code_rows, action_rows, frame_rows, tables))
            for layer_index in range(LAYERS):
                weights = tuple((item[layer_index] for item in stacked))
                hidden = boundary(layer_apply(hidden, weights, allowed))
            return (carry + head_loss(hidden, target_rows, seg_rows, head_weights), None)
        loss, unused = lax.scan(jax.checkpoint(group_loss), jnp.zeros((), jnp.float32), (regroup(codes), regroup(actions), regroup(frame_values), regroup(segment_ids), regroup(targets)))
        return loss
    loss, pullback = jax.vjp(total_loss, floats, frames.astype(jnp.float32))
    grads, frame_grad = pullback(jnp.ones((), jnp.float32))
    return (grads[0], grads[1], grads[2], grads[3], grads[4], grads[5], grads[6], grads[7], grads[8], grads[9], grads[10], grads[11], grads[12], grads[13], grads[14], grads[15], grads[16], grads[17], frame_grad)
```

```python
import functools
from types import SimpleNamespace

import jax
import jax.numpy as jnp
from jax import lax
from jax.experimental import pallas as pl
from jax.experimental.pallas import tpu as pltpu
from jax.sharding import PartitionSpec as P

HEADS = 8
HEAD_DIM = 64
STEPS = 21
STEP_LEN = 6
GELU_C = 0.7978845608028654
EPS = 1e-05
NEG = -1e30
BF = jnp.bfloat16
F32 = jnp.float32
LANES = 128
BLOCK = 512
SMALL_ROWS = 64
SMALL_BLOCK = 256
QKV, OUT, UP, DOWN = 0, 3, 4, 8
VMEM_LIMIT = 63 * 2**20
MESH = pl.DeviceIdType.MESH


def dot_nn(left, right):
    return lax.dot_general(left, right, (((1,), (0,)), ((), ())), preferred_element_type=F32)


def dot_nt(left, right):
    return lax.dot_general(left, right, (((1,), (1,)), ((), ())), preferred_element_type=F32)


def dot_tn(left, right):
    return lax.dot_general(left, right, (((0,), (0,)), ((), ())), preferred_element_type=F32)


def dot_exact(left, right):
    return lax.dot_general(
        left,
        right,
        (((1,), (0,)), ((), ())),
        precision=lax.Precision.HIGHEST,
        preferred_element_type=F32,
    )


def gelu_both(values):
    squared = values * values
    tanh_part = jnp.tanh(GELU_C * values * (1.0 + 0.044715 * squared))
    half = 0.5 * (1.0 + tanh_part)
    inner_slope = GELU_C * (1.0 + 3 * 0.044715 * squared)
    slope = half + 0.5 * values * (1.0 - tanh_part * tanh_part) * inner_slope
    return (values * half, slope)


def iota(shape, dimension):
    return lax.broadcasted_iota(jnp.int32, shape, dimension)


def step_of(slots):
    return (slots * 43) >> 8


def lane_wide(column):
    return jnp.broadcast_to(column, (column.shape[0], LANES))


def columns_of(column, width):
    return jnp.concatenate([column] * (width // LANES), axis=1)


def norm_chunk(values, gain, bias):
    width = values.shape[1]
    centred = values - jnp.sum(values, -1, keepdims=True) * (1.0 / width)
    inverse = lax.rsqrt(jnp.sum(centred * centred, -1, keepdims=True) * (1.0 / width) + EPS)
    hat = centred * inverse
    return (hat * gain + bias, hat, inverse)


def norm_back_chunk(upstream, hat, inverse, gain):
    width = upstream.shape[1]
    scaled = upstream * gain
    mean_scaled = jnp.sum(scaled, -1, keepdims=True) * (1.0 / width)
    mean_prod = jnp.sum(scaled * hat, -1, keepdims=True) * (1.0 / width)
    inner = scaled - mean_scaled - hat * mean_prod
    return (
        columns_of(inverse, width) * inner,
        jnp.sum(upstream * hat, 0, keepdims=True),
        jnp.sum(upstream, 0, keepdims=True),
    )


ACTION_ROWS = 32
VECTOR_ROWS = 24


def compute(refs):
    tick = refs.tick
    codes, actions, segs, targets = refs.codes, refs.actions, refs.segs, refs.targets
    own = refs.own
    rows, slots = refs.rows, codes.shape[1]
    tokens = rows * slots
    width = refs.width
    layers = refs.layers
    ff = refs.ff
    classes = refs.classes
    n_codes = refs.n_codes
    wait_weight = refs.wait_weight
    put = refs.put
    chunk = LANES

    def chunks(body):
        def step(i, carry):
            body(pl.multiple_of(i * chunk, chunk))
            return carry

        lax.fori_loop(0, tokens // chunk, step, 0)

    first = own * rows
    slot_row = iota((rows, slots), 1)
    step_row = step_of(slot_row)
    phase_row = slot_row - step_row * STEP_LEN
    real = slot_row < STEPS * STEP_LEN
    spread = (
        (step_of(iota((STEPS, slots), 1)) == iota((STEPS, slots), 0))
        & (iota((STEPS, slots), 1) == STEP_LEN * iota((STEPS, slots), 0))
    ).astype(F32)
    action_row = dot_exact(actions[pl.ds(first, rows), :].astype(F32), spread)
    code_row = codes[pl.ds(first, rows), :].astype(F32)
    index_row = jnp.where(
        real & (phase_row >= 2),
        code_row,
        jnp.where(real & (phase_row == 0), action_row + float(n_codes), -1.0),
    )
    seg_row = segs[pl.ds(first, rows), :].astype(F32)
    target_row = targets[pl.ds(first, rows), :].astype(F32)
    stacked = jnp.concatenate(
        [index_row, seg_row, target_row, jnp.zeros((slots - 3 * rows, slots), F32)], 0
    )
    refs.int_rows[...] = stacked
    refs.int_cols[...] = jnp.transpose(stacked)
    int_rows, int_cols = refs.int_rows, refs.int_cols

    q_step = step_of(iota((slots, slots), 0))
    k_step = step_of(iota((slots, slots), 1))
    for r in range(rows):
        same = int_cols[:, rows + r : rows + r + 1] == int_rows[rows + r : rows + r + 1, :]
        refs.bias[r] = jnp.where(same & (k_step <= q_step), 0.0, NEG)

    phase_col = iota((slots, 8), 0) - STEP_LEN * step_of(iota((slots, 8), 0))
    slot_one = (phase_col == iota((slots, 8), 1)).astype(F32)
    table = jnp.concatenate([refs.slot_table[...], jnp.zeros((8 - STEP_LEN, width), F32)], 0)
    slot_part = dot_exact(slot_one, table)
    h = refs.h
    refs.wait_codebook()
    n_actions = refs.action_table.shape[0]
    action_table = jnp.concatenate(
        [
            refs.action_table[...].astype(F32),
            jnp.zeros((ACTION_ROWS - n_actions, width), F32),
        ],
        0,
    ).astype(BF)
    refs.wait_frames()
    frames = refs.frames
    sections, steps, rows_dev, frame_width = frames.shape
    n_all = steps * rows_dev
    for r in range(rows):
        tok = slice(r * slots, (r + 1) * slots)
        col = int_cols[:, r : r + 1]
        one = (col == iota((slots, n_codes), 1).astype(F32)).astype(BF)
        part = dot_nn(one, refs.codebook[...])
        one = (col == (iota((slots, ACTION_ROWS), 1) + n_codes).astype(F32)).astype(BF)
        part = part + dot_nn(one, action_table)
        j = iota((slots, n_all), 0)
        js = step_of(j)
        frame_one = (
            (iota((slots, n_all), 1) == js * rows_dev + first + r)
            & (j - js * STEP_LEN == 1)
            & (j < STEPS * STEP_LEN)
        ).astype(BF)
        frame_part = jnp.concatenate(
            [
                dot_nn(frame_one, frames[s].reshape(n_all, frame_width))
                for s in range(sections)
            ],
            1,
        )
        h[tok, :] = (part + frame_part + slot_part).astype(BF)
    refs.load_head()

    lane = iota((slots, LANES), 1)
    low_half = lane < HEAD_DIM
    pairs = HEADS // 2

    def both_heads(tile):
        zero = jnp.zeros_like(tile)
        return jnp.concatenate(
            [jnp.where(low_half, tile, zero), jnp.where(low_half, zero, tile)], 0
        )

    def pick_heads(stacked_pair):
        return jnp.where(low_half, stacked_pair[:slots], stacked_pair[slots:])

    def row_blocks(body):
        def step(r, carry):
            body(r, pl.multiple_of(r * slots, slots))
            return carry

        lax.fori_loop(0, rows, step, 0)

    def block_of(weights, j):
        return weights[pl.ds(j * BLOCK, BLOCK), :]

    def back_through(given, weights, first_block, count):
        for j in range(count):
            part = dot_nt(
                given[:, j * BLOCK : (j + 1) * BLOCK], block_of(weights, first_block + j)
            )
            big[...] = part if j == 0 else big[...] + part

    big = refs.big
    x1 = refs.x1
    normal = refs.dx1r
    for layer in range(layers):
        qkv, probs, o = (k.at[layer] for k in (refs.qkv, refs.probs, refs.o))
        hat1, inv1, hat2, inv2 = (
            k.at[layer] for k in (refs.hat1, refs.inv1, refs.hat2, refs.inv2)
        )
        m, slope = (k.at[layer] for k in (refs.m, refs.slope))
        gain1, bias1 = refs.ln1_gain[layer : layer + 1, :], refs.ln1_bias[layer : layer + 1, :]
        gain2, bias2 = refs.ln2_gain[layer : layer + 1, :], refs.ln2_bias[layer : layer + 1, :]

        def norm_one(at):
            normed, hat, inverse = norm_chunk(h[pl.ds(at, chunk), :].astype(F32), gain1, bias1)
            normal[pl.ds(at, chunk), :] = normed.astype(BF)
            hat1[pl.ds(at, chunk), :] = hat.astype(BF)
            inv1[pl.ds(at, chunk), :] = lane_wide(inverse)

        chunks(norm_one)
        weights = refs.weights[layer]
        wait_weight(layer, QKV, 3)

        def project(j, carry):
            at = pl.ds(pl.multiple_of(j * BLOCK, BLOCK), BLOCK)
            qkv[:, at] = dot_nn(normal[...], block_of(weights, QKV + j)).astype(BF)
            return carry

        lax.fori_loop(0, 3 * width // BLOCK, project, 0)

        def attend(r, at):
            tok = pl.ds(at, slots)
            bias = refs.bias[r]
            bias_two = jnp.concatenate([bias, bias], 1)
            for pair in range(pairs):
                lo = pair * LANES
                query = qkv[tok, lo : lo + LANES]
                keys = both_heads(qkv[tok, width + lo : width + lo + LANES])
                values = both_heads(qkv[tok, 2 * width + lo : 2 * width + lo + LANES])
                s = dot_nt(query, keys) * HEAD_DIM ** (-0.5) + bias_two
                parts = []
                for half in (s[:, :slots], s[:, slots:]):
                    top = jnp.max(half, -1, keepdims=True)
                    expo = jnp.exp(half - top)
                    total = jnp.sum(expo, -1, keepdims=True)
                    parts.append((expo * (1.0 / total)).astype(BF))
                p = jnp.concatenate(parts, 1)
                probs[r, pair] = p
                o[tok, lo : lo + LANES] = dot_nn(p, values).astype(BF)

        row_blocks(attend)
        wait_weight(layer, OUT, 1)
        x1[...] = dot_nn(o[...], block_of(weights, OUT))
        b_out = refs.b_out[layer : layer + 1, :]

        def norm_two(at):
            tok = pl.ds(at, chunk)
            resid = h[tok, :].astype(F32) + x1[tok, :] + b_out
            x1[tok, :] = resid
            normed, hat, inverse = norm_chunk(resid, gain2, bias2)
            normal[tok, :] = normed.astype(BF)
            hat2[tok, :] = hat.astype(BF)
            inv2[tok, :] = lane_wide(inverse)

        chunks(norm_two)
        wait_weight(layer, UP, ff // BLOCK)
        b_up = refs.b_up

        def feed(j, carry):
            at = pl.ds(pl.multiple_of(j * BLOCK, BLOCK), BLOCK)
            u = dot_nn(normal[...], block_of(weights, UP + j)) + b_up[layer : layer + 1, at]
            hidden, bent = gelu_both(u)
            m[:, at] = hidden.astype(BF)
            slope[:, at] = bent.astype(BF)
            return carry

        lax.fori_loop(0, ff // BLOCK, feed, 0)
        b_down = refs.b_down[layer : layer + 1, :]
        wait_weight(layer, DOWN, ff // BLOCK)
        w_down = weights[DOWN * BLOCK : DOWN * BLOCK + ff, :]
        h[...] = (x1[...] + dot_nn(m[...], w_down) + b_down).astype(BF)

    gain, bias_f = refs.lnf_gain[...], refs.lnf_bias[...]
    f, hatf, invf, dz = refs.dx1r, refs.x1, refs.invf, refs.dz
    sums = refs.sums
    sums[...] = jnp.zeros_like(sums)

    def add_row(row, value, width_at=0):
        sums[row : row + 1, width_at : width_at + value.shape[1]] += value

    def norm_final(at):
        tok = pl.ds(at, chunk)
        normed, hat, inverse = norm_chunk(h[tok, :].astype(F32), gain, bias_f)
        f[tok, :] = normed.astype(BF)
        hatf[tok, :] = hat
        invf[tok, :] = lane_wide(inverse)

    chunks(norm_final)
    refs.wait_head()
    w_head = refs.w_head
    phase_one = iota((slots, 1), 0) - STEP_LEN * step_of(iota((slots, 1), 0))
    for r in range(rows):
        tok = slice(r * slots, (r + 1) * slots)
        logits = [
            dot_nn(f[tok, :], w_head[j * width : (j + 1) * width, :])
            for j in range(classes // BLOCK)
        ]
        logits = jnp.concatenate(logits, 1) + refs.b_head[...]
        top = jnp.max(logits, -1, keepdims=True)
        expo = jnp.exp(logits - top)
        total = jnp.sum(expo, -1, keepdims=True)
        chosen = (
            (int_cols[:, rows + r : rows + r + 1] != 0.0) & (phase_one >= 1) & (phase_one <= 4)
        )
        weight = jnp.where(chosen, 1.0 / (4 * STEPS), 0.0)
        wanted = int_cols[:, 2 * rows + r : 2 * rows + r + 1]
        hit = wanted == iota((slots, classes), 1).astype(F32)
        delta = expo * (weight / total) - jnp.where(hit, weight, 0.0)
        low = delta.astype(BF)
        dz[tok, :] = low
        part = jnp.sum(low.astype(F32), 0, keepdims=True)
        for block in range(classes // BLOCK):
            add_row(VECTOR_ROWS - 2 + block, part[:, block * BLOCK : (block + 1) * BLOCK])
    for block in range(classes // BLOCK):
        at = slice(block * BLOCK, (block + 1) * BLOCK)
        put(dot_tn(f[...], dz[:, at]))
        tick()
    back_through(dz, w_head, 0, classes // BLOCK)
    dy = h

    def final_back(at):
        tok = pl.ds(at, chunk)
        back, gain_sum, bias_sum = norm_back_chunk(
            big[tok, :], hatf[tok, :], invf[tok, :], gain
        )
        dy[tok, :] = back.astype(BF)
        add_row(VECTOR_ROWS - 4, gain_sum)
        add_row(VECTOR_ROWS - 3, bias_sum)

    chunks(final_back)
    tick()

    for layer in reversed(range(layers)):
        qkv, probs, o = (k.at[layer] for k in (refs.qkv, refs.probs, refs.o))
        hat1, inv1, hat2, inv2 = (
            k.at[layer] for k in (refs.hat1, refs.inv1, refs.hat2, refs.inv2)
        )
        m, slope = (k.at[layer] for k in (refs.m, refs.slope))
        weights = refs.weights[layer]
        gain1, gain2 = refs.ln1_gain[layer : layer + 1, :], refs.ln2_gain[layer : layer + 1, :]
        du = slope
        base = layer * 10
        dsum = jnp.zeros((1, width), F32)
        for i in range(tokens // chunk):
            dsum = dsum + jnp.sum(dy[i * chunk : (i + 1) * chunk, :].astype(F32), 0, keepdims=True)
        add_row(base + 5, dsum)

        for j in range(ff // BLOCK):
            at = slice(j * BLOCK, (j + 1) * BLOCK)
            put(dot_tn(m[:, at], dy[...]))
            tick()
        bias1, bias2 = refs.ln1_bias[layer : layer + 1, :], refs.ln2_bias[layer : layer + 1, :]

        def normal_again(hat, gain, bias):
            def one(at):
                tok = pl.ds(at, chunk)
                normal[tok, :] = (hat[tok, :].astype(F32) * gain + bias).astype(BF)

            chunks(one)

        normal_again(hat2, gain2, bias2)
        for j in range(ff // BLOCK):
            at = slice(j * BLOCK, (j + 1) * BLOCK)
            low = (dot_nt(dy[...], block_of(weights, DOWN + j)) * slope[:, at].astype(F32)).astype(BF)
            du[:, at] = low
            add_row(base + 6 + j, jnp.sum(low.astype(F32), 0, keepdims=True))
            put(dot_tn(normal[...], low))
            tick()
        back_through(du, weights, UP, ff // BLOCK)
        tick()

        dx1, dx1r = refs.x1, refs.dx1r

        def second_back(at):
            tok = pl.ds(at, chunk)
            back, gain_sum, bias_sum = norm_back_chunk(
                big[tok, :], hat2[tok, :].astype(F32), inv2[tok, :], gain2
            )
            total = dy[tok, :].astype(F32) + back
            dx1[tok, :] = total
            low = total.astype(BF)
            dx1r[tok, :] = low
            add_row(base + 3, gain_sum)
            add_row(base + 4, bias_sum)
            add_row(base + 2, jnp.sum(low.astype(F32), 0, keepdims=True))

        chunks(second_back)
        put(dot_tn(o[...], dx1r[...]))
        do = o
        do[...] = dot_nt(dx1r[...], block_of(weights, OUT)).astype(BF)
        tick()
        dqkv = qkv

        def attend_back(r, at):
            tok = pl.ds(at, slots)
            for pair in range(pairs):
                lo = pair * LANES
                query = qkv[tok, lo : lo + LANES]
                keys = both_heads(qkv[tok, width + lo : width + lo + LANES])
                values = both_heads(qkv[tok, 2 * width + lo : 2 * width + lo + LANES])
                p = probs[r, pair]
                given = do[tok, lo : lo + LANES]
                dp = dot_nt(given, values)
                dqkv[tok, 2 * width + lo : 2 * width + lo + LANES] = pick_heads(
                    dot_tn(p, given)
                ).astype(BF)
                p_f = p.astype(F32)
                parts = []
                for cut in (slice(0, slots), slice(slots, 2 * slots)):
                    prod = p_f[:, cut] * dp[:, cut]
                    total = jnp.sum(prod, -1, keepdims=True)
                    parts.append((prod - p_f[:, cut] * total).astype(BF))
                ds = jnp.concatenate(parts, 1)
                scale = HEAD_DIM ** (-0.5)
                dqkv[tok, lo : lo + LANES] = (dot_nn(ds, keys) * scale).astype(BF)
                dqkv[tok, width + lo : width + lo + LANES] = (
                    pick_heads(dot_tn(ds, query)) * scale
                ).astype(BF)

        half_rows = rows // 2
        for start in (0, half_rows):

            def some(r, carry):
                attend_back(r, pl.multiple_of(r * slots, slots))
                return carry

            lax.fori_loop(start, start + half_rows, some, 0)
            tick()
        normal_again(hat1, gain1, bias1)
        for j in range(3 * width // BLOCK):
            at = slice(j * BLOCK, (j + 1) * BLOCK)
            put(dot_tn(normal[...], dqkv[:, at]))
            tick()
        back_through(dqkv, weights, QKV, 3)
        tick()

        def first_back(at):
            tok = pl.ds(at, chunk)
            back, gain_sum, bias_sum = norm_back_chunk(
                big[tok, :], hat1[tok, :].astype(F32), inv1[tok, :], gain1
            )
            dy[tok, :] = (dx1[tok, :] + back).astype(BF)
            add_row(base + 0, gain_sum)
            add_row(base + 1, bias_sum)

        chunks(first_back)
        if layer == layers - 1:
            refs.layer_done()
        tick()

    refs.send_back()
    index_rows = jnp.concatenate([int_rows[r : r + 1, :] for r in range(rows)], 1)
    half = n_codes // 2
    for block in range(2):
        one = (index_rows == (iota((half, tokens), 0) + block * half).astype(F32)).astype(BF)
        put(dot_nn(one, dy[...]))
        tick()
    token = iota((8, tokens), 1)
    slot = token & (slots - 1)
    slot_hit = (slot - STEP_LEN * step_of(slot) == iota((8, tokens), 0)).astype(BF)
    one = (index_rows == (iota((ACTION_ROWS, tokens), 0) + n_codes).astype(F32)).astype(BF)
    sums[VECTOR_ROWS : VECTOR_ROWS + 8, :] = dot_nn(slot_hit, dy[...])
    rest = jnp.zeros((SMALL_BLOCK - SMALL_ROWS, width), F32)
    put(jnp.concatenate([dot_nn(one, dy[...]), sums[...], rest], 0))


class Exchange:
    def __init__(self, total, result, send_sems, recv_sems, own_sems, line):
        self.total, self.result = total, result
        self.own_sems = own_sems
        self.send_sems, self.recv_sems = send_sems, recv_sems
        self.line = line
        dp, section = lax.axis_index("dp"), lax.axis_index("section")
        self.z, self.y = dp // 2, dp % 2
        self.x, self.core = section // 2, section % 2
        self.bit = (
            self.x + self.core * (self.y - self.x),
            self.y + self.core * (self.x - self.y),
        )
        self.near = (
            self.device(self.x + (1 - self.core) * (1 - 2 * self.x), self.y + self.core * (1 - 2 * self.y)),
            self.device(self.x + self.core * (1 - 2 * self.x), self.y + (1 - self.core) * (1 - 2 * self.y)),
        )
        self.twin = (dp, section + 1 - 2 * self.core)
        self.corner = (dp, 3 - section)
        self.above = (dp + 2, section)
        self.below = (dp - 2, section)
        self.used = 0
        self.blocks = 0

    def device(self, x, y):
        return (self.z * 2 + y, x * 2 + self.core)

    def greet(self, barrier):
        self.signal_all(barrier)
        pl.semaphore_wait(barrier, self.neighbours())

    def neighbours(self):
        last = self.line - 1
        lines = (self.z + last - 1) // last + (2 * last - 1 - self.z) // last
        return 4 + lines

    def signal_all(self, barrier):
        for other in (self.twin, *self.near, self.corner):
            pl.semaphore_signal(barrier, inc=1, device_id=other, device_id_type=MESH)

        @pl.when(self.z < self.line - 1)
        def _():
            pl.semaphore_signal(barrier, inc=1, device_id=self.above, device_id_type=MESH)

        @pl.when(self.z > 0)
        def _():
            pl.semaphore_signal(barrier, inc=1, device_id=self.below, device_id_type=MESH)

    def copy(self, source, target, other, again=False):
        k = self.used - again
        self.used = k + 1
        return pltpu.make_async_remote_copy(
            src_ref=source,
            dst_ref=target,
            send_sem=self.send_sems.at[k],
            recv_sem=self.recv_sems.at[k],
            device_id=other,
            device_id_type=MESH,
        )

    def rows(self, ref, at, count):
        return ref.at[pl.ds(pl.multiple_of(at, 16), count)]

    def add(self, at, landing, landed, count):
        step = min(count, 64)

        def one(i, carry):
            here = pl.ds(pl.multiple_of(at + i * step, 16), step)
            there = pl.ds(pl.multiple_of(landed + i * step, 16), step)
            self.total[here, :] = (
                self.total[here, :].astype(F32) + landing[there, :].astype(F32)
            ).astype(BF)
            return carry

        lax.fori_loop(0, count // step, one, 0)

    def stages(self, start, size, kind, landing, landing_at):
        last = self.line - 1
        z = self.z
        total, result = self.total, self.result
        own_sem = self.own_sems.at[self.blocks]
        self.blocks += 1
        half = size // 2
        own = start + self.core * half
        give = start + (1 - self.core) * half
        twin_copy = self.copy(
            self.rows(total, give, half), self.rows(landing, landing_at, half), self.twin
        )
        out = []

        def begin():
            twin_copy.start()

        def twin_done():
            twin_copy.wait_recv()
            self.add(own, landing, landing_at, half)

        def swap(near, bit, base, count, landed):
            part = count // 2
            copy = self.copy(
                self.rows(total, base + (1 - bit) * part, part),
                self.rows(landing, landed, part),
                near,
            )

            def done():
                copy.wait_recv()
                self.add(base + bit * part, landing, landed, part)

            return copy, done, base + bit * part

        def spread(near, base, count):
            here = self.rows(result, base, count)
            return self.copy(here, here, near)

        def keep(base, count):
            return pltpu.make_async_copy(
                self.rows(total, base, count), self.rows(result, base, count), own_sem
            )

        def line_copies(base, count, landed, from_total):
            part = count // 2
            low, high = self.rows(total, base, part), self.rows(total, base + part, part)
            up = self.copy(high, self.rows(landing, landed, part), self.above)
            down = self.copy(low, self.rows(landing, landed + part, part), self.below)
            low_out, high_out = (
                self.rows(result, base, part),
                self.rows(result, base + part, part),
            )
            up_back = self.copy(low_out, low_out, self.above)
            up_first = self.copy(low, low_out, self.above, again=True) if from_total else up_back
            down_back = self.copy(high_out, high_out, self.below)
            down_first = (
                self.copy(high, high_out, self.below, again=True) if from_total else down_back
            )
            return part, up, down, up_back, down_back, up_first, down_first

        def line_first(lines):
            part, up, down, up_back, down_back, up_first, down_first = lines

            @pl.when(z == 0)
            def _():
                up.start()

            @pl.when(z == last)
            def _():
                down.start()

        def line_hop(lines, base, landed, k):
            part, up, down, up_back, down_back, up_first, down_first = lines

            @pl.when(z == k)
            def _():
                up.wait_recv()
                self.add(base + part, landing, landed, part)
                if k < last:
                    up.start()

            @pl.when(z == last - k)
            def _():
                down.wait_recv()
                self.add(base, landing, landed + part, part)
                if k < last:
                    down.start()

        def back_first(lines):
            part, up, down, up_back, down_back, up_first, down_first = lines

            @pl.when(z == 0)
            def _():
                up_first.start()

            @pl.when(z == last)
            def _():
                down_first.start()

        def back_hop(lines, k):
            part, up, down, up_back, down_back, up_first, down_first = lines

            @pl.when(z == k)
            def _():
                up_back.wait_recv()
                if k < last:
                    up_back.start()

            @pl.when(z == last - k)
            def _():
                down_back.wait_recv()
                if k < last:
                    down_back.start()

        def line_sent(lines):
            part, up, down, up_back, down_back, up_first, down_first = lines

            @pl.when(z < last)
            def _():
                up.wait_send()
                up_back.wait_send()

            @pl.when(z > 0)
            def _():
                down.wait_send()
                down_back.wait_send()

        def ends(body):
            pl.when((z == 0) | (z == last))(body)

        twin_back = spread(self.twin, own, half)
        if kind == 0:
            first, first_done, base1 = swap(self.near[0], self.bit[0], own, half, landing_at + half)
            second, second_done, base2 = swap(
                self.near[1], self.bit[1], base1, half // 2, landing_at + half + half // 2
            )
            landed = landing_at + half + half // 2 + half // 4
            lines = line_copies(base2, half // 4, landed, True)
            mine = keep(base2 + (z // last) * (half // 8), half // 8)
            second_back = spread(self.near[1], base2, half // 4)
            first_back = spread(self.near[0], base1, half // 2)

            def s1():
                twin_done()
                first.start()

            def s2():
                first_done()
                second.start()

            def s3():
                second_done()
                line_first(lines)

            out = [begin, s1, s2, s3]
            for k in range(1, last + 1):

                def hop(k=k):
                    line_hop(lines, base2, landed, k)
                    if k == last:
                        ends(mine.start)
                        back_first(lines)

                out.append(hop)
            for k in range(1, last + 1):

                def hop_back(k=k):
                    back_hop(lines, k)
                    if k == last:
                        ends(mine.wait)
                        second_back.start()

                out.append(hop_back)

            def s4():
                second_back.wait_recv()
                first_back.start()

            def s5():
                first_back.wait_recv()
                twin_back.start()

            def s6():
                twin_back.wait_recv()

            def finish():
                for copy in (twin_copy, first, second, second_back, first_back, twin_back):
                    copy.wait_send()
                line_sent(lines)

            out += [s4, s5, s6, finish]
        else:
            landed = landing_at + half
            lines = line_copies(own, half, landed, False)
            top = z // last
            base = own + top * (half // 2)
            free = landed + (1 - top) * 0 + top * (half // 2)
            first, first_done, base1 = swap(self.near[0], self.bit[0], base, half // 2, free)
            second, second_done, base2 = swap(
                self.near[1], self.bit[1], base1, half // 4, free + half // 4
            )
            mine = keep(base2, half // 8)
            here = self.rows(total, base2, half // 8)
            second_back = self.copy(here, self.rows(result, base2, half // 8), self.near[1])
            first_back = spread(self.near[0], base1, half // 4)

            def s1():
                twin_done()
                line_first(lines)

            out = [begin, s1]
            for k in range(1, last + 1):

                def hop(k=k):
                    line_hop(lines, own, landed, k)
                    if k == last:
                        ends(first.start)

                out.append(hop)

            def s2():
                @ends
                def _():
                    first_done()
                    second.start()

            def s3():
                @ends
                def _():
                    second_done()
                    second_back.start()
                    mine.start()

            def s4():
                @ends
                def _():
                    second_back.wait_recv()
                    mine.wait()
                    first_back.start()

            def s5():
                @ends
                def _():
                    first_back.wait_recv()

                back_first(lines)

            out += [s2, s3, s4, s5]
            for k in range(1, last + 1):

                def hop_back(k=k):
                    back_hop(lines, k)
                    if k == last:
                        twin_back.start()

                out.append(hop_back)

            def s6():
                twin_back.wait_recv()

            def finish():
                for copy in (twin_copy, twin_back):
                    copy.wait_send()

                @ends
                def _():
                    for copy in (first, second, second_back, first_back):
                        copy.wait_send()

                line_sent(lines)

            out += [s6, finish]
        return out


def make_plan(count, stages):
    ready = [0, 1] + [3, 4, 5, 6, 7, 8, 9, 10, 12, 15, 16, 17]
    ready += [20, 21, 22, 23, 24, 25, 26, 27, 29, 32, 33, 34, 37, 38, 39]
    ticks = 39
    lag = 4
    events = []
    for i in range(count):
        for stage in range(stages):
            events.append((max(ready[i], 0) + lag * stage, -stage, i))
    plan = [[] for _ in range(ticks)]
    for when, stage, i in sorted(events):
        while len(plan) <= when:
            plan.append([])
        plan[when].append((i, -stage))
    return plan


def make_units(layers, ff, classes, n_codes):
    count = classes // BLOCK + layers * (2 * ff // BLOCK + 4) + n_codes // BLOCK
    units = [(i * BLOCK, BLOCK) for i in range(count)]
    units.append((count * BLOCK, SMALL_BLOCK))
    return units


def gradient_kernel(names, units, kinds, plan, line, rows, *args):
    refs = SimpleNamespace(**dict(zip(names, args)))
    layers, width, ff = refs.w_up.shape
    classes, n_codes = refs.w_head.shape[1], refs.codebook.shape[0]
    layer_blocks = 4 + 2 * ff // BLOCK
    early_units = classes // BLOCK + layer_blocks
    dp, section = lax.axis_index("dp"), lax.axis_index("section")
    sections = lax.axis_size("section")

    sems = iter(range(refs.weight_sems.shape[0]))

    def load(source, target):
        copy = pltpu.make_async_copy(source, target, refs.weight_sems.at[next(sems)])
        copy.start()
        return copy

    spare = layer_blocks * BLOCK
    v_codebook = refs.late.at[spare : spare + n_codes]
    codebook_copy = load(refs.codebook, v_codebook)
    block_copies = {}
    layer_weights = [refs.first_weights, refs.late]
    for layer in range(layers):
        target = layer_weights[layer]
        for first, count, whole in (
            (QKV, 3, refs.w_qkv),
            (OUT, 1, refs.w_out),
            (UP, ff // BLOCK, refs.w_up),
        ):
            for j in range(count):
                block_copies[layer, first + j] = load(
                    whole.at[layer, :, pl.ds(j * BLOCK, BLOCK)],
                    target.at[pl.ds((first + j) * BLOCK, BLOCK)],
                )
        for j in range(ff // BLOCK):
            block_copies[layer, DOWN + j] = load(
                refs.w_down.at[layer, pl.ds(j * BLOCK, BLOCK)],
                target.at[pl.ds((DOWN + j) * BLOCK, BLOCK)],
            )
    head_place = refs.late.at[spare : spare + classes // BLOCK * width]
    head_sems = [next(sems) for _ in range(classes // BLOCK)]
    head_copies = [
        pltpu.make_async_copy(
            refs.w_head.at[:, pl.ds(j * BLOCK, BLOCK)],
            head_place.at[pl.ds(j * width, width)],
            refs.weight_sems.at[head_sems[j]],
        )
        for j in range(classes // BLOCK)
    ]

    def load_head():
        for copy in head_copies:
            copy.start()

    def wait_head():
        for copy in head_copies:
            copy.wait()


    def wait_weight(layer, first, count):
        for j in range(count):
            block_copies[layer, first + j].wait()

    exchange = None
    barrier = pltpu.get_barrier_semaphore()
    if line:
        exchange = Exchange(
            refs.total, refs.result, refs.send_sems, refs.recv_sems, refs.own_sems, line
        )
        exchange.greet(barrier)
    else:
        for step in range(1, sections):
            other = (dp, lax.rem(section + step, sections))
            pl.semaphore_signal(barrier, inc=1, device_id=other, device_id_type=MESH)
        pl.semaphore_wait(barrier, sections - 1)

    frame_copies = []
    for step in range(1, sections):
        other = lax.rem(section + step, sections)
        frame_copies.append(
            pltpu.make_async_remote_copy(
                src_ref=refs.own_frames,
                dst_ref=refs.frames.at[section],
                send_sem=refs.frame_sems.at[0, step - 1],
                recv_sem=refs.frame_sems.at[1, step - 1],
                device_id=(dp, other),
                device_id_type=MESH,
            )
        )
        frame_copies[-1].start()
    frame_here = pltpu.make_async_copy(
        refs.own_frames, refs.frames.at[section], refs.frame_sems.at[2, 0]
    )
    frame_here.start()

    def wait_frames():
        frame_here.wait()
        for copy in frame_copies:
            copy.wait()

    back_copies = []

    def send_back():
        for step in range(1, sections):
            other = lax.rem(section + step, sections)
            at = pl.ds(pl.multiple_of(other * LANES, LANES), LANES)
            back_copies.append(
                pltpu.make_async_remote_copy(
                    src_ref=refs.h.at[:, at],
                    dst_ref=refs.back.at[section],
                    send_sem=refs.frame_sems.at[3, step - 1],
                    recv_sem=refs.frame_sems.at[4, step - 1],
                    device_id=(dp, other),
                    device_id_type=MESH,
                )
            )
        at = pl.ds(pl.multiple_of(section * LANES, LANES), LANES)
        back_copies.append(
            pltpu.make_async_copy(refs.h.at[:, at], refs.back.at[section], refs.frame_sems.at[2, 1])
        )
        for copy in back_copies:
            copy.start()

    stages = []
    early_rows = early_units * BLOCK
    for i, (start, size) in enumerate(units):
        if exchange is not None:
            late = start >= early_rows
            landing = refs.late if late else refs.early
            at = start - early_rows if late else start
            stages.append(exchange.stages(start, size, kinds[i], landing, at))
    if exchange is not None:
        assert exchange.used <= refs.send_sems.shape[0]
    ticks = iter(range(10**6))
    ready = []
    freed = []

    def run(events):
        for i, stage in events:
            assert i < len(ready)
            if i >= early_units and not freed:
                lines = exchange.neighbours()
                pl.semaphore_wait(refs.free_sem, lines)
                freed.append(True)
            stages[i][stage]()

    def tick():
        if exchange is not None:
            run(plan[next(ticks)])

    def put(value):
        start, size = units[len(ready)]
        refs.total[start : start + size, :] = value.astype(BF)
        ready.append(start)

    def layer_done():
        if exchange is not None:
            exchange.signal_all(refs.free_sem)

    view = SimpleNamespace(**vars(refs))
    view.codebook, view.w_head = v_codebook, head_place
    view.weights = layer_weights
    view.own, view.rows, view.width, view.layers = section, rows, width, layers
    view.ff, view.classes, view.n_codes = ff, classes, n_codes
    view.wait_weight, view.wait_frames = wait_weight, wait_frames
    view.wait_codebook, view.wait_head = codebook_copy.wait, wait_head
    view.load_head = load_head
    view.tick, view.put, view.layer_done, view.send_back = tick, put, layer_done, send_back
    compute(view)
    if exchange is not None:
        for events in plan[next(ticks) :]:
            run(events)
        for stage in stages:
            stage[-1]()
    else:
        keep = pltpu.make_async_copy(refs.total, refs.result, refs.own_sems.at[0])
        keep.start()
        keep.wait()
    for copy in back_copies:
        copy.wait()


def convert_kernel(names, units, layers, ff, classes, n_codes, *args):
    refs = SimpleNamespace(**dict(zip(names, args)))
    depth = refs.narrow.shape[0]
    width = refs.narrow.shape[2]
    targets = []
    for j in range(classes // BLOCK):
        targets.append(refs.head.at[:, pl.ds(j * BLOCK, BLOCK)])
    for layer in reversed(range(layers)):
        for j in range(ff // BLOCK):
            targets.append(refs.down.at[layer, pl.ds(j * BLOCK, BLOCK)])
        for j in range(ff // BLOCK):
            targets.append(refs.up.at[layer, :, pl.ds(j * BLOCK, BLOCK)])
        targets.append(refs.out.at[layer])
        for j in range(3):
            targets.append(refs.qkv.at[layer, :, pl.ds(j * BLOCK, BLOCK)])
    for j in range(n_codes // BLOCK):
        targets.append(refs.table.at[pl.ds(j * BLOCK, BLOCK)])
    count = len(targets)
    loads, stores = [], []
    for i in range(count):
        start, size = units[i]
        loads.append(
            pltpu.make_async_copy(
                refs.result.at[pl.ds(start, size)], refs.narrow.at[i % depth], refs.load_sems.at[i]
            )
        )
        stores.append(
            pltpu.make_async_copy(refs.wide.at[i % depth], targets[i], refs.store_sems.at[i])
        )
    small_load = pltpu.make_async_copy(
        refs.result.at[pl.ds(units[count][0], SMALL_ROWS)], refs.tiny, refs.load_sems.at[count]
    )
    small_load.start()
    back_load = pltpu.make_async_copy(refs.back, refs.v_back, refs.load_sems.at[count + 1])
    back_load.start()
    for i in range(depth):
        loads[i].start()
    small_load.wait()
    small = refs.tiny[...].astype(F32)
    refs.action_table[...] = small[: refs.action_table.shape[0]]
    vectors = small[ACTION_ROWS:]
    refs.slot_table[...] = vectors[VECTOR_ROWS : VECTOR_ROWS + STEP_LEN]
    for layer in range(layers):
        at = slice(layer, layer + 1)
        row = layer * 10
        for k, ref in enumerate(
            (refs.ln1_gain, refs.ln1_bias, refs.b_out, refs.ln2_gain, refs.ln2_bias, refs.b_down)
        ):
            ref[at, :] = vectors[row + k : row + k + 1]
        for j in range(ff // BLOCK):
            refs.b_up[at, j * BLOCK : (j + 1) * BLOCK] = vectors[row + 6 + j : row + 7 + j]
    refs.lnf_gain[...] = vectors[VECTOR_ROWS - 4 : VECTOR_ROWS - 3]
    refs.lnf_bias[...] = vectors[VECTOR_ROWS - 3 : VECTOR_ROWS - 2]
    for j in range(classes // BLOCK):
        refs.b_head[:, j * BLOCK : (j + 1) * BLOCK] = vectors[
            VECTOR_ROWS - 2 + j : VECTOR_ROWS - 1 + j
        ]
    for i in range(count):
        loads[i].wait()
        if i >= depth:
            stores[i - depth].wait()

        def one(k, carry, slot=i % depth):
            at = pl.ds(pl.multiple_of(k * 64, 64), 64)
            refs.wide[slot, at, :] = refs.narrow[slot, at, :].astype(F32)
            return carry

        lax.fori_loop(0, BLOCK // 64, one, 0)
        stores[i].start()
        if i + depth < count:
            loads[i + depth].start()
    back_load.wait()
    sections, tokens, lanes = refs.v_back.shape
    steps, rows_dev, _ = refs.frames.shape
    rows = rows_dev // sections
    slots = tokens // rows
    total = None
    for s in range(sections):
        token = iota((steps * rows_dev, tokens), 1)
        where = iota((steps * rows_dev, tokens), 0)
        step, row = where // rows_dev, where % rows_dev
        wanted = (row - s * rows) * slots + STEP_LEN * step + 1
        mine = (row >= s * rows) & (row < (s + 1) * rows)
        hit = ((token == wanted) & mine).astype(BF)
        part = dot_nn(hit, refs.v_back[s])
        total = part if total is None else total + part
    refs.frames[...] = total.reshape(steps, rows_dev, lanes)
    for i in range(count - depth, count):
        stores[i].wait()


def body(
    codes,
    actions,
    frames,
    segment_ids,
    targets,
    codebook,
    action_table,
    slot_table,
    ln1_gain,
    ln1_bias,
    w_qkv,
    w_out,
    b_out,
    ln2_gain,
    ln2_bias,
    w_up,
    b_up,
    w_down,
    b_down,
    lnf_gain,
    lnf_bias,
    w_head,
    b_head,
):
    layers, width, ff = w_up.shape
    classes, n_codes = w_head.shape[1], codebook.shape[0]
    sections, dp_count = lax.axis_size("section"), lax.axis_size("dp")
    rows_dev, slots = codes.shape
    rows = rows_dev // sections
    tokens = rows * slots
    frames_t = jnp.transpose(frames, (1, 0, 2))
    units = make_units(layers, ff, classes, n_codes)
    line = dp_count // 2
    if sections != 4 or dp_count != 2 * line or not 2 <= line <= 4:
        line = 0
    kinds = [i % 9 % 2 for i in range(len(units))]
    plan = make_plan(len(units), 2 * line + 5)

    vmem, hbm = pl.BlockSpec(memory_space=pltpu.VMEM), pl.BlockSpec(memory_space=pl.ANY)
    small = dict(
        codes=codes,
        actions=actions,
        segs=segment_ids,
        targets=targets,
        action_table=action_table,
        slot_table=slot_table,
        ln1_gain=ln1_gain,
        ln1_bias=ln1_bias,
        b_out=b_out,
        ln2_gain=ln2_gain,
        ln2_bias=ln2_bias,
        b_down=b_down,
        b_up=b_up,
        lnf_gain=lnf_gain[None],
        lnf_bias=lnf_bias[None],
        b_head=b_head[None],
        own_frames=frames_t,
    )
    large = dict(
        codebook=codebook, w_qkv=w_qkv, w_out=w_out, w_up=w_up, w_down=w_down, w_head=w_head
    )
    total_rows = units[-1][0] + units[-1][1]
    layer_blocks = 4 + 2 * ff // BLOCK
    early_rows = (classes // BLOCK + layer_blocks) * BLOCK
    outs = dict(
        result=jax.ShapeDtypeStruct((total_rows, width), BF),
        back=jax.ShapeDtypeStruct((sections, tokens, frames.shape[2]), BF),
    )
    buffers = dict(
        qkv=((layers, tokens, 3 * width), BF),
        probs=((layers, rows, HEADS // 2, slots, 2 * slots), BF),
        o=((layers, tokens, width), BF),
        hat1=((layers, tokens, width), BF),
        inv1=((layers, tokens, LANES), F32),
        hat2=((layers, tokens, width), BF),
        inv2=((layers, tokens, LANES), F32),
        m=((layers, tokens, ff), BF),
        slope=((layers, tokens, ff), BF),
        int_rows=((slots, slots), F32),
        int_cols=((slots, slots), F32),
        bias=((rows, slots, slots), F32),
        h=((tokens, width), BF),
        x1=((tokens, width), F32),
        invf=((tokens, LANES), F32),
        dz=((tokens, classes), BF),
        sums=((ACTION_ROWS, width), F32),
        big=((tokens, width), F32),
        dx1r=((tokens, width), BF),
        frames=((sections,) + frames_t.shape, BF),
        first_weights=((layer_blocks * BLOCK, width), BF),
        late=((max(total_rows - early_rows, layer_blocks * BLOCK + n_codes), width), BF),
        early=((early_rows, width), BF),
        total=((total_rows, width), BF),
    )
    scratch = {name: pltpu.VMEM(*what) for name, what in buffers.items()}
    copies = 10 * len(units)
    scratch.update(
        weight_sems=pltpu.SemaphoreType.DMA((1 + classes // BLOCK + layers * layer_blocks,)),
        frame_sems=pltpu.SemaphoreType.DMA((5, sections)),
        own_sems=pltpu.SemaphoreType.DMA((len(units),)),
        send_sems=pltpu.SemaphoreType.DMA((copies,)),
        recv_sems=pltpu.SemaphoreType.DMA((copies,)),
        free_sem=pltpu.SemaphoreType.REGULAR,
    )
    names = tuple(small) + tuple(large) + tuple(outs) + tuple(scratch)
    result, back = pl.pallas_call(
        functools.partial(gradient_kernel, names, units, kinds, plan, line, rows),
        out_shape=tuple(outs.values()),
        in_specs=[vmem] * len(small) + [hbm] * len(large),
        out_specs=(hbm, hbm),
        scratch_shapes=list(scratch.values()),
        compiler_params=pltpu.CompilerParams(
            collective_id=0, has_side_effects=True, vmem_limit_bytes=VMEM_LIMIT
        ),
    )(*small.values(), *large.values())
    if not line:
        result = lax.psum(result, ("dp", "section"))

    depth = 6
    sources = dict(result=result, back=back)
    wide = dict(
        head=(width, classes),
        down=(layers, ff, width),
        up=(layers, width, ff),
        out=(layers, width, width),
        qkv=(layers, width, 3 * width),
        table=(n_codes, width),
        action_table=action_table.shape,
        slot_table=slot_table.shape,
        ln1_gain=(layers, width),
        ln1_bias=(layers, width),
        b_out=(layers, width),
        ln2_gain=(layers, width),
        ln2_bias=(layers, width),
        b_down=(layers, width),
        b_up=(layers, ff),
        lnf_gain=(1, width),
        lnf_bias=(1, width),
        b_head=(1, classes),
        frames=frames_t.shape,
    )
    count = len(units)
    held = dict(
        narrow=pltpu.VMEM((depth, BLOCK, width), BF),
        wide=pltpu.VMEM((depth, BLOCK, width), F32),
        tiny=pltpu.VMEM((SMALL_ROWS, width), BF),
        v_back=pltpu.VMEM(back.shape, BF),
        load_sems=pltpu.SemaphoreType.DMA((count + 2,)),
        store_sems=pltpu.SemaphoreType.DMA((count,)),
    )
    names = tuple(sources) + tuple(wide) + tuple(held)
    converted = pl.pallas_call(
        functools.partial(convert_kernel, names, units, layers, ff, classes, n_codes),
        out_shape=tuple(jax.ShapeDtypeStruct(shape, F32) for shape in wide.values()),
        in_specs=[hbm, hbm],
        out_specs=(hbm,) * 6 + (vmem,) * (len(wide) - 6),
        scratch_shapes=list(held.values()),
        compiler_params=pltpu.CompilerParams(vmem_limit_bytes=VMEM_LIMIT),
    )(result, back)

    by_name = SimpleNamespace(**dict(zip(wide, converted)))
    return (
        by_name.table,
        by_name.action_table,
        by_name.slot_table,
        by_name.ln1_gain,
        by_name.ln1_bias,
        by_name.qkv,
        by_name.out,
        by_name.b_out,
        by_name.ln2_gain,
        by_name.ln2_bias,
        by_name.up,
        by_name.b_up,
        by_name.down,
        by_name.b_down,
        by_name.lnf_gain.reshape(-1),
        by_name.lnf_bias.reshape(-1),
        by_name.head,
        by_name.b_head.reshape(-1),
        jnp.transpose(by_name.frames, (1, 0, 2)),
    )


def solution(mesh):
    placed = (
        P("dp", None),
        P("dp", None),
        P("dp", None, "section"),
        P("dp", None),
        P("dp", None),
        P(),
        P(),
        P(),
        P(),
        P(),
        P(),
        P(),
        P(),
        P(),
        P(),
        P(),
        P(),
        P(),
        P(),
        P(),
        P(),
        P(),
        P(),
    )
    return jax.shard_map(
        body,
        mesh=mesh,
        in_specs=placed,
        out_specs=(
            P(),
            P(),
            P(),
            P(),
            P(),
            P(),
            P(),
            P(),
            P(),
            P(),
            P(),
            P(),
            P(),
            P(),
            P(),
            P(),
            P(),
            P(),
            P("dp", None, "section"),
        ),
        check_vma=False,
    )
```

```python
import functools
from types import SimpleNamespace

import jax
import jax.numpy as jnp
from jax import lax
from jax.experimental import pallas as pl
from jax.experimental.pallas import tpu as pltpu
from jax.sharding import PartitionSpec as P

HEADS = 8
HEAD_DIM = 64
STEPS = 21
STEP_LEN = 6
GELU_C = 0.7978845608028654
EPS = 1e-05
NEG = -1e30
BF = jnp.bfloat16
F32 = jnp.float32
LANES = 128
BLOCK = 512
SMALL_ROWS = 64
SMALL_BLOCK = 256
STEP_PLACES = 24
QKV, OUT, UP, DOWN = 0, 3, 4, 8
VMEM_LIMIT = 63 * 2**20
MESH = pl.DeviceIdType.MESH


def dot_nn(left, right):
    return lax.dot_general(left, right, (((1,), (0,)), ((), ())), preferred_element_type=F32)


def dot_nt(left, right):
    return lax.dot_general(left, right, (((1,), (1,)), ((), ())), preferred_element_type=F32)


def dot_tn(left, right):
    return lax.dot_general(left, right, (((0,), (0,)), ((), ())), preferred_element_type=F32)


def dot_exact(left, right):
    return lax.dot_general(
        left,
        right,
        (((1,), (0,)), ((), ())),
        precision=lax.Precision.HIGHEST,
        preferred_element_type=F32,
    )


def gelu_both(values):
    squared = values * values
    tanh_part = jnp.tanh(GELU_C * values * (1.0 + 0.044715 * squared))
    half = 0.5 * (1.0 + tanh_part)
    inner_slope = GELU_C * (1.0 + 3 * 0.044715 * squared)
    slope = half + 0.5 * values * (1.0 - tanh_part * tanh_part) * inner_slope
    return (values * half, slope)


def iota(shape, dimension):
    return lax.broadcasted_iota(jnp.int32, shape, dimension)


def step_of(slots):
    return (slots * 43) >> 8


def lane_wide(column):
    return jnp.broadcast_to(column, (column.shape[0], LANES))


def columns_of(column, width):
    return jnp.concatenate([column] * (width // LANES), axis=1)


def norm_chunk(values, gain, bias):
    width = values.shape[1]
    centred = values - jnp.sum(values, -1, keepdims=True) * (1.0 / width)
    inverse = lax.rsqrt(jnp.sum(centred * centred, -1, keepdims=True) * (1.0 / width) + EPS)
    hat = centred * inverse
    return (hat * gain + bias, hat, inverse)


def norm_back_chunk(upstream, hat, inverse, gain):
    width = upstream.shape[1]
    scaled = upstream * gain
    mean_scaled = jnp.sum(scaled, -1, keepdims=True) * (1.0 / width)
    mean_prod = jnp.sum(scaled * hat, -1, keepdims=True) * (1.0 / width)
    inner = scaled - mean_scaled - hat * mean_prod
    return (
        columns_of(inverse, width) * inner,
        jnp.sum(upstream * hat, 0, keepdims=True),
        jnp.sum(upstream, 0, keepdims=True),
    )


ACTION_ROWS = 32
VECTOR_ROWS = 24


def compute(refs):
    tick = refs.tick
    codes, actions, segs, targets = refs.codes, refs.actions, refs.segs, refs.targets
    own = refs.own
    rows, slots = refs.rows, codes.shape[1]
    tokens = rows * slots
    width = refs.width
    layers = refs.layers
    ff = refs.ff
    classes = refs.classes
    n_codes = refs.n_codes
    wait_weight = refs.wait_weight
    put = refs.put
    chunk = LANES

    def chunks(body):
        def step(i, carry):
            body(pl.multiple_of(i * chunk, chunk))
            return carry

        lax.fori_loop(0, tokens // chunk, step, 0)

    refs.wait_small()

    first = own * rows
    slot_row = iota((rows, slots), 1)
    step_row = step_of(slot_row)
    phase_row = slot_row - step_row * STEP_LEN
    real = slot_row < STEPS * STEP_LEN
    spread = (
        (step_of(iota((STEPS, slots), 1)) == iota((STEPS, slots), 0))
        & (iota((STEPS, slots), 1) == STEP_LEN * iota((STEPS, slots), 0))
    ).astype(F32)
    action_row = dot_exact(actions[pl.ds(first, rows), :].astype(F32), spread)
    code_row = codes[pl.ds(first, rows), :].astype(F32)
    index_row = jnp.where(
        real & (phase_row >= 2),
        code_row,
        jnp.where(real & (phase_row == 0), action_row + float(n_codes), -1.0),
    )
    seg_row = segs[pl.ds(first, rows), :].astype(F32)
    target_row = targets[pl.ds(first, rows), :].astype(F32)
    stacked = jnp.concatenate(
        [index_row, seg_row, target_row, jnp.zeros((slots - 3 * rows, slots), F32)], 0
    )
    refs.int_rows[...] = stacked
    refs.int_cols[...] = jnp.transpose(stacked)
    int_rows, int_cols = refs.int_rows, refs.int_cols

    k_step = step_of(iota((slots, slots), 0))
    q_step = step_of(iota((slots, slots), 1))
    for r in range(rows):
        same = int_cols[:, rows + r : rows + r + 1] == int_rows[rows + r : rows + r + 1, :]
        refs.bias[r] = jnp.where(same & (k_step <= q_step), 0.0, NEG)

    phase_col = iota((slots, 8), 0) - STEP_LEN * step_of(iota((slots, 8), 0))
    slot_one = (phase_col == iota((slots, 8), 1)).astype(F32)
    table = jnp.concatenate([refs.slot_table[...], jnp.zeros((8 - STEP_LEN, width), F32)], 0)
    slot_part = dot_exact(slot_one, table)
    h = refs.h
    refs.send_frames()
    n_actions = refs.action_table.shape[0]
    action_table = jnp.concatenate(
        [
            refs.action_table[...].astype(F32),
            jnp.zeros((ACTION_ROWS - n_actions, width), F32),
        ],
        0,
    ).astype(BF)
    refs.wait_codebook()
    x1 = refs.x1
    for r in range(rows):
        tok = slice(r * slots, (r + 1) * slots)
        col = int_cols[:, r : r + 1]
        one = (col == iota((slots, n_codes), 1).astype(F32)).astype(BF)
        part = dot_nn(one, refs.codebook[...])
        one = (col == (iota((slots, ACTION_ROWS), 1) + n_codes).astype(F32)).astype(BF)
        x1[tok, :] = part + dot_nn(one, action_table) + slot_part
    refs.wait_frames()
    frames = refs.frames
    sections, places, frame_width = frames.shape
    for r in range(rows):
        tok = slice(r * slots, (r + 1) * slots)
        j = iota((slots, places), 0)
        js = step_of(j)
        frame_one = (
            (iota((slots, places), 1) == r * STEP_PLACES + js)
            & (j - js * STEP_LEN == 1)
            & (j < STEPS * STEP_LEN)
        ).astype(BF)
        frame_part = jnp.concatenate(
            [dot_nn(frame_one, frames[k]) for k in range(sections)], 1
        )
        h[tok, :] = (x1[tok, :] + frame_part).astype(BF)
    refs.load_head()

    lane = iota((slots, LANES), 1)
    low_half = lane < HEAD_DIM
    pairs = HEADS // 2

    def both_heads(tile):
        zero = jnp.zeros_like(tile)
        return jnp.concatenate(
            [jnp.where(low_half, tile, zero), jnp.where(low_half, zero, tile)], 0
        )

    def pick_heads(stacked_pair):
        return jnp.where(low_half, stacked_pair[:slots], stacked_pair[slots:])

    def row_blocks(body):
        def step(r, carry):
            body(r, pl.multiple_of(r * slots, slots))
            return carry

        lax.fori_loop(0, rows, step, 0)

    def block_of(weights, j):
        return weights[pl.ds(j * BLOCK, BLOCK), :]

    def back_through(given, weights, first_block, count):
        for j in range(count):
            part = dot_nt(
                given[:, j * BLOCK : (j + 1) * BLOCK], block_of(weights, first_block + j)
            )
            big[...] = part if j == 0 else big[...] + part

    big = refs.big
    normal = refs.dx1r
    for layer in range(layers):
        qkv, probs, o = (k.at[layer] for k in (refs.qkv, refs.probs, refs.o))
        hat1, inv1, hat2, inv2 = (
            k.at[layer] for k in (refs.hat1, refs.inv1, refs.hat2, refs.inv2)
        )
        m, slope = (k.at[layer] for k in (refs.m, refs.slope))
        gain1, bias1 = refs.ln1_gain[layer : layer + 1, :], refs.ln1_bias[layer : layer + 1, :]
        gain2, bias2 = refs.ln2_gain[layer : layer + 1, :], refs.ln2_bias[layer : layer + 1, :]

        def norm_one(at):
            normed, hat, inverse = norm_chunk(h[pl.ds(at, chunk), :].astype(F32), gain1, bias1)
            normal[pl.ds(at, chunk), :] = normed.astype(BF)
            hat1[pl.ds(at, chunk), :] = hat.astype(BF)
            inv1[pl.ds(at, chunk), :] = lane_wide(inverse)

        chunks(norm_one)
        weights = refs.weights[layer]
        wait_weight(layer, QKV, 3)

        def project(j, carry):
            at = pl.ds(pl.multiple_of(j * BLOCK, BLOCK), BLOCK)
            qkv[:, at] = dot_nn(normal[...], block_of(weights, QKV + j)).astype(BF)
            return carry

        lax.fori_loop(0, 3 * width // BLOCK, project, 0)

        def attend(r, at):
            tok = pl.ds(at, slots)
            bias = refs.bias[r]
            cuts = [slice(pair * LANES, (pair + 1) * LANES) for pair in range(pairs)]
            query, key, value = (
                [qkv[tok, part * width + cut.start : part * width + cut.stop] for cut in cuts]
                for part in range(3)
            )
            scores = [dot_nt(both_heads(key[i]), query[i]) for i in range(pairs)]
            weights_low = []
            for s in scores:
                parts = []
                for half in (s[:slots], s[slots:]):
                    half = half * HEAD_DIM ** (-0.5) + bias
                    top = jnp.max(half, 0, keepdims=True)
                    expo = jnp.exp(half - top)
                    total = jnp.sum(expo, 0, keepdims=True)
                    parts.append((expo * (1.0 / total)).astype(BF))
                weights_low.append(jnp.concatenate(parts, 0))
            mixed = [dot_tn(weights_low[i], both_heads(value[i])) for i in range(pairs)]
            for i in range(pairs):
                probs[r, i] = weights_low[i]
                o[tok, cuts[i]] = mixed[i].astype(BF)

        row_blocks(attend)
        wait_weight(layer, OUT, 1)
        x1[...] = dot_nn(o[...], block_of(weights, OUT))
        b_out = refs.b_out[layer : layer + 1, :]

        def norm_two(at):
            tok = pl.ds(at, chunk)
            resid = h[tok, :].astype(F32) + x1[tok, :] + b_out
            x1[tok, :] = resid
            normed, hat, inverse = norm_chunk(resid, gain2, bias2)
            normal[tok, :] = normed.astype(BF)
            hat2[tok, :] = hat.astype(BF)
            inv2[tok, :] = lane_wide(inverse)

        chunks(norm_two)
        wait_weight(layer, UP, ff // BLOCK)
        b_up = refs.b_up

        def feed(j, carry):
            at = pl.ds(pl.multiple_of(j * BLOCK, BLOCK), BLOCK)
            u = dot_nn(normal[...], block_of(weights, UP + j)) + b_up[layer : layer + 1, at]
            hidden, bent = gelu_both(u)
            m[:, at] = hidden.astype(BF)
            slope[:, at] = bent.astype(BF)
            return carry

        lax.fori_loop(0, ff // BLOCK, feed, 0)
        b_down = refs.b_down[layer : layer + 1, :]
        wait_weight(layer, DOWN, ff // BLOCK)
        w_down = weights[DOWN * BLOCK : DOWN * BLOCK + ff, :]
        h[...] = (x1[...] + dot_nn(m[...], w_down) + b_down).astype(BF)

    gain, bias_f = refs.lnf_gain[...], refs.lnf_bias[...]
    f, hatf, invf, dz = refs.dx1r, refs.x1, refs.invf, refs.dz
    sums = refs.sums
    sums[...] = jnp.zeros_like(sums)

    def add_row(row, value, width_at=0):
        sums[row : row + 1, width_at : width_at + value.shape[1]] += value

    def norm_final(at):
        tok = pl.ds(at, chunk)
        normed, hat, inverse = norm_chunk(h[tok, :].astype(F32), gain, bias_f)
        f[tok, :] = normed.astype(BF)
        hatf[tok, :] = hat
        invf[tok, :] = lane_wide(inverse)

    chunks(norm_final)
    refs.wait_head()
    w_head = refs.w_head
    phase_one = iota((slots, 1), 0) - STEP_LEN * step_of(iota((slots, 1), 0))
    for r in range(rows):
        tok = slice(r * slots, (r + 1) * slots)
        logits = [
            dot_nn(f[tok, :], w_head[j * width : (j + 1) * width, :])
            for j in range(classes // BLOCK)
        ]
        logits = jnp.concatenate(logits, 1) + refs.b_head[...]
        top = jnp.max(logits, -1, keepdims=True)
        expo = jnp.exp(logits - top)
        total = jnp.sum(expo, -1, keepdims=True)
        chosen = (
            (int_cols[:, rows + r : rows + r + 1] != 0.0) & (phase_one >= 1) & (phase_one <= 4)
        )
        weight = jnp.where(chosen, 1.0 / (4 * STEPS), 0.0)
        wanted = int_cols[:, 2 * rows + r : 2 * rows + r + 1]
        hit = wanted == iota((slots, classes), 1).astype(F32)
        delta = expo * (weight / total) - jnp.where(hit, weight, 0.0)
        low = delta.astype(BF)
        dz[tok, :] = low
        part = jnp.sum(low.astype(F32), 0, keepdims=True)
        for block in range(classes // BLOCK):
            add_row(VECTOR_ROWS - 2 + block, part[:, block * BLOCK : (block + 1) * BLOCK])
    for block in range(classes // BLOCK):
        at = slice(block * BLOCK, (block + 1) * BLOCK)
        put(dot_tn(f[...], dz[:, at]))
        tick()
    back_through(dz, w_head, 0, classes // BLOCK)
    dy = h

    def final_back(at):
        tok = pl.ds(at, chunk)
        back, gain_sum, bias_sum = norm_back_chunk(
            big[tok, :], hatf[tok, :], invf[tok, :], gain
        )
        dy[tok, :] = back.astype(BF)
        add_row(VECTOR_ROWS - 4, gain_sum)
        add_row(VECTOR_ROWS - 3, bias_sum)

    chunks(final_back)
    tick()

    for layer in reversed(range(layers)):
        qkv, probs, o = (k.at[layer] for k in (refs.qkv, refs.probs, refs.o))
        hat1, inv1, hat2, inv2 = (
            k.at[layer] for k in (refs.hat1, refs.inv1, refs.hat2, refs.inv2)
        )
        m, slope = (k.at[layer] for k in (refs.m, refs.slope))
        weights = refs.weights[layer]
        gain1, gain2 = refs.ln1_gain[layer : layer + 1, :], refs.ln2_gain[layer : layer + 1, :]
        du = slope
        base = layer * 10
        dsum = jnp.zeros((1, width), F32)
        for i in range(tokens // chunk):
            dsum = dsum + jnp.sum(dy[i * chunk : (i + 1) * chunk, :].astype(F32), 0, keepdims=True)
        add_row(base + 5, dsum)

        for j in range(ff // BLOCK):
            at = slice(j * BLOCK, (j + 1) * BLOCK)
            put(dot_tn(m[:, at], dy[...]))
            tick()
        bias1, bias2 = refs.ln1_bias[layer : layer + 1, :], refs.ln2_bias[layer : layer + 1, :]

        def normal_again(hat, gain, bias):
            def one(at):
                tok = pl.ds(at, chunk)
                normal[tok, :] = (hat[tok, :].astype(F32) * gain + bias).astype(BF)

            chunks(one)

        normal_again(hat2, gain2, bias2)
        for j in range(ff // BLOCK):
            at = slice(j * BLOCK, (j + 1) * BLOCK)
            low = (dot_nt(dy[...], block_of(weights, DOWN + j)) * slope[:, at].astype(F32)).astype(BF)
            du[:, at] = low
            add_row(base + 6 + j, jnp.sum(low.astype(F32), 0, keepdims=True))
            put(dot_tn(normal[...], low))
            tick()
        back_through(du, weights, UP, ff // BLOCK)
        tick()

        dx1, dx1r = refs.x1, refs.dx1r

        def second_back(at):
            tok = pl.ds(at, chunk)
            back, gain_sum, bias_sum = norm_back_chunk(
                big[tok, :], hat2[tok, :].astype(F32), inv2[tok, :], gain2
            )
            total = dy[tok, :].astype(F32) + back
            dx1[tok, :] = total
            low = total.astype(BF)
            dx1r[tok, :] = low
            add_row(base + 3, gain_sum)
            add_row(base + 4, bias_sum)
            add_row(base + 2, jnp.sum(low.astype(F32), 0, keepdims=True))

        chunks(second_back)
        put(dot_tn(o[...], dx1r[...]))
        do = o
        do[...] = dot_nt(dx1r[...], block_of(weights, OUT)).astype(BF)
        tick()
        dqkv = qkv

        def attend_back(r, at):
            tok = pl.ds(at, slots)
            cuts = [slice(pair * LANES, (pair + 1) * LANES) for pair in range(pairs)]
            query, key, value = (
                [qkv[tok, part * width + cut.start : part * width + cut.stop] for cut in cuts]
                for part in range(3)
            )
            given = [do[tok, cut] for cut in cuts]
            dp = [dot_nt(both_heads(value[i]), given[i]) for i in range(pairs)]
            p = [probs[r, i] for i in range(pairs)]
            dv = [dot_nn(p[i], given[i]) for i in range(pairs)]
            ds = []
            for i in range(pairs):
                parts = []
                for cut in (slice(0, slots), slice(slots, 2 * slots)):
                    p_f = p[i][cut].astype(F32)
                    prod = p_f * dp[i][cut]
                    total = jnp.sum(prod, 0, keepdims=True)
                    parts.append((prod - p_f * total).astype(BF))
                ds.append(jnp.concatenate(parts, 0))
            scale = HEAD_DIM ** (-0.5)
            dq = [dot_tn(ds[i], both_heads(key[i])) for i in range(pairs)]
            dk = [dot_nn(ds[i], query[i]) for i in range(pairs)]
            for i in range(pairs):
                at_q, at_k, at_v = (
                    slice(part * width + cuts[i].start, part * width + cuts[i].stop)
                    for part in range(3)
                )
                dqkv[tok, at_q] = (dq[i] * scale).astype(BF)
                dqkv[tok, at_k] = (pick_heads(dk[i]) * scale).astype(BF)
                dqkv[tok, at_v] = pick_heads(dv[i]).astype(BF)

        half_rows = rows // 2
        for start in (0, half_rows):

            def some(r, carry):
                attend_back(r, pl.multiple_of(r * slots, slots))
                return carry

            lax.fori_loop(start, start + half_rows, some, 0)
            tick()
        normal_again(hat1, gain1, bias1)
        for j in range(3 * width // BLOCK):
            at = slice(j * BLOCK, (j + 1) * BLOCK)
            put(dot_tn(normal[...], dqkv[:, at]))
            tick()
        back_through(dqkv, weights, QKV, 3)
        tick()

        def first_back(at):
            tok = pl.ds(at, chunk)
            back, gain_sum, bias_sum = norm_back_chunk(
                big[tok, :], hat1[tok, :].astype(F32), inv1[tok, :], gain1
            )
            dy[tok, :] = (dx1[tok, :] + back).astype(BF)
            add_row(base + 0, gain_sum)
            add_row(base + 1, bias_sum)

        chunks(first_back)
        if layer == layers - 1:
            refs.layer_done()
        tick()

    refs.send_back()
    index_rows = jnp.concatenate([int_rows[r : r + 1, :] for r in range(rows)], 1)
    half = n_codes // 2
    for block in range(2):
        one = (index_rows == (iota((half, tokens), 0) + block * half).astype(F32)).astype(BF)
        put(dot_nn(one, dy[...]))
        tick()
    token = iota((8, tokens), 1)
    slot = token & (slots - 1)
    slot_hit = (slot - STEP_LEN * step_of(slot) == iota((8, tokens), 0)).astype(BF)
    one = (index_rows == (iota((ACTION_ROWS, tokens), 0) + n_codes).astype(F32)).astype(BF)
    sums[VECTOR_ROWS : VECTOR_ROWS + 8, :] = dot_nn(slot_hit, dy[...])
    rest = jnp.zeros((SMALL_BLOCK - SMALL_ROWS, width), F32)
    put(jnp.concatenate([dot_nn(one, dy[...]), sums[...], rest], 0))


class Exchange:
    def __init__(self, total, result, send_sems, recv_sems, own_sems, line):
        self.total, self.result = total, result
        self.own_sems, self.send_sems, self.recv_sems = own_sems, send_sems, recv_sems
        self.line = line
        dp, section = lax.axis_index("dp"), lax.axis_index("section")
        self.z, self.y = dp // 2, dp % 2
        self.x, self.core = section // 2, section % 2
        self.bit = (
            self.x + self.core * (self.y - self.x),
            self.y + self.core * (self.x - self.y),
        )
        flip_x, flip_y = 1 - 2 * self.x, 1 - 2 * self.y
        self.near = (
            self.device(self.x + (1 - self.core) * flip_x, self.y + self.core * flip_y),
            self.device(self.x + self.core * flip_x, self.y + (1 - self.core) * flip_y),
        )
        self.twin = (dp, section + 1 - 2 * self.core)
        self.corner = (dp, 3 - section)
        self.above = (dp + 2, section)
        self.below = (dp - 2, section)
        self.side = self.z // (line // 2)
        self.inner = (dp + 2 - 4 * self.side, section)
        self.outer = (dp - 2 + 4 * self.side, section)

    def device(self, x, y):
        return (self.z * 2 + y, x * 2 + self.core)

    def neighbours(self):
        last = self.line - 1
        lines = (self.z + last - 1) // last + (2 * last - 1 - self.z) // last
        return 4 + lines

    def signal_all(self, semaphore):
        for other in (self.twin, *self.near, self.corner):
            pl.semaphore_signal(semaphore, inc=1, device_id=other, device_id_type=MESH)

        @pl.when(self.z < self.line - 1)
        def _():
            pl.semaphore_signal(semaphore, inc=1, device_id=self.above, device_id_type=MESH)

        @pl.when(self.z > 0)
        def _():
            pl.semaphore_signal(semaphore, inc=1, device_id=self.below, device_id_type=MESH)

    @staticmethod
    def landing_rows(size, kind):
        half = size // 2
        return (2 * half + half // 8, 2 * half, 2 * half + 3 * half // 4 + half // 8)[kind]

    def rows(self, ref, at, count):
        return ref.at[pl.ds(pl.multiple_of(at, 16), count)]

    def add(self, at, landing, landed, count):
        step = next(rows for rows in (64, 48, 32, 16) if count % rows == 0)

        def one(i, carry):
            here = pl.ds(pl.multiple_of(at + i * step, 16), step)
            there = pl.ds(pl.multiple_of(landed + i * step, 16), step)
            self.total[here, :] = (
                self.total[here, :].astype(F32) + landing[there, :].astype(F32)
            ).astype(BF)
            return carry

        lax.fori_loop(0, count // step, one, 0)

    def stages(self, i, start, size, kind, landing, landing_at, middle):
        z, last, side = self.z, self.line - 1, self.side
        total, result = self.total, self.result
        own_sem, send_sem = self.own_sems.at[i], self.send_sems.at[i]
        first_sem = 9 * i
        half = size // 2
        own = start + self.core * half
        end = not middle

        def when(condition):
            if isinstance(condition, bool):
                return lambda body: body() if condition else None
            return lambda body: pl.when(condition)(body)

        def copy(k, source, target, other):
            return lambda: pltpu.make_async_remote_copy(
                src_ref=source,
                dst_ref=target,
                send_sem=send_sem,
                recv_sem=self.recv_sems.at[first_sem + k],
                device_id=other,
                device_id_type=MESH,
            )

        def send(*copies):
            for make in copies:
                make().start()

        def wait(*copies):
            for make in copies:
                make().wait_recv()

        def give(k, at, count, landed, other):
            return copy(k, self.rows(total, at, count), self.rows(landing, landed, count), other)

        def back(k, at, count, other, source=result):
            return copy(k, self.rows(source, at, count), self.rows(result, at, count), other)

        def keep(at, count):
            return lambda: pltpu.make_async_copy(
                self.rows(total, at, count), self.rows(result, at, count), own_sem
            )

        twin = give(0, start + (1 - self.core) * half, half, landing_at, self.twin)
        twin_back = back(8, own, half, self.twin)
        free = landing_at + half

        def twin_done():
            wait(twin)
            self.add(own, landing, landing_at, half)

        def swaps(base, count, free):
            part, bit = count // 2, self.bit
            base1 = base + bit[0] * part
            first = give(1, base + (1 - bit[0]) * part, part, free, self.near[0])
            base2 = base1 + bit[1] * (part // 2)
            second = give(
                2, base1 + (1 - bit[1]) * (part // 2), part // 2, free + part, self.near[1]
            )

            def first_done():
                wait(first)
                self.add(base1, landing, free, part)

            def second_done():
                wait(second)
                self.add(base2, landing, free + part, part // 2)

            return first, first_done, base1, second, second_done, base2

        def middle_line(base, count, free, source):
            part = count // 2
            mine, other = base + side * part, base + (1 - side) * part
            inward = give(3, base, count, free, self.inner)
            across = give(4, other, part, free + count, self.inner)
            out_mine = back(3, mine, part, self.outer, source)
            across_back = back(5, mine, part, self.inner, source)
            out_other = back(4, other, part, self.outer)

            def start_line():
                when(end)(lambda: send(inward))

            def hop():
                @when(middle)
                def _():
                    wait(inward)
                    self.add(base, landing, free, count)
                    send(across)

            def hop_done():
                wait(across)
                self.add(mine, landing, free + count, part)

            def start_back():
                send(across_back, out_mine)

            def hop_back():
                wait(across_back)
                send(out_other)

            def ends_done():
                wait(out_mine, out_other)

            return mine, start_line, hop, hop_done, start_back, hop_back, ends_done

        def line_rows(ends, others):
            def all_sent(count):
                whole = self.rows(total, 0, count)
                return lambda: pltpu.make_async_copy(whole, whole, send_sem).wait()

            def finish():
                when(end)(all_sent(ends))
                when(middle)(all_sent(others))

            return finish

        if kind == 0:
            first, first_done, base1, second, second_done, base2 = swaps(own, half, free)
            rest = half // 4
            free += half // 2 + rest
            mine, start_line, hop, hop_done, start_back, hop_back, ends_done = middle_line(
                base2, rest, free, total
            )
            mine_kept = keep(mine, rest // 2)
            second_back = back(6, base2, rest, self.near[1])
            first_back = back(7, base1, half // 2, self.near[0])

            def s1():
                twin_done()
                send(first)

            def s2():
                first_done()
                send(second)

            def s3():
                second_done()
                start_line()

            def s5():
                @when(middle)
                def _():
                    hop_done()
                    start_back()
                    mine_kept().start()

            def s6():
                @when(middle)
                def _():
                    hop_back()
                    mine_kept().wait()
                    send(second_back)

            def s7():
                @when(end)
                def _():
                    ends_done()
                    send(second_back)

            def s8():
                wait(second_back)
                send(first_back)

            def s9():
                wait(first_back)
                send(twin_back)

            def s10():
                wait(twin_back)

            finish = line_rows(3 * half + 3 * half // 4, 4 * half)
            return [lambda: send(twin), s1, s2, s3, hop, s5, s6, s7, s8, s9, s10, finish]

        if kind == 2:
            mine, start_line, hop, hop_done, start_back, hop_back, ends_done = middle_line(
                own, half, free, result
            )
            first, first_done, base1, second, second_done, base2 = swaps(
                mine, half // 2, free + half + half // 2
            )
            mine_kept = keep(base2, half // 8)
            second_back = back(6, base2, half // 8, self.near[1], total)
            first_back = back(7, base1, half // 4, self.near[0])

            def s1():
                twin_done()
                start_line()

            def s3():
                @when(middle)
                def _():
                    hop_done()
                    send(first)

            def s4():
                @when(middle)
                def _():
                    first_done()
                    send(second)

            def s5():
                @when(middle)
                def _():
                    second_done()
                    send(second_back)
                    mine_kept().start()

            def s6():
                @when(middle)
                def _():
                    wait(second_back)
                    mine_kept().wait()
                    send(first_back)

            def s7():
                @when(middle)
                def _():
                    wait(first_back)
                    start_back()

            def s8():
                @when(middle)
                def _():
                    hop_back()
                    send(twin_back)

            def s9():
                @when(end)
                def _():
                    ends_done()
                    send(twin_back)

            def s10():
                wait(twin_back)

            finish = line_rows(3 * half, 4 * half + 3 * half // 4)
            return [lambda: send(twin), s1, hop, s3, s4, s5, s6, s7, s8, s9, s10, finish]

        part = half // 2
        low, high = own, own + part
        up = give(3, high, part, free, self.above)
        down = give(4, low, part, free + part, self.below)
        up_back = back(5, low, part, self.above)
        down_back = back(3, high, part, self.below)
        first, first_done, base1, second, second_done, base2 = swaps(
            own + side * part, part, free + side * part
        )
        mine_kept = keep(base2, half // 8)
        second_back = back(6, base2, half // 8, self.near[1], total)
        first_back = back(7, base1, half // 4, self.near[0])

        def up_hop(k):
            @when((z == k) if middle == (0 < k < last) else False)
            def _():
                wait(up)
                self.add(high, landing, free, part)
                if k < last:
                    send(up)

            @when((z == last - k) if middle == (0 < k < last) else False)
            def _():
                wait(down)
                self.add(low, landing, free + part, part)
                if k < last:
                    send(down)

            if k == last:
                when(end)(lambda: send(first))

        def back_hop(k):
            @when((z == k) if middle == (0 < k < last) else False)
            def _():
                wait(up_back)
                if k < last:
                    send(up_back)

            @when((z == last - k) if middle == (0 < k < last) else False)
            def _():
                wait(down_back)
                if k < last:
                    send(down_back)

            if k == last:
                send(twin_back)

        def s1():
            twin_done()
            when((z == 0) if end else False)(lambda: send(up))
            when((z == last) if end else False)(lambda: send(down))

        def t1():
            @when(end)
            def _():
                first_done()
                send(second)

        def t2():
            @when(end)
            def _():
                second_done()
                send(second_back)
                mine_kept().start()

        def t3():
            @when(end)
            def _():
                wait(second_back)
                mine_kept().wait()
                send(first_back)

        def t4():
            when(end)(lambda: wait(first_back))
            when((z == 0) if end else False)(lambda: send(up_back))
            when((z == last) if end else False)(lambda: send(down_back))

        def t5():
            wait(twin_back)

        hops = [functools.partial(up_hop, k) for k in range(1, last + 1)]
        hops_back = [functools.partial(back_hop, k) for k in range(1, last + 1)]
        finish = line_rows(3 * half + 3 * half // 4, 4 * half)
        return [lambda: send(twin), s1, *hops, t1, t2, t3, t4, *hops_back, t5, finish]


SIZES = (512, 512, 512, 512, 1024, 512, 512, 1024, 512, 512, 1024, 512, 512, 1024, 512, 512, 512, 512, 512, 1536, 512, 768)
KINDS = (2, 0, 1, 0, 0, 1, 0, 0, 0, 1, 0, 0, 1, 0, 0, 2, 0, 0, 2, 0, 0, 0)
PLAN_ENDS = (
    (0,),
    (),
    (16,),
    (),
    (32,),
    (1, 2, 3, 4, 5, 6, 48,),
    (),
    (17, 64,),
    (80,),
    (33, 34, 35, 49,),
    (96, 65,),
    (81, 82, 83, 18,),
    (112, 97,),
    (50,),
    (128, 113,),
    (),
    (),
    (),
    (66, 19, 20, 129,),
    (),
    (144, 98,),
    (),
    (160,),
    (51, 52,),
    (),
    (145, 146, 147,),
    (176, 161, 192,),
    (114,),
    (208,),
    (224, 177, 193, 194, 195,),
    (240, 67, 68, 130, 209,),
    (256, 99, 100, 225, 272,),
    (36,),
    (241, 242, 243, 244, 245, 246,),
    (),
    (162, 257,),
    (),
    (288, 273, 115, 116,),
    (84, 21, 22,),
    (131, 132, 178,),
    (
        289, 290, 291, 292, 293, 294, 304, 210, 320, 305, 148, 37, 226, 69, 70, 336, 321, 23, 7,
        8, 163, 164, 258, 337, 196, 85, 274, 53, 54, 179, 180, 211, 212, 38, 71, 149, 55, 227,
        228, 306, 165, 166, 24, 117, 118, 259, 260, 322, 101, 102, 133, 134, 338, 197, 86, 275,
        276, 247, 248, 39, 181, 182, 72, 229, 230, 150, 56, 307, 308, 119, 213, 214, 277, 278,
        25, 323, 324, 198, 26, 87, 339, 340, 341, 342, 103, 135, 295, 296, 167, 73, 40, 41, 42,
        151, 74, 325, 326, 9, 57, 120, 183, 10, 88, 89, 90, 199, 58, 104, 215, 309, 310, 231,
        136, 279, 152, 153, 154, 168, 261, 262, 121, 184, 200, 201, 202, 327, 122, 105, 216, 43,
        343, 106, 137, 232, 44, 280, 311, 138, 169, 91, 263, 185, 170, 328, 92, 186, 217, 155,
        344, 218, 156, 233, 203, 234, 204, 281, 312, 264, 282, 249, 329, 250, 330, 345, 346,
        297, 313, 298, 265, 314, 266,
    ),
)
PLAN_MIDDLE = (
    (0,),
    (),
    (16,),
    (),
    (32,),
    (1, 48,),
    (),
    (17, 64,),
    (80,),
    (33, 49,),
    (96, 65,),
    (81, 18,),
    (112, 97,),
    (50,),
    (128, 2, 113,),
    (),
    (),
    (),
    (19, 66, 129,),
    (),
    (),
    (34, 144, 98,),
    (51,),
    (160, 3,),
    (),
    (145,),
    (82,),
    (176, 114, 192, 161,),
    (20, 35, 36, 37, 38, 39, 208,),
    (52, 177, 224,),
    (193, 67, 240, 83, 84, 85, 86, 87,),
    (130, 209, 256, 4, 99,),
    (146, 225,),
    (272,),
    (241,),
    (),
    (257,),
    (288,),
    (162, 273, 21, 115,),
    (147, 148, 149, 150, 151, 194,),
    (
        68, 178, 289, 100, 304, 22, 23, 210, 131, 5, 40, 195, 196, 197, 198, 199, 320, 226, 305,
        69, 258, 336, 242, 321, 163, 274, 337, 116, 179, 53, 70, 71, 24, 132, 243, 6, 211, 54,
        55, 290, 227, 306, 259, 322, 164, 117, 275, 291, 180, 101, 133, 338, 165, 212, 118, 119,
        228, 25, 72, 244, 7, 181, 260, 56, 26, 102, 103, 134, 135, 276, 200, 307, 166, 167, 323,
        213, 292, 88, 229, 339, 8, 9, 120, 182, 183, 10, 152, 308, 277, 73, 245, 324, 214, 215,
        230, 231, 74, 57, 104, 340, 136, 58, 278, 279, 168, 325, 293, 41, 341, 309, 121, 326,
        327, 184, 89, 122, 246, 216, 261, 42, 43, 342, 343, 44, 105, 232, 153, 310, 311, 106,
        137, 280, 138, 90, 91, 262, 263, 169, 92, 294, 201, 328, 170, 154, 155, 185, 156, 186,
        202, 203, 217, 204, 247, 218, 233, 344, 234, 312, 248, 249, 281, 250, 264, 295, 282,
        329, 330, 345, 346, 296, 297, 298, 313, 265, 314, 266,
    ),
)


def make_units(layers, ff, classes, n_codes):
    count = classes // BLOCK + layers * (2 * ff // BLOCK + 4) + n_codes // BLOCK
    units = [(i * BLOCK, BLOCK) for i in range(count)]
    units.append((count * BLOCK, SMALL_BLOCK))
    return units


def make_parts(early_rows):
    parts = []
    start = 0
    for size in SIZES:
        parts.append((start, size))
        start += size
    return parts, sum(1 for start, size in parts if start < early_rows)


def gradient_kernel(small, names, units, line, rows, *args):
    count = len(small)
    refs = SimpleNamespace(**dict(zip(names, args[count:])))
    small_copies = []
    for i, (name, source, target) in enumerate(zip(small, args[:count], args[-count:])):
        setattr(refs, name, target)
        small_copies.append(pltpu.make_async_copy(source, target, refs.small_sems.at[i]))
        small_copies[-1].start()
    layers, width, ff = refs.w_up.shape
    classes, n_codes = refs.w_head.shape[1], refs.codebook.shape[0]
    layer_blocks = 4 + 2 * ff // BLOCK
    early_units = classes // BLOCK + layer_blocks
    dp, section = lax.axis_index("dp"), lax.axis_index("section")
    sections = lax.axis_size("section")

    sems = iter(range(refs.weight_sems.shape[0]))

    def load(source, target):
        copy = pltpu.make_async_copy(source, target, refs.weight_sems.at[next(sems)])
        copy.start()
        return copy

    spare = layer_blocks * BLOCK
    v_codebook = refs.late.at[spare : spare + n_codes]
    codebook_copy = load(refs.codebook, v_codebook)
    block_copies = {}
    layer_weights = [refs.first_weights, refs.late]
    for layer in range(layers):
        target = layer_weights[layer]
        for first, count, whole in (
            (QKV, 3, refs.w_qkv),
            (OUT, 1, refs.w_out),
            (UP, ff // BLOCK, refs.w_up),
        ):
            for j in range(count):
                block_copies[layer, first + j] = load(
                    whole.at[layer, :, pl.ds(j * BLOCK, BLOCK)],
                    target.at[pl.ds((first + j) * BLOCK, BLOCK)],
                )
        for j in range(ff // BLOCK):
            block_copies[layer, DOWN + j] = load(
                refs.w_down.at[layer, pl.ds(j * BLOCK, BLOCK)],
                target.at[pl.ds((DOWN + j) * BLOCK, BLOCK)],
            )
    head_place = refs.late.at[spare : spare + classes // BLOCK * width]
    head_sems = [next(sems) for _ in range(classes // BLOCK)]
    head_copies = [
        pltpu.make_async_copy(
            refs.w_head.at[:, pl.ds(j * BLOCK, BLOCK)],
            head_place.at[pl.ds(j * width, width)],
            refs.weight_sems.at[head_sems[j]],
        )
        for j in range(classes // BLOCK)
    ]

    def load_head():
        for copy in head_copies:
            copy.start()

    def wait_head():
        for copy in head_copies:
            copy.wait()


    def wait_weight(layer, first, count):
        for j in range(count):
            block_copies[layer, first + j].wait()

    exchange = None
    barrier = pltpu.get_barrier_semaphore()
    if line:
        exchange = Exchange(
            refs.total, refs.result, refs.send_sems, refs.recv_sems, refs.own_sems, line
        )
        exchange.signal_all(barrier)
    else:
        for step in range(1, sections):
            other = (dp, lax.rem(section + step, sections))
            pl.semaphore_signal(barrier, inc=1, device_id=other, device_id_type=MESH)

    frame_copies = []
    for step in range(1, sections):
        other = lax.rem(section + step, sections)
        frame_copies.append(
            pltpu.make_async_remote_copy(
                src_ref=refs.sent_frames.at[other],
                dst_ref=refs.frames.at[section],
                send_sem=refs.frame_sems.at[0, step - 1],
                recv_sem=refs.frame_sems.at[1, step - 1],
                device_id=(dp, other),
                device_id_type=MESH,
            )
        )

    def send_frames():
        steps, rows_dev, frame_width = refs.held_frames.shape
        n_all = steps * rows_dev
        flat = refs.held_frames[...].reshape(n_all, frame_width)
        place = iota((rows * STEP_PLACES, n_all), 0)
        row = (place * 43) >> 10
        step = place - row * STEP_PLACES
        column = iota((rows * STEP_PLACES, n_all), 1)
        for other in range(sections):
            hit = (column == step * rows_dev + row + other * rows) & (step < steps)
            refs.sent_frames[other] = dot_nn(hit.astype(BF), flat).astype(BF)
        refs.frames[section] = refs.sent_frames[section]
        if exchange is not None:
            pl.semaphore_wait(barrier, exchange.neighbours())
        else:
            pl.semaphore_wait(barrier, sections - 1)
        for copy in frame_copies:
            copy.start()

    def wait_frames():
        for copy in frame_copies:
            copy.wait()

    def wait_small():
        for copy in small_copies:
            copy.wait()

    back_copies = []

    def send_back():
        for step in range(1, sections):
            other = lax.rem(section + step, sections)
            at = pl.ds(pl.multiple_of(other * LANES, LANES), LANES)
            back_copies.append(
                pltpu.make_async_remote_copy(
                    src_ref=refs.h.at[:, at],
                    dst_ref=refs.back.at[section],
                    send_sem=refs.frame_sems.at[3, step - 1],
                    recv_sem=refs.frame_sems.at[4, step - 1],
                    device_id=(dp, other),
                    device_id_type=MESH,
                )
            )
        at = pl.ds(pl.multiple_of(section * LANES, LANES), LANES)
        back_copies.append(
            pltpu.make_async_copy(refs.h.at[:, at], refs.back.at[section], refs.frame_sems.at[2, 0])
        )
        for copy in back_copies:
            copy.start()

    stages = {False: [], True: []}
    if exchange is not None:
        parts, early_parts = make_parts(early_units * BLOCK)
        for middle in stages:
            offsets = [0, 0]
            for i, (start, size) in enumerate(parts):
                late = i >= early_parts
                landing = refs.late if late else refs.early
                stages[middle].append(
                    exchange.stages(i, start, size, KINDS[i], landing, offsets[late], middle)
                )
                offsets[late] += exchange.landing_rows(size, KINDS[i])
    ticks = iter(range(10**6))
    ready = []
    freed = []
    at_end = (exchange.z == 0) | (exchange.z == line - 1) if line else None

    def run(k):
        events = PLAN_ENDS[k] + PLAN_MIDDLE[k]
        if not freed and any(event // 16 >= early_parts for event in events):
            pl.semaphore_wait(refs.free_sem, exchange.neighbours())
            freed.append(True)

        @pl.when(at_end)
        def _():
            for event in PLAN_ENDS[k]:
                stages[False][event // 16][event % 16]()

        @pl.when(jnp.logical_not(at_end))
        def _():
            for event in PLAN_MIDDLE[k]:
                stages[True][event // 16][event % 16]()

    def tick():
        if exchange is not None:
            run(next(ticks))

    def put(value):
        start, size = units[len(ready)]
        refs.total[start : start + size, :] = value.astype(BF)
        ready.append(start)

    def layer_done():
        if exchange is not None:
            exchange.signal_all(refs.free_sem)

    view = SimpleNamespace(**vars(refs))
    view.codebook, view.w_head = v_codebook, head_place
    view.weights = layer_weights
    view.own, view.rows, view.width, view.layers = section, rows, width, layers
    view.ff, view.classes, view.n_codes = ff, classes, n_codes
    view.wait_weight, view.wait_frames = wait_weight, wait_frames
    view.send_frames, view.wait_small = send_frames, wait_small
    view.wait_codebook, view.wait_head = codebook_copy.wait, wait_head
    view.load_head = load_head
    view.tick, view.put, view.layer_done, view.send_back = tick, put, layer_done, send_back
    compute(view)
    if exchange is not None:
        for k in range(next(ticks), len(PLAN_ENDS)):
            run(k)

        @pl.when(at_end)
        def _():
            for stage in stages[False]:
                stage[-1]()

        @pl.when(jnp.logical_not(at_end))
        def _():
            for stage in stages[True]:
                stage[-1]()

    else:
        keep = pltpu.make_async_copy(refs.total, refs.result, refs.own_sems.at[0])
        keep.start()
        keep.wait()
    for copy in back_copies:
        copy.wait()


def convert_kernel(names, units, layers, ff, classes, n_codes, *args):
    refs = SimpleNamespace(**dict(zip(names, args)))
    depth = refs.narrow.shape[0]
    width = refs.narrow.shape[2]
    targets = []
    for j in range(classes // BLOCK):
        targets.append(refs.head.at[:, pl.ds(j * BLOCK, BLOCK)])
    for layer in reversed(range(layers)):
        for j in range(ff // BLOCK):
            targets.append(refs.down.at[layer, pl.ds(j * BLOCK, BLOCK)])
        for j in range(ff // BLOCK):
            targets.append(refs.up.at[layer, :, pl.ds(j * BLOCK, BLOCK)])
        targets.append(refs.out.at[layer])
        for j in range(3):
            targets.append(refs.qkv.at[layer, :, pl.ds(j * BLOCK, BLOCK)])
    for j in range(n_codes // BLOCK):
        targets.append(refs.table.at[pl.ds(j * BLOCK, BLOCK)])
    count = len(targets)
    loads, stores = [], []
    for i in range(count):
        start, size = units[i]
        loads.append(
            pltpu.make_async_copy(
                refs.result.at[pl.ds(start, size)], refs.narrow.at[i % depth], refs.load_sems.at[i]
            )
        )
        stores.append(
            pltpu.make_async_copy(refs.wide.at[i % depth], targets[i], refs.store_sems.at[i])
        )
    small_load = pltpu.make_async_copy(
        refs.result.at[pl.ds(units[count][0], SMALL_ROWS)], refs.tiny, refs.load_sems.at[count]
    )
    small_load.start()
    back_load = pltpu.make_async_copy(refs.back, refs.v_back, refs.load_sems.at[count + 1])
    back_load.start()
    for i in range(depth):
        loads[i].start()
    small_load.wait()
    small = refs.tiny[...].astype(F32)
    refs.action_table[...] = small[: refs.action_table.shape[0]]
    vectors = small[ACTION_ROWS:]
    refs.slot_table[...] = vectors[VECTOR_ROWS : VECTOR_ROWS + STEP_LEN]
    for layer in range(layers):
        at = slice(layer, layer + 1)
        row = layer * 10
        for k, ref in enumerate(
            (refs.ln1_gain, refs.ln1_bias, refs.b_out, refs.ln2_gain, refs.ln2_bias, refs.b_down)
        ):
            ref[at, :] = vectors[row + k : row + k + 1]
        for j in range(ff // BLOCK):
            refs.b_up[at, j * BLOCK : (j + 1) * BLOCK] = vectors[row + 6 + j : row + 7 + j]
    refs.lnf_gain[...] = vectors[VECTOR_ROWS - 4 : VECTOR_ROWS - 3]
    refs.lnf_bias[...] = vectors[VECTOR_ROWS - 3 : VECTOR_ROWS - 2]
    for j in range(classes // BLOCK):
        refs.b_head[:, j * BLOCK : (j + 1) * BLOCK] = vectors[
            VECTOR_ROWS - 2 + j : VECTOR_ROWS - 1 + j
        ]
    for i in range(count):
        loads[i].wait()
        if i >= depth:
            stores[i - depth].wait()

        def one(k, carry, slot=i % depth):
            at = pl.ds(pl.multiple_of(k * 64, 64), 64)
            refs.wide[slot, at, :] = refs.narrow[slot, at, :].astype(F32)
            return carry

        lax.fori_loop(0, BLOCK // 64, one, 0)
        stores[i].start()
        if i + depth < count:
            loads[i + depth].start()
    back_load.wait()
    sections, tokens, lanes = refs.v_back.shape
    steps, rows_dev, _ = refs.frames.shape
    rows = rows_dev // sections
    slots = tokens // rows
    total = None
    for s in range(sections):
        token = iota((steps * rows_dev, tokens), 1)
        where = iota((steps * rows_dev, tokens), 0)
        step, row = where // rows_dev, where % rows_dev
        wanted = (row - s * rows) * slots + STEP_LEN * step + 1
        mine = (row >= s * rows) & (row < (s + 1) * rows)
        hit = ((token == wanted) & mine).astype(BF)
        part = dot_nn(hit, refs.v_back[s])
        total = part if total is None else total + part
    refs.frames[...] = total.reshape(steps, rows_dev, lanes)
    for i in range(count - depth, count):
        stores[i].wait()


def body(
    codes,
    actions,
    frames,
    segment_ids,
    targets,
    codebook,
    action_table,
    slot_table,
    ln1_gain,
    ln1_bias,
    w_qkv,
    w_out,
    b_out,
    ln2_gain,
    ln2_bias,
    w_up,
    b_up,
    w_down,
    b_down,
    lnf_gain,
    lnf_bias,
    w_head,
    b_head,
):
    layers, width, ff = w_up.shape
    classes, n_codes = w_head.shape[1], codebook.shape[0]
    sections, dp_count = lax.axis_size("section"), lax.axis_size("dp")
    rows_dev, slots = codes.shape
    rows = rows_dev // sections
    tokens = rows * slots
    frames_t = jnp.transpose(frames, (1, 0, 2))
    units = make_units(layers, ff, classes, n_codes)
    line = dp_count // 2
    if sections != 4 or dp_count != 2 * line or line != 4 or units[-1][0] + units[-1][1] != sum(SIZES):
        line = 0

    vmem, hbm = pl.BlockSpec(memory_space=pltpu.VMEM), pl.BlockSpec(memory_space=pl.ANY)
    small = dict(
        codes=codes,
        actions=actions,
        segs=segment_ids,
        targets=targets,
        action_table=action_table,
        slot_table=slot_table,
        ln1_gain=ln1_gain,
        ln1_bias=ln1_bias,
        b_out=b_out,
        ln2_gain=ln2_gain,
        ln2_bias=ln2_bias,
        b_down=b_down,
        b_up=b_up,
        lnf_gain=lnf_gain[None],
        lnf_bias=lnf_bias[None],
        b_head=b_head[None],
        held_frames=frames_t,
    )
    large = dict(
        codebook=codebook, w_qkv=w_qkv, w_out=w_out, w_up=w_up, w_down=w_down, w_head=w_head
    )
    total_rows = units[-1][0] + units[-1][1]
    layer_blocks = 4 + 2 * ff // BLOCK
    early_units = classes // BLOCK + layer_blocks
    early_rows, late_rows = 0, 0
    parts, early_parts = make_parts(early_units * BLOCK)
    for i, (start, size) in enumerate(parts):
        taken = Exchange.landing_rows(size, KINDS[i])
        early_rows, late_rows = (
            early_rows + taken * (i < early_parts),
            late_rows + taken * (i >= early_parts),
        )
    outs = dict(
        result=jax.ShapeDtypeStruct((total_rows, width), BF),
        back=jax.ShapeDtypeStruct((sections, tokens, frames.shape[2]), BF),
    )
    buffers = dict(
        qkv=((layers, tokens, 3 * width), BF),
        probs=((layers, rows, HEADS // 2, 2 * slots, slots), BF),
        o=((layers, tokens, width), BF),
        hat1=((layers, tokens, width), BF),
        inv1=((layers, tokens, LANES), F32),
        hat2=((layers, tokens, width), BF),
        inv2=((layers, tokens, LANES), F32),
        m=((layers, tokens, ff), BF),
        slope=((layers, tokens, ff), BF),
        int_rows=((slots, slots), F32),
        int_cols=((slots, slots), F32),
        bias=((rows, slots, slots), F32),
        h=((tokens, width), BF),
        x1=((tokens, width), F32),
        invf=((tokens, LANES), F32),
        dz=((tokens, classes), BF),
        sums=((ACTION_ROWS, width), F32),
        big=((tokens, width), F32),
        dx1r=((tokens, width), BF),
        frames=((sections, rows * STEP_PLACES, frames.shape[2]), BF),
        sent_frames=((sections, rows * STEP_PLACES, frames.shape[2]), BF),
        first_weights=((layer_blocks * BLOCK, width), BF),
        late=((max(late_rows, layer_blocks * BLOCK + n_codes), width), BF),
        early=((early_rows, width), BF),
        total=((total_rows, width), BF),
    )
    scratch = {name: pltpu.VMEM(*what) for name, what in buffers.items()}
    held = {name: pltpu.VMEM(array.shape, array.dtype) for name, array in small.items()}
    scratch.update(
        weight_sems=pltpu.SemaphoreType.DMA((1 + classes // BLOCK + layers * layer_blocks,)),
        frame_sems=pltpu.SemaphoreType.DMA((5, sections)),
        own_sems=pltpu.SemaphoreType.DMA((len(parts),)),
        send_sems=pltpu.SemaphoreType.DMA((len(parts),)),
        recv_sems=pltpu.SemaphoreType.DMA((9 * len(parts),)),
        free_sem=pltpu.SemaphoreType.REGULAR,
        small_sems=pltpu.SemaphoreType.DMA((len(small),)),
    )
    names = tuple(large) + tuple(outs) + tuple(scratch)
    result, back = pl.pallas_call(
        functools.partial(gradient_kernel, tuple(small), names, units, line, rows),
        out_shape=tuple(outs.values()),
        in_specs=[hbm] * (len(small) + len(large)),
        out_specs=(hbm, hbm),
        scratch_shapes=list(scratch.values()) + list(held.values()),
        compiler_params=pltpu.CompilerParams(
            collective_id=0, has_side_effects=True, vmem_limit_bytes=VMEM_LIMIT
        ),
    )(*small.values(), *large.values())
    if not line:
        result = lax.psum(result, ("dp", "section"))

    depth = 6
    sources = dict(result=result, back=back)
    wide = dict(
        head=(width, classes),
        down=(layers, ff, width),
        up=(layers, width, ff),
        out=(layers, width, width),
        qkv=(layers, width, 3 * width),
        table=(n_codes, width),
        action_table=action_table.shape,
        slot_table=slot_table.shape,
        ln1_gain=(layers, width),
        ln1_bias=(layers, width),
        b_out=(layers, width),
        ln2_gain=(layers, width),
        ln2_bias=(layers, width),
        b_down=(layers, width),
        b_up=(layers, ff),
        lnf_gain=(1, width),
        lnf_bias=(1, width),
        b_head=(1, classes),
        frames=frames_t.shape,
    )
    count = len(units)
    held = dict(
        narrow=pltpu.VMEM((depth, BLOCK, width), BF),
        wide=pltpu.VMEM((depth, BLOCK, width), F32),
        tiny=pltpu.VMEM((SMALL_ROWS, width), BF),
        v_back=pltpu.VMEM(back.shape, BF),
        load_sems=pltpu.SemaphoreType.DMA((count + 2,)),
        store_sems=pltpu.SemaphoreType.DMA((count,)),
    )
    names = tuple(sources) + tuple(wide) + tuple(held)
    converted = pl.pallas_call(
        functools.partial(convert_kernel, names, units, layers, ff, classes, n_codes),
        out_shape=tuple(jax.ShapeDtypeStruct(shape, F32) for shape in wide.values()),
        in_specs=[hbm, hbm],
        out_specs=(hbm,) * 6 + (vmem,) * (len(wide) - 6),
        scratch_shapes=list(held.values()),
        compiler_params=pltpu.CompilerParams(vmem_limit_bytes=VMEM_LIMIT),
    )(result, back)

    by_name = SimpleNamespace(**dict(zip(wide, converted)))
    return (
        by_name.table,
        by_name.action_table,
        by_name.slot_table,
        by_name.ln1_gain,
        by_name.ln1_bias,
        by_name.qkv,
        by_name.out,
        by_name.b_out,
        by_name.ln2_gain,
        by_name.ln2_bias,
        by_name.up,
        by_name.b_up,
        by_name.down,
        by_name.b_down,
        by_name.lnf_gain.reshape(-1),
        by_name.lnf_bias.reshape(-1),
        by_name.head,
        by_name.b_head.reshape(-1),
        jnp.transpose(by_name.frames, (1, 0, 2)),
    )


def solution(mesh):
    placed = (
        P("dp", None),
        P("dp", None),
        P("dp", None, "section"),
        P("dp", None),
        P("dp", None),
        P(),
        P(),
        P(),
        P(),
        P(),
        P(),
        P(),
        P(),
        P(),
        P(),
        P(),
        P(),
        P(),
        P(),
        P(),
        P(),
        P(),
        P(),
    )
    return jax.shard_map(
        body,
        mesh=mesh,
        in_specs=placed,
        out_specs=(
            P(),
            P(),
            P(),
            P(),
            P(),
            P(),
            P(),
            P(),
            P(),
            P(),
            P(),
            P(),
            P(),
            P(),
            P(),
            P(),
            P(),
            P(),
            P("dp", None, "section"),
        ),
        check_vma=False,
    )
```

```python
import functools
from types import SimpleNamespace

import jax
import jax.numpy as jnp
from jax import lax
from jax.experimental import pallas as pl
from jax.experimental.pallas import tpu as pltpu
from jax.sharding import PartitionSpec as P

HEADS = 8
HEAD_DIM = 64
STEPS = 21
STEP_LEN = 6
GELU_C = 0.7978845608028654
EPS = 1e-05
NEG = -1e30
BF = jnp.bfloat16
F32 = jnp.float32
LANES = 128
BLOCK = 512
SMALL_ROWS = 64
SMALL_BLOCK = 256
STEP_PLACES = 24
QKV, OUT, UP, DOWN = 0, 3, 4, 8
VMEM_LIMIT = 63 * 2**20
MESH = pl.DeviceIdType.MESH


def dot_nn(left, right):
    return lax.dot_general(left, right, (((1,), (0,)), ((), ())), preferred_element_type=F32)


def dot_nt(left, right):
    return lax.dot_general(left, right, (((1,), (1,)), ((), ())), preferred_element_type=F32)


def dot_tn(left, right):
    return lax.dot_general(left, right, (((0,), (0,)), ((), ())), preferred_element_type=F32)


def dot_exact(left, right):
    return lax.dot_general(
        left,
        right,
        (((1,), (0,)), ((), ())),
        precision=lax.Precision.HIGHEST,
        preferred_element_type=F32,
    )


def gelu_both(values):
    squared = values * values
    tanh_part = jnp.tanh(GELU_C * values * (1.0 + 0.044715 * squared))
    half = 0.5 * (1.0 + tanh_part)
    inner_slope = GELU_C * (1.0 + 3 * 0.044715 * squared)
    slope = half + 0.5 * values * (1.0 - tanh_part * tanh_part) * inner_slope
    return (values * half, slope)


def iota(shape, dimension):
    return lax.broadcasted_iota(jnp.int32, shape, dimension)


def step_of(slots):
    return (slots * 43) >> 8


def lane_wide(column):
    return jnp.broadcast_to(column, (column.shape[0], LANES))


def columns_of(column, width):
    return jnp.concatenate([column] * (width // LANES), axis=1)


def norm_chunk(values, gain, bias):
    width = values.shape[1]
    centred = values - jnp.sum(values, -1, keepdims=True) * (1.0 / width)
    inverse = lax.rsqrt(jnp.sum(centred * centred, -1, keepdims=True) * (1.0 / width) + EPS)
    hat = centred * inverse
    return (hat * gain + bias, hat, inverse)


def norm_back_chunk(upstream, hat, inverse, gain):
    width = upstream.shape[1]
    scaled = upstream * gain
    mean_scaled = jnp.sum(scaled, -1, keepdims=True) * (1.0 / width)
    mean_prod = jnp.sum(scaled * hat, -1, keepdims=True) * (1.0 / width)
    inner = scaled - mean_scaled - hat * mean_prod
    return (
        columns_of(inverse, width) * inner,
        jnp.sum(upstream * hat, 0, keepdims=True),
        jnp.sum(upstream, 0, keepdims=True),
    )


ACTION_ROWS = 32
VECTOR_ROWS = 24


def compute(refs):
    tick = refs.tick
    codes, actions, segs, targets = refs.codes, refs.actions, refs.segs, refs.targets
    own = refs.own
    rows, slots = refs.rows, codes.shape[1]
    tokens = rows * slots
    width = refs.width
    layers = refs.layers
    ff = refs.ff
    classes = refs.classes
    n_codes = refs.n_codes
    wait_weight = refs.wait_weight
    put = refs.put
    chunk = LANES

    def chunks(body):
        for i in range(tokens // chunk):
            body(i * chunk)

    refs.wait_small()

    first = own * rows
    slot_row = iota((rows, slots), 1)
    step_row = step_of(slot_row)
    phase_row = slot_row - step_row * STEP_LEN
    real = slot_row < STEPS * STEP_LEN
    spread = (
        (step_of(iota((STEPS, slots), 1)) == iota((STEPS, slots), 0))
        & (iota((STEPS, slots), 1) == STEP_LEN * iota((STEPS, slots), 0))
    ).astype(F32)
    action_row = dot_exact(actions[pl.ds(first, rows), :].astype(F32), spread)
    code_row = codes[pl.ds(first, rows), :].astype(F32)
    index_row = jnp.where(
        real & (phase_row >= 2),
        code_row,
        jnp.where(real & (phase_row == 0), action_row + float(n_codes), -1.0),
    )
    seg_row = segs[pl.ds(first, rows), :].astype(F32)
    target_row = targets[pl.ds(first, rows), :].astype(F32)
    stacked = jnp.concatenate(
        [index_row, seg_row, target_row, jnp.zeros((slots - 3 * rows, slots), F32)], 0
    )
    refs.int_rows[...] = stacked
    refs.int_cols[...] = jnp.transpose(stacked)
    int_rows, int_cols = refs.int_rows, refs.int_cols

    k_step = step_of(iota((slots, slots), 0))
    q_step = step_of(iota((slots, slots), 1))
    for r in range(rows):
        same = int_cols[:, rows + r : rows + r + 1] == int_rows[rows + r : rows + r + 1, :]
        refs.bias[r] = jnp.where(same & (k_step <= q_step), 0.0, NEG)

    phase_col = iota((slots, 8), 0) - STEP_LEN * step_of(iota((slots, 8), 0))
    slot_one = (phase_col == iota((slots, 8), 1)).astype(F32)
    table = jnp.concatenate([refs.slot_table[...], jnp.zeros((8 - STEP_LEN, width), F32)], 0)
    slot_part = dot_exact(slot_one, table)
    h = refs.h
    refs.send_frames()
    n_actions = refs.action_table.shape[0]
    action_table = jnp.concatenate(
        [
            refs.action_table[...].astype(F32),
            jnp.zeros((ACTION_ROWS - n_actions, width), F32),
        ],
        0,
    ).astype(BF)
    refs.wait_codebook()
    x1 = refs.x1
    for r in range(rows):
        tok = slice(r * slots, (r + 1) * slots)
        col = int_cols[:, r : r + 1]
        one = (col == iota((slots, n_codes), 1).astype(F32)).astype(BF)
        part = dot_nn(one, refs.codebook[...])
        one = (col == (iota((slots, ACTION_ROWS), 1) + n_codes).astype(F32)).astype(BF)
        x1[tok, :] = part + dot_nn(one, action_table) + slot_part
    refs.wait_frames()
    frames = refs.frames
    sections, places, frame_width = frames.shape
    for r in range(rows):
        tok = slice(r * slots, (r + 1) * slots)
        j = iota((slots, places), 0)
        js = step_of(j)
        frame_one = (
            (iota((slots, places), 1) == r * STEP_PLACES + js)
            & (j - js * STEP_LEN == 1)
            & (j < STEPS * STEP_LEN)
        ).astype(BF)
        frame_part = jnp.concatenate(
            [dot_nn(frame_one, frames[k]) for k in range(sections)], 1
        )
        h[tok, :] = (x1[tok, :] + frame_part).astype(BF)
    refs.load_head()

    lane = iota((slots, LANES), 1)
    low_half = lane < HEAD_DIM
    pairs = HEADS // 2

    def both_heads(tile):
        zero = jnp.zeros_like(tile)
        return jnp.concatenate(
            [jnp.where(low_half, tile, zero), jnp.where(low_half, zero, tile)], 0
        )

    def pick_heads(stacked_pair):
        return jnp.where(low_half, stacked_pair[:slots], stacked_pair[slots:])

    def row_blocks(body):
        for r in range(rows):
            body(r, r * slots)

    def block_of(weights, j):
        return weights[pl.ds(j * BLOCK, BLOCK), :]

    def back_through(given, weights, first_block, count):
        for j in range(count):
            part = dot_nt(
                given[:, j * BLOCK : (j + 1) * BLOCK], block_of(weights, first_block + j)
            )
            big[...] = part if j == 0 else big[...] + part

    big = refs.big
    normal = refs.dx1r
    for layer in range(layers):
        qkv, probs, o = (k.at[layer] for k in (refs.qkv, refs.probs, refs.o))
        hat1, inv1, hat2, inv2 = (
            k.at[layer] for k in (refs.hat1, refs.inv1, refs.hat2, refs.inv2)
        )
        m, slope = (k.at[layer] for k in (refs.m, refs.slope))
        gain1, bias1 = refs.ln1_gain[layer : layer + 1, :], refs.ln1_bias[layer : layer + 1, :]
        gain2, bias2 = refs.ln2_gain[layer : layer + 1, :], refs.ln2_bias[layer : layer + 1, :]

        def norm_one(at):
            normed, hat, inverse = norm_chunk(h[pl.ds(at, chunk), :].astype(F32), gain1, bias1)
            normal[pl.ds(at, chunk), :] = normed.astype(BF)
            hat1[pl.ds(at, chunk), :] = hat.astype(BF)
            inv1[pl.ds(at, chunk), :] = lane_wide(inverse)

        chunks(norm_one)
        weights = refs.weights[layer]
        wait_weight(layer, QKV, 3)

        for j in range(3 * width // BLOCK):
            at = slice(j * BLOCK, (j + 1) * BLOCK)
            qkv[:, at] = dot_nn(normal[...], block_of(weights, QKV + j)).astype(BF)

        def attend(r, at):
            tok = pl.ds(at, slots)
            bias = refs.bias[r]
            cuts = [slice(pair * LANES, (pair + 1) * LANES) for pair in range(pairs)]
            query, key, value = (
                [qkv[tok, part * width + cut.start : part * width + cut.stop] for cut in cuts]
                for part in range(3)
            )
            scores = [dot_nt(both_heads(key[i]), query[i]) for i in range(pairs)]
            weights_low = []
            for s in scores:
                parts = []
                for half in (s[:slots], s[slots:]):
                    half = half * HEAD_DIM ** (-0.5) + bias
                    top = jnp.max(half, 0, keepdims=True)
                    expo = jnp.exp(half - top)
                    total = jnp.sum(expo, 0, keepdims=True)
                    parts.append((expo * (1.0 / total)).astype(BF))
                weights_low.append(jnp.concatenate(parts, 0))
            mixed = [dot_tn(weights_low[i], both_heads(value[i])) for i in range(pairs)]
            for i in range(pairs):
                probs[r, i] = weights_low[i]
                o[tok, cuts[i]] = mixed[i].astype(BF)

        row_blocks(attend)
        wait_weight(layer, OUT, 1)
        x1[...] = dot_nn(o[...], block_of(weights, OUT))
        b_out = refs.b_out[layer : layer + 1, :]

        def norm_two(at):
            tok = pl.ds(at, chunk)
            resid = h[tok, :].astype(F32) + x1[tok, :] + b_out
            x1[tok, :] = resid
            normed, hat, inverse = norm_chunk(resid, gain2, bias2)
            normal[tok, :] = normed.astype(BF)
            hat2[tok, :] = hat.astype(BF)
            inv2[tok, :] = lane_wide(inverse)

        chunks(norm_two)
        wait_weight(layer, UP, ff // BLOCK)
        b_up = refs.b_up

        for j in range(ff // BLOCK):
            at = slice(j * BLOCK, (j + 1) * BLOCK)
            u = dot_nn(normal[...], block_of(weights, UP + j)) + b_up[layer : layer + 1, at]
            hidden, bent = gelu_both(u)
            m[:, at] = hidden.astype(BF)
            slope[:, at] = bent.astype(BF)

        b_down = refs.b_down[layer : layer + 1, :]
        wait_weight(layer, DOWN, ff // BLOCK)
        w_down = weights[DOWN * BLOCK : DOWN * BLOCK + ff, :]
        h[...] = (x1[...] + dot_nn(m[...], w_down) + b_down).astype(BF)

    gain, bias_f = refs.lnf_gain[...], refs.lnf_bias[...]
    f, hatf, invf, dz = refs.dx1r, refs.x1, refs.invf, refs.dz
    sums = refs.sums
    sums[...] = jnp.zeros_like(sums)

    def add_row(row, value, width_at=0):
        sums[row : row + 1, width_at : width_at + value.shape[1]] += value

    def norm_final(at):
        tok = pl.ds(at, chunk)
        normed, hat, inverse = norm_chunk(h[tok, :].astype(F32), gain, bias_f)
        f[tok, :] = normed.astype(BF)
        hatf[tok, :] = hat
        invf[tok, :] = lane_wide(inverse)

    chunks(norm_final)
    refs.wait_head()
    w_head = refs.w_head
    phase_one = iota((slots, 1), 0) - STEP_LEN * step_of(iota((slots, 1), 0))
    for r in range(rows):
        tok = slice(r * slots, (r + 1) * slots)
        logits = [
            dot_nn(f[tok, :], w_head[j * width : (j + 1) * width, :])
            for j in range(classes // BLOCK)
        ]
        logits = jnp.concatenate(logits, 1) + refs.b_head[...]
        top = jnp.max(logits, -1, keepdims=True)
        expo = jnp.exp(logits - top)
        total = jnp.sum(expo, -1, keepdims=True)
        chosen = (
            (int_cols[:, rows + r : rows + r + 1] != 0.0) & (phase_one >= 1) & (phase_one <= 4)
        )
        weight = jnp.where(chosen, 1.0 / (4 * STEPS), 0.0)
        wanted = int_cols[:, 2 * rows + r : 2 * rows + r + 1]
        hit = wanted == iota((slots, classes), 1).astype(F32)
        delta = expo * (weight / total) - jnp.where(hit, weight, 0.0)
        low = delta.astype(BF)
        dz[tok, :] = low
        part = jnp.sum(low.astype(F32), 0, keepdims=True)
        for block in range(classes // BLOCK):
            add_row(VECTOR_ROWS - 2 + block, part[:, block * BLOCK : (block + 1) * BLOCK])
    for block in range(classes // BLOCK):
        at = slice(block * BLOCK, (block + 1) * BLOCK)
        put(dot_tn(f[...], dz[:, at]))
        tick()
    back_through(dz, w_head, 0, classes // BLOCK)
    dy = h

    def final_back(at):
        tok = pl.ds(at, chunk)
        back, gain_sum, bias_sum = norm_back_chunk(
            big[tok, :], hatf[tok, :], invf[tok, :], gain
        )
        dy[tok, :] = back.astype(BF)
        add_row(VECTOR_ROWS - 4, gain_sum)
        add_row(VECTOR_ROWS - 3, bias_sum)

    chunks(final_back)
    tick()

    for layer in reversed(range(layers)):
        qkv, probs, o = (k.at[layer] for k in (refs.qkv, refs.probs, refs.o))
        hat1, inv1, hat2, inv2 = (
            k.at[layer] for k in (refs.hat1, refs.inv1, refs.hat2, refs.inv2)
        )
        m, slope = (k.at[layer] for k in (refs.m, refs.slope))
        weights = refs.weights[layer]
        gain1, gain2 = refs.ln1_gain[layer : layer + 1, :], refs.ln2_gain[layer : layer + 1, :]
        du = slope
        base = layer * 10
        dsum = jnp.zeros((1, width), F32)
        for i in range(tokens // chunk):
            dsum = dsum + jnp.sum(dy[i * chunk : (i + 1) * chunk, :].astype(F32), 0, keepdims=True)
        add_row(base + 5, dsum)

        for j in range(ff // BLOCK):
            at = slice(j * BLOCK, (j + 1) * BLOCK)
            put(dot_tn(m[:, at], dy[...]))
            tick()
        bias1, bias2 = refs.ln1_bias[layer : layer + 1, :], refs.ln2_bias[layer : layer + 1, :]

        def normal_again(hat, gain, bias):
            def one(at):
                tok = pl.ds(at, chunk)
                normal[tok, :] = (hat[tok, :].astype(F32) * gain + bias).astype(BF)

            chunks(one)

        normal_again(hat2, gain2, bias2)
        for j in range(ff // BLOCK):
            at = slice(j * BLOCK, (j + 1) * BLOCK)
            low = (dot_nt(dy[...], block_of(weights, DOWN + j)) * slope[:, at].astype(F32)).astype(BF)
            du[:, at] = low
            add_row(base + 6 + j, jnp.sum(low.astype(F32), 0, keepdims=True))
            put(dot_tn(normal[...], low))
            tick()
        back_through(du, weights, UP, ff // BLOCK)
        tick()

        dx1, dx1r = refs.x1, refs.dx1r

        def second_back(at):
            tok = pl.ds(at, chunk)
            back, gain_sum, bias_sum = norm_back_chunk(
                big[tok, :], hat2[tok, :].astype(F32), inv2[tok, :], gain2
            )
            total = dy[tok, :].astype(F32) + back
            dx1[tok, :] = total
            low = total.astype(BF)
            dx1r[tok, :] = low
            add_row(base + 3, gain_sum)
            add_row(base + 4, bias_sum)
            add_row(base + 2, jnp.sum(low.astype(F32), 0, keepdims=True))

        chunks(second_back)
        put(dot_tn(o[...], dx1r[...]))
        do = o
        do[...] = dot_nt(dx1r[...], block_of(weights, OUT)).astype(BF)
        tick()
        dqkv = qkv

        def attend_back(r, at):
            tok = pl.ds(at, slots)
            cuts = [slice(pair * LANES, (pair + 1) * LANES) for pair in range(pairs)]
            query, key, value = (
                [qkv[tok, part * width + cut.start : part * width + cut.stop] for cut in cuts]
                for part in range(3)
            )
            given = [do[tok, cut] for cut in cuts]
            dp = [dot_nt(both_heads(value[i]), given[i]) for i in range(pairs)]
            p = [probs[r, i] for i in range(pairs)]
            dv = [dot_nn(p[i], given[i]) for i in range(pairs)]
            ds = []
            for i in range(pairs):
                parts = []
                for cut in (slice(0, slots), slice(slots, 2 * slots)):
                    p_f = p[i][cut].astype(F32)
                    prod = p_f * dp[i][cut]
                    total = jnp.sum(prod, 0, keepdims=True)
                    parts.append((prod - p_f * total).astype(BF))
                ds.append(jnp.concatenate(parts, 0))
            scale = HEAD_DIM ** (-0.5)
            dq = [dot_tn(ds[i], both_heads(key[i])) for i in range(pairs)]
            dk = [dot_nn(ds[i], query[i]) for i in range(pairs)]
            for i in range(pairs):
                at_q, at_k, at_v = (
                    slice(part * width + cuts[i].start, part * width + cuts[i].stop)
                    for part in range(3)
                )
                dqkv[tok, at_q] = (dq[i] * scale).astype(BF)
                dqkv[tok, at_k] = (pick_heads(dk[i]) * scale).astype(BF)
                dqkv[tok, at_v] = pick_heads(dv[i]).astype(BF)

        half_rows = rows // 2
        for start in (0, half_rows):

            def some(r, carry):
                attend_back(r, pl.multiple_of(r * slots, slots))
                return carry

            lax.fori_loop(start, start + half_rows, some, 0)
            tick()
        normal_again(hat1, gain1, bias1)
        for j in range(3 * width // BLOCK):
            at = slice(j * BLOCK, (j + 1) * BLOCK)
            put(dot_tn(normal[...], dqkv[:, at]))
            tick()
        back_through(dqkv, weights, QKV, 3)
        tick()

        def first_back(at):
            tok = pl.ds(at, chunk)
            back, gain_sum, bias_sum = norm_back_chunk(
                big[tok, :], hat1[tok, :].astype(F32), inv1[tok, :], gain1
            )
            dy[tok, :] = (dx1[tok, :] + back).astype(BF)
            add_row(base + 0, gain_sum)
            add_row(base + 1, bias_sum)

        chunks(first_back)
        if layer == layers - 1:
            refs.layer_done()
        tick()

    refs.send_back()
    index_rows = jnp.concatenate([int_rows[r : r + 1, :] for r in range(rows)], 1)
    half = n_codes // 2
    for block in range(2):
        one = (index_rows == (iota((half, tokens), 0) + block * half).astype(F32)).astype(BF)
        put(dot_nn(one, dy[...]))
        tick()
    token = iota((8, tokens), 1)
    slot = token & (slots - 1)
    slot_hit = (slot - STEP_LEN * step_of(slot) == iota((8, tokens), 0)).astype(BF)
    one = (index_rows == (iota((ACTION_ROWS, tokens), 0) + n_codes).astype(F32)).astype(BF)
    sums[VECTOR_ROWS : VECTOR_ROWS + 8, :] = dot_nn(slot_hit, dy[...])
    rest = jnp.zeros((SMALL_BLOCK - SMALL_ROWS, width), F32)
    put(jnp.concatenate([dot_nn(one, dy[...]), sums[...], rest], 0))


class Exchange:
    def __init__(self, total, result, send_sems, recv_sems, own_sems, line):
        self.total, self.result = total, result
        self.own_sems, self.send_sems, self.recv_sems = own_sems, send_sems, recv_sems
        self.line = line
        dp, section = lax.axis_index("dp"), lax.axis_index("section")
        self.z, self.y = dp // 2, dp % 2
        self.x, self.core = section // 2, section % 2
        self.bit = (
            self.x + self.core * (self.y - self.x),
            self.y + self.core * (self.x - self.y),
        )
        flip_x, flip_y = 1 - 2 * self.x, 1 - 2 * self.y
        self.near = (
            self.device(self.x + (1 - self.core) * flip_x, self.y + self.core * flip_y),
            self.device(self.x + self.core * flip_x, self.y + (1 - self.core) * flip_y),
        )
        self.twin = (dp, section + 1 - 2 * self.core)
        self.corner = (dp, 3 - section)
        self.above = (dp + 2, section)
        self.below = (dp - 2, section)
        self.side = self.z // (line // 2)
        self.inner = (dp + 2 - 4 * self.side, section)
        self.outer = (dp - 2 + 4 * self.side, section)

    def device(self, x, y):
        return (self.z * 2 + y, x * 2 + self.core)

    def neighbours(self):
        last = self.line - 1
        lines = (self.z + last - 1) // last + (2 * last - 1 - self.z) // last
        return 4 + lines

    def signal_all(self, semaphore):
        for other in (self.twin, *self.near, self.corner):
            pl.semaphore_signal(semaphore, inc=1, device_id=other, device_id_type=MESH)

        @pl.when(self.z < self.line - 1)
        def _():
            pl.semaphore_signal(semaphore, inc=1, device_id=self.above, device_id_type=MESH)

        @pl.when(self.z > 0)
        def _():
            pl.semaphore_signal(semaphore, inc=1, device_id=self.below, device_id_type=MESH)

    @staticmethod
    def landing_rows(size, kind):
        half = size // 2
        return (2 * half + half // 8, 2 * half, 2 * half + 3 * half // 4 + half // 8)[kind]

    def rows(self, ref, at, count):
        return ref.at[pl.ds(pl.multiple_of(at, 16), count)]

    def add(self, at, landing, landed, count):
        step = next(rows for rows in (64, 48, 32, 16) if count % rows == 0)

        def one(i, carry):
            here = pl.ds(pl.multiple_of(at + i * step, 16), step)
            there = pl.ds(pl.multiple_of(landed + i * step, 16), step)
            self.total[here, :] = (
                self.total[here, :].astype(F32) + landing[there, :].astype(F32)
            ).astype(BF)
            return carry

        if count == step:
            one(0, 0)
        else:
            lax.fori_loop(0, count // step, one, 0)

    def stages(self, i, start, size, kind, landing, landing_at, middle):
        z, last, side = self.z, self.line - 1, self.side
        total, result = self.total, self.result
        own_sem, send_sem = self.own_sems.at[i], self.send_sems.at[i]
        first_sem = 9 * i
        half = size // 2
        own = start + self.core * half
        end = not middle

        def when(condition):
            if isinstance(condition, bool):
                return lambda body: body() if condition else None
            return lambda body: pl.when(condition)(body)

        def copy(k, source, target, other):
            return lambda: pltpu.make_async_remote_copy(
                src_ref=source,
                dst_ref=target,
                send_sem=send_sem,
                recv_sem=self.recv_sems.at[first_sem + k],
                device_id=other,
                device_id_type=MESH,
            )

        def send(*copies):
            for make in copies:
                make().start()

        def wait(*copies):
            for make in copies:
                make().wait_recv()

        def give(k, at, count, landed, other):
            return copy(k, self.rows(total, at, count), self.rows(landing, landed, count), other)

        def back(k, at, count, other, source=result):
            return copy(k, self.rows(source, at, count), self.rows(result, at, count), other)

        def keep(at, count):
            return lambda: pltpu.make_async_copy(
                self.rows(total, at, count), self.rows(result, at, count), own_sem
            )

        twin = give(0, start + (1 - self.core) * half, half, landing_at, self.twin)
        twin_back = back(8, own, half, self.twin)
        free = landing_at + half

        def twin_done():
            wait(twin)
            self.add(own, landing, landing_at, half)

        def swaps(base, count, free):
            part, bit = count // 2, self.bit
            base1 = base + bit[0] * part
            first = give(1, base + (1 - bit[0]) * part, part, free, self.near[0])
            base2 = base1 + bit[1] * (part // 2)
            second = give(
                2, base1 + (1 - bit[1]) * (part // 2), part // 2, free + part, self.near[1]
            )

            def first_done():
                wait(first)
                self.add(base1, landing, free, part)

            def second_done():
                wait(second)
                self.add(base2, landing, free + part, part // 2)

            return first, first_done, base1, second, second_done, base2

        def middle_line(base, count, free, source):
            part = count // 2
            mine, other = base + side * part, base + (1 - side) * part
            inward = give(3, base, count, free, self.inner)
            across = give(4, other, part, free + count, self.inner)
            out_mine = back(3, mine, part, self.outer, source)
            across_back = back(5, mine, part, self.inner, source)
            out_other = back(4, other, part, self.outer)

            def start_line():
                when(end)(lambda: send(inward))

            def hop():
                @when(middle)
                def _():
                    wait(inward)
                    self.add(base, landing, free, count)
                    send(across)

            def hop_done():
                wait(across)
                self.add(mine, landing, free + count, part)

            def start_back():
                send(across_back, out_mine)

            def hop_back():
                wait(across_back)
                send(out_other)

            def ends_done():
                wait(out_mine, out_other)

            return mine, start_line, hop, hop_done, start_back, hop_back, ends_done

        def line_rows(ends, others):
            def all_sent(count):
                whole = self.rows(total, 0, count)
                return lambda: pltpu.make_async_copy(whole, whole, send_sem).wait()

            def finish():
                when(end)(all_sent(ends))
                when(middle)(all_sent(others))

            return finish

        if kind == 0:
            first, first_done, base1, second, second_done, base2 = swaps(own, half, free)
            rest = half // 4
            free += half // 2 + rest
            mine, start_line, hop, hop_done, start_back, hop_back, ends_done = middle_line(
                base2, rest, free, total
            )
            mine_kept = keep(mine, rest // 2)
            second_back = back(6, base2, rest, self.near[1])
            first_back = back(7, base1, half // 2, self.near[0])

            def s1():
                twin_done()
                send(first)

            def s2():
                first_done()
                send(second)

            def s3():
                second_done()
                start_line()

            def s5():
                @when(middle)
                def _():
                    hop_done()
                    start_back()
                    mine_kept().start()

            def s6():
                @when(middle)
                def _():
                    hop_back()
                    mine_kept().wait()
                    send(second_back)

            def s7():
                @when(end)
                def _():
                    ends_done()
                    send(second_back)

            def s8():
                wait(second_back)
                send(first_back)

            def s9():
                wait(first_back)
                send(twin_back)

            def s10():
                wait(twin_back)

            finish = line_rows(3 * half + 3 * half // 4, 4 * half)
            return [lambda: send(twin), s1, s2, s3, hop, s5, s6, s7, s8, s9, s10, finish]

        if kind == 2:
            mine, start_line, hop, hop_done, start_back, hop_back, ends_done = middle_line(
                own, half, free, result
            )
            first, first_done, base1, second, second_done, base2 = swaps(
                mine, half // 2, free + half + half // 2
            )
            mine_kept = keep(base2, half // 8)
            second_back = back(6, base2, half // 8, self.near[1], total)
            first_back = back(7, base1, half // 4, self.near[0])

            def s1():
                twin_done()
                start_line()

            def s3():
                @when(middle)
                def _():
                    hop_done()
                    send(first)

            def s4():
                @when(middle)
                def _():
                    first_done()
                    send(second)

            def s5():
                @when(middle)
                def _():
                    second_done()
                    send(second_back)
                    mine_kept().start()

            def s6():
                @when(middle)
                def _():
                    wait(second_back)
                    mine_kept().wait()
                    send(first_back)

            def s7():
                @when(middle)
                def _():
                    wait(first_back)
                    start_back()

            def s8():
                @when(middle)
                def _():
                    hop_back()
                    send(twin_back)

            def s9():
                @when(end)
                def _():
                    ends_done()
                    send(twin_back)

            def s10():
                wait(twin_back)

            finish = line_rows(3 * half, 4 * half + 3 * half // 4)
            return [lambda: send(twin), s1, hop, s3, s4, s5, s6, s7, s8, s9, s10, finish]

        part = half // 2
        low, high = own, own + part
        up = give(3, high, part, free, self.above)
        down = give(4, low, part, free + part, self.below)
        up_back = back(5, low, part, self.above)
        down_back = back(3, high, part, self.below)
        first, first_done, base1, second, second_done, base2 = swaps(
            own + side * part, part, free + side * part
        )
        mine_kept = keep(base2, half // 8)
        second_back = back(6, base2, half // 8, self.near[1], total)
        first_back = back(7, base1, half // 4, self.near[0])

        def up_hop(k):
            @when((z == k) if middle == (0 < k < last) else False)
            def _():
                wait(up)
                self.add(high, landing, free, part)
                if k < last:
                    send(up)

            @when((z == last - k) if middle == (0 < k < last) else False)
            def _():
                wait(down)
                self.add(low, landing, free + part, part)
                if k < last:
                    send(down)

            if k == last:
                when(end)(lambda: send(first))

        def back_hop(k):
            @when((z == k) if middle == (0 < k < last) else False)
            def _():
                wait(up_back)
                if k < last:
                    send(up_back)

            @when((z == last - k) if middle == (0 < k < last) else False)
            def _():
                wait(down_back)
                if k < last:
                    send(down_back)

            if k == last:
                send(twin_back)

        def s1():
            twin_done()
            when((z == 0) if end else False)(lambda: send(up))
            when((z == last) if end else False)(lambda: send(down))

        def t1():
            @when(end)
            def _():
                first_done()
                send(second)

        def t2():
            @when(end)
            def _():
                second_done()
                send(second_back)
                mine_kept().start()

        def t3():
            @when(end)
            def _():
                wait(second_back)
                mine_kept().wait()
                send(first_back)

        def t4():
            when(end)(lambda: wait(first_back))
            when((z == 0) if end else False)(lambda: send(up_back))
            when((z == last) if end else False)(lambda: send(down_back))

        def t5():
            wait(twin_back)

        hops = [functools.partial(up_hop, k) for k in range(1, last + 1)]
        hops_back = [functools.partial(back_hop, k) for k in range(1, last + 1)]
        finish = line_rows(3 * half + 3 * half // 4, 4 * half)
        return [lambda: send(twin), s1, *hops, t1, t2, t3, t4, *hops_back, t5, finish]


SIZES = (1024, 512, 512, 512, 512, 512, 1536, 1024, 1024, 512, 1536, 512, 512, 512, 512, 1536, 512, 512, 512, 256)
KINDS = (0, 1, 0, 0, 2, 0, 0, 0, 0, 1, 0, 1, 0, 0, 1, 0, 2, 2, 0, 0)
PLAN_ENDS = (
    (),
    (),
    (0,),
    (),
    (16,),
    (32,),
    (48,),
    (64, 1,),
    (),
    (17, 18, 19, 80, 33, 49,),
    (65, 66, 67, 68, 69, 70,),
    (81,),
    (96,),
    (),
    (),
    (2,),
    (),
    (),
    (),
    (34,),
    (97,),
    (),
    (),
    (50, 112,),
    (82, 128,),
    (),
    (3, 4, 144, 113,),
    (),
    (129, 160, 145, 146, 147,),
    (176,),
    (192, 20,),
    (35, 36, 98, 161, 208, 177, 178, 179, 51, 52,),
    (193, 83, 84,),
    (),
    (224,),
    (),
    (209, 114,),
    (225, 226, 227,),
    (),
    (130,),
    (
        240, 256, 21, 99, 100, 53, 85, 54, 86, 272, 241, 257, 258, 259, 260, 261, 262, 263, 264,
        288, 162, 148, 304, 194, 273, 274, 275, 276, 277, 278, 289, 305, 115, 116, 117, 118,
        210, 131, 132, 133, 134, 22, 180, 37, 38, 55, 71, 72, 242, 228, 87, 5, 6, 163, 164, 165,
        166, 39, 195, 196, 197, 198, 101, 149, 102, 290, 306, 211, 212, 213, 214, 23, 181, 56,
        7, 243, 244, 245, 246, 88, 229, 150, 40, 291, 292, 293, 294, 103, 307, 308, 309, 310,
        182, 24, 25, 26, 57, 279, 280, 58, 8, 230, 89, 151, 41, 90, 42, 183, 104, 119, 135, 231,
        9, 152, 153, 154, 10, 73, 74, 105, 167, 184, 185, 186, 120, 106, 136, 232, 233, 234,
        199, 215, 168, 121, 27, 247, 295, 122, 311, 28, 200, 137, 216, 155, 138, 156, 169, 248,
        187, 170, 188, 296, 312, 201, 235, 217, 202, 236, 218, 265, 266, 249, 297, 313, 250,
        298, 281, 314, 282,
    ),
)
PLAN_MIDDLE = (
    (),
    (),
    (0,),
    (),
    (16,),
    (32,),
    (48,),
    (64, 1,),
    (),
    (17, 80, 33, 49,),
    (65,),
    (81,),
    (96,),
    (),
    (),
    (2, 18,),
    (97,),
    (34,),
    (),
    (),
    (),
    (),
    (),
    (50,),
    (112, 82,),
    (128,),
    (3, 19, 20, 21, 22, 23,),
    (144, 66, 113,),
    (129, 160,),
    (176, 145,),
    (35, 98,),
    (192, 51, 67, 161,),
    (177, 4, 208, 83,),
    (),
    (224, 193,),
    (),
    (),
    (114, 146, 209, 225,),
    (36,),
    (130,),
    (
        52, 68, 99, 178, 240, 147, 148, 149, 150, 151, 256, 84, 53, 162, 226, 241, 257, 85, 272,
        179, 180, 181, 182, 183, 184, 194, 152, 288, 273, 115, 210, 54, 55, 100, 304, 289, 131,
        227, 228, 229, 230, 231, 232, 69, 86, 87, 37, 24, 305, 258, 38, 39, 5, 163, 242, 195,
        101, 259, 56, 211, 274, 290, 6, 7, 70, 88, 306, 116, 40, 102, 103, 243, 132, 275, 57,
        260, 117, 58, 133, 164, 8, 71, 196, 291, 89, 307, 118, 119, 212, 90, 134, 135, 41, 165,
        42, 104, 276, 261, 244, 72, 73, 292, 197, 308, 9, 74, 213, 120, 10, 25, 166, 167, 136,
        245, 293, 198, 199, 309, 214, 215, 105, 277, 262, 153, 106, 26, 27, 246, 247, 294, 295,
        28, 310, 311, 121, 168, 185, 122, 154, 155, 137, 200, 233, 156, 278, 216, 138, 263, 186,
        187, 248, 188, 234, 235, 236, 264, 265, 296, 169, 312, 266, 201, 170, 217, 279, 202,
        218, 249, 280, 281, 297, 313, 250, 282, 298, 314,
    ),
)


def make_units(layers, ff, classes, n_codes):
    count = classes // BLOCK + layers * (2 * ff // BLOCK + 4) + n_codes // BLOCK
    units = [(i * BLOCK, BLOCK) for i in range(count)]
    units.append((count * BLOCK, SMALL_BLOCK))
    return units


def make_parts(early_rows):
    parts = []
    start = 0
    for size in SIZES:
        parts.append((start, size))
        start += size
    return parts, sum(1 for start, size in parts if start < early_rows)


def gradient_kernel(small, names, units, line, rows, *args):
    count = len(small)
    refs = SimpleNamespace(**dict(zip(names, args[count:])))
    small_copies = []
    for i, (name, source, target) in enumerate(zip(small, args[:count], args[-count:])):
        setattr(refs, name, target)
        small_copies.append(pltpu.make_async_copy(source, target, refs.small_sems.at[i]))
        small_copies[-1].start()
    layers, width, ff = refs.w_up.shape
    classes, n_codes = refs.w_head.shape[1], refs.codebook.shape[0]
    layer_blocks = 4 + 2 * ff // BLOCK
    early_units = classes // BLOCK + layer_blocks
    dp, section = lax.axis_index("dp"), lax.axis_index("section")
    sections = lax.axis_size("section")

    exchange = None
    barrier = pltpu.get_barrier_semaphore()
    if line:
        exchange = Exchange(
            refs.total, refs.result, refs.send_sems, refs.recv_sems, refs.own_sems, line
        )
        exchange.signal_all(barrier)
    else:
        for step in range(1, sections):
            other = (dp, lax.rem(section + step, sections))
            pl.semaphore_signal(barrier, inc=1, device_id=other, device_id_type=MESH)

    sems = iter(range(refs.weight_sems.shape[0]))

    def load(source, target):
        copy = pltpu.make_async_copy(source, target, refs.weight_sems.at[next(sems)])
        copy.start()
        return copy

    spare = layer_blocks * BLOCK
    v_codebook = refs.late.at[spare : spare + n_codes]
    codebook_copy = load(refs.codebook, v_codebook)
    block_copies = {}
    layer_weights = [refs.first_weights, refs.late]
    for layer in range(layers):
        target = layer_weights[layer]
        for first, count, whole in (
            (QKV, 3, refs.w_qkv),
            (OUT, 1, refs.w_out),
            (UP, ff // BLOCK, refs.w_up),
        ):
            for j in range(count):
                block_copies[layer, first + j] = load(
                    whole.at[layer, :, pl.ds(j * BLOCK, BLOCK)],
                    target.at[pl.ds((first + j) * BLOCK, BLOCK)],
                )
        for j in range(ff // BLOCK):
            block_copies[layer, DOWN + j] = load(
                refs.w_down.at[layer, pl.ds(j * BLOCK, BLOCK)],
                target.at[pl.ds((DOWN + j) * BLOCK, BLOCK)],
            )
    head_place = refs.late.at[spare : spare + classes // BLOCK * width]
    head_sems = [next(sems) for _ in range(classes // BLOCK)]
    head_copies = [
        pltpu.make_async_copy(
            refs.w_head.at[:, pl.ds(j * BLOCK, BLOCK)],
            head_place.at[pl.ds(j * width, width)],
            refs.weight_sems.at[head_sems[j]],
        )
        for j in range(classes // BLOCK)
    ]

    def load_head():
        for copy in head_copies:
            copy.start()

    def wait_head():
        for copy in head_copies:
            copy.wait()


    def wait_weight(layer, first, count):
        for j in range(count):
            block_copies[layer, first + j].wait()

    frame_copies = []
    for step in range(1, sections):
        other = lax.rem(section + step, sections)
        frame_copies.append(
            pltpu.make_async_remote_copy(
                src_ref=refs.sent_frames.at[other],
                dst_ref=refs.frames.at[section],
                send_sem=refs.frame_sems.at[0, step - 1],
                recv_sem=refs.frame_sems.at[1, step - 1],
                device_id=(dp, other),
                device_id_type=MESH,
            )
        )

    def send_frames():
        steps, rows_dev, frame_width = refs.held_frames.shape
        n_all = steps * rows_dev
        flat = refs.held_frames[...].reshape(n_all, frame_width)
        place = iota((rows * STEP_PLACES, n_all), 0)
        row = (place * 43) >> 10
        step = place - row * STEP_PLACES
        column = iota((rows * STEP_PLACES, n_all), 1)
        for other in range(sections):
            hit = (column == step * rows_dev + row + other * rows) & (step < steps)
            refs.sent_frames[other] = dot_nn(hit.astype(BF), flat).astype(BF)
        refs.frames[section] = refs.sent_frames[section]
        if exchange is not None:
            pl.semaphore_wait(barrier, exchange.neighbours())
        else:
            pl.semaphore_wait(barrier, sections - 1)
        for copy in frame_copies:
            copy.start()

    def wait_frames():
        for copy in frame_copies:
            copy.wait()

    def wait_small():
        for copy in small_copies:
            copy.wait()

    back_copies = []

    def send_back():
        for step in range(1, sections):
            other = lax.rem(section + step, sections)
            at = pl.ds(pl.multiple_of(other * LANES, LANES), LANES)
            back_copies.append(
                pltpu.make_async_remote_copy(
                    src_ref=refs.h.at[:, at],
                    dst_ref=refs.back.at[section],
                    send_sem=refs.frame_sems.at[3, step - 1],
                    recv_sem=refs.frame_sems.at[4, step - 1],
                    device_id=(dp, other),
                    device_id_type=MESH,
                )
            )
        at = pl.ds(pl.multiple_of(section * LANES, LANES), LANES)
        back_copies.append(
            pltpu.make_async_copy(refs.h.at[:, at], refs.back.at[section], refs.frame_sems.at[2, 0])
        )
        for copy in back_copies:
            copy.start()

    stages = {False: [], True: []}
    if exchange is not None:
        parts, early_parts = make_parts(early_units * BLOCK)
        for middle in stages:
            offsets = [0, 0]
            for i, (start, size) in enumerate(parts):
                late = i >= early_parts
                landing = refs.late if late else refs.early
                stages[middle].append(
                    exchange.stages(i, start, size, KINDS[i], landing, offsets[late], middle)
                )
                offsets[late] += exchange.landing_rows(size, KINDS[i])
    ticks = iter(range(10**6))
    ready = []
    freed = []
    at_end = (exchange.z == 0) | (exchange.z == line - 1) if line else None

    def run(k):
        events = PLAN_ENDS[k] + PLAN_MIDDLE[k]
        if not freed and any(event // 16 >= early_parts for event in events):
            pl.semaphore_wait(refs.free_sem, exchange.neighbours())
            freed.append(True)

        @pl.when(at_end)
        def _():
            for event in PLAN_ENDS[k]:
                stages[False][event // 16][event % 16]()

        @pl.when(jnp.logical_not(at_end))
        def _():
            for event in PLAN_MIDDLE[k]:
                stages[True][event // 16][event % 16]()

    def tick():
        if exchange is not None:
            run(next(ticks))

    def put(value):
        start, size = units[len(ready)]
        refs.total[start : start + size, :] = value.astype(BF)
        ready.append(start)

    def layer_done():
        if exchange is not None:
            exchange.signal_all(refs.free_sem)

    view = SimpleNamespace(**vars(refs))
    view.codebook, view.w_head = v_codebook, head_place
    view.weights = layer_weights
    view.own, view.rows, view.width, view.layers = section, rows, width, layers
    view.ff, view.classes, view.n_codes = ff, classes, n_codes
    view.wait_weight, view.wait_frames = wait_weight, wait_frames
    view.send_frames, view.wait_small = send_frames, wait_small
    view.wait_codebook, view.wait_head = codebook_copy.wait, wait_head
    view.load_head = load_head
    view.tick, view.put, view.layer_done, view.send_back = tick, put, layer_done, send_back
    compute(view)
    if exchange is not None:
        for k in range(next(ticks), len(PLAN_ENDS)):
            run(k)

        @pl.when(at_end)
        def _():
            for stage in stages[False]:
                stage[-1]()

        @pl.when(jnp.logical_not(at_end))
        def _():
            for stage in stages[True]:
                stage[-1]()

    else:
        keep = pltpu.make_async_copy(refs.total, refs.result, refs.own_sems.at[0])
        keep.start()
        keep.wait()
    for copy in back_copies:
        copy.wait()


def convert_kernel(names, units, layers, ff, classes, n_codes, *args):
    refs = SimpleNamespace(**dict(zip(names, args)))
    depth = refs.narrow.shape[0]
    width = refs.narrow.shape[2]
    targets = []
    for j in range(classes // BLOCK):
        targets.append(refs.head.at[:, pl.ds(j * BLOCK, BLOCK)])
    for layer in reversed(range(layers)):
        for j in range(ff // BLOCK):
            targets.append(refs.down.at[layer, pl.ds(j * BLOCK, BLOCK)])
        for j in range(ff // BLOCK):
            targets.append(refs.up.at[layer, :, pl.ds(j * BLOCK, BLOCK)])
        targets.append(refs.out.at[layer])
        for j in range(3):
            targets.append(refs.qkv.at[layer, :, pl.ds(j * BLOCK, BLOCK)])
    for j in range(n_codes // BLOCK):
        targets.append(refs.table.at[pl.ds(j * BLOCK, BLOCK)])
    count = len(targets)
    loads, stores = [], []
    for i in range(count):
        start, size = units[i]
        loads.append(
            pltpu.make_async_copy(
                refs.result.at[pl.ds(start, size)], refs.narrow.at[i % depth], refs.load_sems.at[i]
            )
        )
        stores.append(
            pltpu.make_async_copy(refs.wide.at[i % depth], targets[i], refs.store_sems.at[i])
        )
    small_load = pltpu.make_async_copy(
        refs.result.at[pl.ds(units[count][0], SMALL_ROWS)], refs.tiny, refs.load_sems.at[count]
    )
    small_load.start()
    back_load = pltpu.make_async_copy(refs.back, refs.v_back, refs.load_sems.at[count + 1])
    back_load.start()
    for i in range(depth):
        loads[i].start()
    small_load.wait()
    small = refs.tiny[...].astype(F32)
    refs.action_table[...] = small[: refs.action_table.shape[0]]
    vectors = small[ACTION_ROWS:]
    refs.slot_table[...] = vectors[VECTOR_ROWS : VECTOR_ROWS + STEP_LEN]
    for layer in range(layers):
        at = slice(layer, layer + 1)
        row = layer * 10
        for k, ref in enumerate(
            (refs.ln1_gain, refs.ln1_bias, refs.b_out, refs.ln2_gain, refs.ln2_bias, refs.b_down)
        ):
            ref[at, :] = vectors[row + k : row + k + 1]
        for j in range(ff // BLOCK):
            refs.b_up[at, j * BLOCK : (j + 1) * BLOCK] = vectors[row + 6 + j : row + 7 + j]
    refs.lnf_gain[...] = vectors[VECTOR_ROWS - 4 : VECTOR_ROWS - 3]
    refs.lnf_bias[...] = vectors[VECTOR_ROWS - 3 : VECTOR_ROWS - 2]
    for j in range(classes // BLOCK):
        refs.b_head[:, j * BLOCK : (j + 1) * BLOCK] = vectors[
            VECTOR_ROWS - 2 + j : VECTOR_ROWS - 1 + j
        ]
    for i in range(count):
        loads[i].wait()
        if i >= depth:
            stores[i - depth].wait()

        def one(k, carry, slot=i % depth):
            at = pl.ds(pl.multiple_of(k * 64, 64), 64)
            refs.wide[slot, at, :] = refs.narrow[slot, at, :].astype(F32)
            return carry

        lax.fori_loop(0, BLOCK // 64, one, 0)
        stores[i].start()
        if i + depth < count:
            loads[i + depth].start()
    back_load.wait()
    sections, tokens, lanes = refs.v_back.shape
    steps, rows_dev, _ = refs.frames.shape
    rows = rows_dev // sections
    slots = tokens // rows
    total = None
    for s in range(sections):
        token = iota((steps * rows_dev, tokens), 1)
        where = iota((steps * rows_dev, tokens), 0)
        step, row = where // rows_dev, where % rows_dev
        wanted = (row - s * rows) * slots + STEP_LEN * step + 1
        mine = (row >= s * rows) & (row < (s + 1) * rows)
        hit = ((token == wanted) & mine).astype(BF)
        part = dot_nn(hit, refs.v_back[s])
        total = part if total is None else total + part
    refs.frames[...] = total.reshape(steps, rows_dev, lanes)
    for i in range(count - depth, count):
        stores[i].wait()


def body(
    codes,
    actions,
    frames,
    segment_ids,
    targets,
    codebook,
    action_table,
    slot_table,
    ln1_gain,
    ln1_bias,
    w_qkv,
    w_out,
    b_out,
    ln2_gain,
    ln2_bias,
    w_up,
    b_up,
    w_down,
    b_down,
    lnf_gain,
    lnf_bias,
    w_head,
    b_head,
):
    layers, width, ff = w_up.shape
    classes, n_codes = w_head.shape[1], codebook.shape[0]
    sections, dp_count = lax.axis_size("section"), lax.axis_size("dp")
    rows_dev, slots = codes.shape
    rows = rows_dev // sections
    tokens = rows * slots
    frames_t = jnp.transpose(frames, (1, 0, 2))
    units = make_units(layers, ff, classes, n_codes)
    line = dp_count // 2
    if sections != 4 or dp_count != 2 * line or line != 4 or units[-1][0] + units[-1][1] != sum(SIZES):
        line = 0

    vmem, hbm = pl.BlockSpec(memory_space=pltpu.VMEM), pl.BlockSpec(memory_space=pl.ANY)
    small = dict(
        codes=codes,
        actions=actions,
        segs=segment_ids,
        targets=targets,
        action_table=action_table,
        slot_table=slot_table,
        ln1_gain=ln1_gain,
        ln1_bias=ln1_bias,
        b_out=b_out,
        ln2_gain=ln2_gain,
        ln2_bias=ln2_bias,
        b_down=b_down,
        b_up=b_up,
        lnf_gain=lnf_gain[None],
        lnf_bias=lnf_bias[None],
        b_head=b_head[None],
        held_frames=frames_t,
    )
    large = dict(
        codebook=codebook, w_qkv=w_qkv, w_out=w_out, w_up=w_up, w_down=w_down, w_head=w_head
    )
    total_rows = units[-1][0] + units[-1][1]
    layer_blocks = 4 + 2 * ff // BLOCK
    early_units = classes // BLOCK + layer_blocks
    early_rows, late_rows = 0, 0
    parts, early_parts = make_parts(early_units * BLOCK)
    for i, (start, size) in enumerate(parts):
        taken = Exchange.landing_rows(size, KINDS[i])
        early_rows, late_rows = (
            early_rows + taken * (i < early_parts),
            late_rows + taken * (i >= early_parts),
        )
    outs = dict(
        result=jax.ShapeDtypeStruct((total_rows, width), BF),
        back=jax.ShapeDtypeStruct((sections, tokens, frames.shape[2]), BF),
    )
    buffers = dict(
        qkv=((layers, tokens, 3 * width), BF),
        probs=((layers, rows, HEADS // 2, 2 * slots, slots), BF),
        o=((layers, tokens, width), BF),
        hat1=((layers, tokens, width), BF),
        inv1=((layers, tokens, LANES), F32),
        hat2=((layers, tokens, width), BF),
        inv2=((layers, tokens, LANES), F32),
        m=((layers, tokens, ff), BF),
        slope=((layers, tokens, ff), BF),
        int_rows=((slots, slots), F32),
        int_cols=((slots, slots), F32),
        bias=((rows, slots, slots), F32),
        h=((tokens, width), BF),
        x1=((tokens, width), F32),
        invf=((tokens, LANES), F32),
        dz=((tokens, classes), BF),
        sums=((ACTION_ROWS, width), F32),
        big=((tokens, width), F32),
        dx1r=((tokens, width), BF),
        frames=((sections, rows * STEP_PLACES, frames.shape[2]), BF),
        sent_frames=((sections, rows * STEP_PLACES, frames.shape[2]), BF),
        first_weights=((layer_blocks * BLOCK, width), BF),
        late=((max(late_rows, layer_blocks * BLOCK + n_codes), width), BF),
        early=((early_rows, width), BF),
        total=((total_rows, width), BF),
    )
    scratch = {name: pltpu.VMEM(*what) for name, what in buffers.items()}
    held = {name: pltpu.VMEM(array.shape, array.dtype) for name, array in small.items()}
    scratch.update(
        weight_sems=pltpu.SemaphoreType.DMA((1 + classes // BLOCK + layers * layer_blocks,)),
        frame_sems=pltpu.SemaphoreType.DMA((5, sections)),
        own_sems=pltpu.SemaphoreType.DMA((len(parts),)),
        send_sems=pltpu.SemaphoreType.DMA((len(parts),)),
        recv_sems=pltpu.SemaphoreType.DMA((9 * len(parts),)),
        free_sem=pltpu.SemaphoreType.REGULAR,
        small_sems=pltpu.SemaphoreType.DMA((len(small),)),
    )
    names = tuple(large) + tuple(outs) + tuple(scratch)
    result, back = pl.pallas_call(
        functools.partial(gradient_kernel, tuple(small), names, units, line, rows),
        out_shape=tuple(outs.values()),
        in_specs=[hbm] * (len(small) + len(large)),
        out_specs=(hbm, hbm),
        scratch_shapes=list(scratch.values()) + list(held.values()),
        compiler_params=pltpu.CompilerParams(
            collective_id=0, has_side_effects=True, vmem_limit_bytes=VMEM_LIMIT
        ),
    )(*small.values(), *large.values())
    if not line:
        result = lax.psum(result, ("dp", "section"))

    depth = 12
    sources = dict(result=result, back=back)
    wide = dict(
        head=(width, classes),
        down=(layers, ff, width),
        up=(layers, width, ff),
        out=(layers, width, width),
        qkv=(layers, width, 3 * width),
        table=(n_codes, width),
        action_table=action_table.shape,
        slot_table=slot_table.shape,
        ln1_gain=(layers, width),
        ln1_bias=(layers, width),
        b_out=(layers, width),
        ln2_gain=(layers, width),
        ln2_bias=(layers, width),
        b_down=(layers, width),
        b_up=(layers, ff),
        lnf_gain=(1, width),
        lnf_bias=(1, width),
        b_head=(1, classes),
        frames=frames_t.shape,
    )
    count = len(units)
    held = dict(
        narrow=pltpu.VMEM((depth, BLOCK, width), BF),
        wide=pltpu.VMEM((depth, BLOCK, width), F32),
        tiny=pltpu.VMEM((SMALL_ROWS, width), BF),
        v_back=pltpu.VMEM(back.shape, BF),
        load_sems=pltpu.SemaphoreType.DMA((count + 2,)),
        store_sems=pltpu.SemaphoreType.DMA((count,)),
    )
    names = tuple(sources) + tuple(wide) + tuple(held)
    converted = pl.pallas_call(
        functools.partial(convert_kernel, names, units, layers, ff, classes, n_codes),
        out_shape=tuple(jax.ShapeDtypeStruct(shape, F32) for shape in wide.values()),
        in_specs=[hbm, hbm],
        out_specs=(hbm,) * 6 + (vmem,) * (len(wide) - 6),
        scratch_shapes=list(held.values()),
        compiler_params=pltpu.CompilerParams(vmem_limit_bytes=VMEM_LIMIT),
    )(result, back)

    by_name = SimpleNamespace(**dict(zip(wide, converted)))
    return (
        by_name.table,
        by_name.action_table,
        by_name.slot_table,
        by_name.ln1_gain,
        by_name.ln1_bias,
        by_name.qkv,
        by_name.out,
        by_name.b_out,
        by_name.ln2_gain,
        by_name.ln2_bias,
        by_name.up,
        by_name.b_up,
        by_name.down,
        by_name.b_down,
        by_name.lnf_gain.reshape(-1),
        by_name.lnf_bias.reshape(-1),
        by_name.head,
        by_name.b_head.reshape(-1),
        jnp.transpose(by_name.frames, (1, 0, 2)),
    )


def solution(mesh):
    placed = (
        P("dp", None),
        P("dp", None),
        P("dp", None, "section"),
        P("dp", None),
        P("dp", None),
        P(),
        P(),
        P(),
        P(),
        P(),
        P(),
        P(),
        P(),
        P(),
        P(),
        P(),
        P(),
        P(),
        P(),
        P(),
        P(),
        P(),
        P(),
    )
    return jax.shard_map(
        body,
        mesh=mesh,
        in_specs=placed,
        out_specs=(
            P(),
            P(),
            P(),
            P(),
            P(),
            P(),
            P(),
            P(),
            P(),
            P(),
            P(),
            P(),
            P(),
            P(),
            P(),
            P(),
            P(),
            P(),
            P("dp", None, "section"),
        ),
        check_vma=False,
    )
```

```python
import functools
from types import SimpleNamespace

import jax
import jax.numpy as jnp
from jax import lax
from jax.experimental import pallas as pl
from jax.experimental.pallas import tpu as pltpu
from jax.sharding import PartitionSpec as P

HEADS = 8
HEAD_DIM = 64
STEPS = 21
STEP_LEN = 6
GELU_C = 0.7978845608028654
EPS = 1e-05
NEG = -1e30
BF = jnp.bfloat16
F32 = jnp.float32
LANES = 128
BLOCK = 512
SMALL_ROWS = 64
SMALL_BLOCK = 256
STEP_PLACES = 24
QKV, OUT, UP, DOWN = 0, 3, 4, 8
VMEM_LIMIT = 63 * 2**20
MESH = pl.DeviceIdType.MESH


def dot_nn(left, right):
    return lax.dot_general(left, right, (((1,), (0,)), ((), ())), preferred_element_type=F32)


def dot_nt(left, right):
    return lax.dot_general(left, right, (((1,), (1,)), ((), ())), preferred_element_type=F32)


def dot_tn(left, right):
    return lax.dot_general(left, right, (((0,), (0,)), ((), ())), preferred_element_type=F32)


def dot_exact(left, right):
    return lax.dot_general(
        left,
        right,
        (((1,), (0,)), ((), ())),
        precision=lax.Precision.HIGHEST,
        preferred_element_type=F32,
    )


def gelu_both(values):
    squared = values * values
    tanh_part = jnp.tanh(GELU_C * values * (1.0 + 0.044715 * squared))
    half = 0.5 * (1.0 + tanh_part)
    inner_slope = GELU_C * (1.0 + 3 * 0.044715 * squared)
    slope = half + 0.5 * values * (1.0 - tanh_part * tanh_part) * inner_slope
    return (values * half, slope)


def iota(shape, dimension):
    return lax.broadcasted_iota(jnp.int32, shape, dimension)


def step_of(slots):
    return (slots * 43) >> 8


def lane_wide(column):
    return jnp.broadcast_to(column, (column.shape[0], LANES))


def columns_of(column, width):
    return jnp.concatenate([column] * (width // LANES), axis=1)


def norm_chunk(values, gain, bias):
    width = values.shape[1]
    centred = values - jnp.sum(values, -1, keepdims=True) * (1.0 / width)
    inverse = lax.rsqrt(jnp.sum(centred * centred, -1, keepdims=True) * (1.0 / width) + EPS)
    hat = centred * inverse
    return (hat * gain + bias, hat, inverse)


def norm_back_chunk(upstream, hat, inverse, gain):
    width = upstream.shape[1]
    scaled = upstream * gain
    mean_scaled = jnp.sum(scaled, -1, keepdims=True) * (1.0 / width)
    mean_prod = jnp.sum(scaled * hat, -1, keepdims=True) * (1.0 / width)
    inner = scaled - mean_scaled - hat * mean_prod
    return (
        columns_of(inverse, width) * inner,
        jnp.sum(upstream * hat, 0, keepdims=True),
        jnp.sum(upstream, 0, keepdims=True),
    )


ACTION_ROWS = 32
VECTOR_ROWS = 24


def compute(refs):
    tick = refs.tick
    codes, actions, segs, targets = refs.codes, refs.actions, refs.segs, refs.targets
    own = refs.own
    rows, slots = refs.rows, codes.shape[1]
    tokens = rows * slots
    width = refs.width
    layers = refs.layers
    ff = refs.ff
    classes = refs.classes
    n_codes = refs.n_codes
    wait_weight = refs.wait_weight
    put = refs.put
    chunk = LANES

    def chunks(body):
        for i in range(tokens // chunk):
            body(i * chunk)

    refs.wait_small()

    first = own * rows
    slot_row = iota((rows, slots), 1)
    step_row = step_of(slot_row)
    phase_row = slot_row - step_row * STEP_LEN
    real = slot_row < STEPS * STEP_LEN
    spread = (
        (step_of(iota((STEPS, slots), 1)) == iota((STEPS, slots), 0))
        & (iota((STEPS, slots), 1) == STEP_LEN * iota((STEPS, slots), 0))
    ).astype(F32)
    action_row = dot_exact(actions[pl.ds(first, rows), :].astype(F32), spread)
    code_row = codes[pl.ds(first, rows), :].astype(F32)
    index_row = jnp.where(
        real & (phase_row >= 2),
        code_row,
        jnp.where(real & (phase_row == 0), action_row + float(n_codes), -1.0),
    )
    seg_row = segs[pl.ds(first, rows), :].astype(F32)
    target_row = targets[pl.ds(first, rows), :].astype(F32)
    stacked = jnp.concatenate(
        [index_row, seg_row, target_row, jnp.zeros((slots - 3 * rows, slots), F32)], 0
    )
    refs.int_rows[...] = stacked
    refs.int_cols[...] = jnp.transpose(stacked)
    int_rows, int_cols = refs.int_rows, refs.int_cols

    k_step = step_of(iota((slots, slots), 0))
    q_step = step_of(iota((slots, slots), 1))
    for r in range(rows):
        same = int_cols[:, rows + r : rows + r + 1] == int_rows[rows + r : rows + r + 1, :]
        refs.bias[r] = jnp.where(same & (k_step <= q_step), 0.0, NEG)

    phase_col = iota((slots, 8), 0) - STEP_LEN * step_of(iota((slots, 8), 0))
    slot_one = (phase_col == iota((slots, 8), 1)).astype(F32)
    table = jnp.concatenate([refs.slot_table[...], jnp.zeros((8 - STEP_LEN, width), F32)], 0)
    slot_part = dot_exact(slot_one, table)
    h = refs.h
    refs.send_frames()
    n_actions = refs.action_table.shape[0]
    action_table = jnp.concatenate(
        [
            refs.action_table[...].astype(F32),
            jnp.zeros((ACTION_ROWS - n_actions, width), F32),
        ],
        0,
    ).astype(BF)
    refs.wait_codebook()
    x1 = refs.x1
    for r in range(rows):
        tok = slice(r * slots, (r + 1) * slots)
        col = int_cols[:, r : r + 1]
        one = (col == iota((slots, n_codes), 1).astype(F32)).astype(BF)
        part = dot_nn(one, refs.codebook[...])
        one = (col == (iota((slots, ACTION_ROWS), 1) + n_codes).astype(F32)).astype(BF)
        x1[tok, :] = part + dot_nn(one, action_table) + slot_part
    refs.wait_frames()
    frames = refs.frames
    sections, places, frame_width = frames.shape
    for r in range(rows):
        tok = slice(r * slots, (r + 1) * slots)
        j = iota((slots, places), 0)
        js = step_of(j)
        frame_one = (
            (iota((slots, places), 1) == r * STEP_PLACES + js)
            & (j - js * STEP_LEN == 1)
            & (j < STEPS * STEP_LEN)
        ).astype(BF)
        frame_part = jnp.concatenate(
            [dot_nn(frame_one, frames[k]) for k in range(sections)], 1
        )
        h[tok, :] = (x1[tok, :] + frame_part).astype(BF)
    refs.load_head()

    lane = iota((slots, LANES), 1)
    low_half = lane < HEAD_DIM
    pairs = HEADS // 2

    def both_heads(tile):
        zero = jnp.zeros_like(tile)
        return jnp.concatenate(
            [jnp.where(low_half, tile, zero), jnp.where(low_half, zero, tile)], 0
        )

    def pick_heads(stacked_pair):
        return jnp.where(low_half, stacked_pair[:slots], stacked_pair[slots:])

    def row_blocks(body):
        for r in range(rows):
            body(r, r * slots)

    def block_of(weights, j):
        return weights[pl.ds(j * BLOCK, BLOCK), :]

    def back_through(given, weights, first_block, count):
        for j in range(count):
            part = dot_nt(
                given[:, j * BLOCK : (j + 1) * BLOCK], block_of(weights, first_block + j)
            )
            big[...] = part if j == 0 else big[...] + part

    big = refs.big
    normal = refs.dx1r
    for layer in range(layers):
        qkv, probs, o = (k.at[layer] for k in (refs.qkv, refs.probs, refs.o))
        hat1, inv1, hat2, inv2 = (
            k.at[layer] for k in (refs.hat1, refs.inv1, refs.hat2, refs.inv2)
        )
        m, slope = (k.at[layer] for k in (refs.m, refs.slope))
        gain1, bias1 = refs.ln1_gain[layer : layer + 1, :], refs.ln1_bias[layer : layer + 1, :]
        gain2, bias2 = refs.ln2_gain[layer : layer + 1, :], refs.ln2_bias[layer : layer + 1, :]

        def norm_one(at):
            normed, hat, inverse = norm_chunk(h[pl.ds(at, chunk), :].astype(F32), gain1, bias1)
            normal[pl.ds(at, chunk), :] = normed.astype(BF)
            hat1[pl.ds(at, chunk), :] = hat.astype(BF)
            inv1[pl.ds(at, chunk), :] = lane_wide(inverse)

        chunks(norm_one)
        weights = refs.weights[layer]
        wait_weight(layer, QKV, 3)

        for j in range(3 * width // BLOCK):
            at = slice(j * BLOCK, (j + 1) * BLOCK)
            qkv[:, at] = dot_nn(normal[...], block_of(weights, QKV + j)).astype(BF)

        def attend(r, at):
            tok = pl.ds(at, slots)
            bias = refs.bias[r]
            cuts = [slice(pair * LANES, (pair + 1) * LANES) for pair in range(pairs)]
            query, key, value = (
                [qkv[tok, part * width + cut.start : part * width + cut.stop] for cut in cuts]
                for part in range(3)
            )
            scores = [dot_nt(both_heads(key[i]), query[i]) for i in range(pairs)]
            weights_low = []
            for s in scores:
                parts = []
                for half in (s[:slots], s[slots:]):
                    half = half * HEAD_DIM ** (-0.5) + bias
                    top = jnp.max(half, 0, keepdims=True)
                    expo = jnp.exp(half - top)
                    total = jnp.sum(expo, 0, keepdims=True)
                    parts.append((expo * (1.0 / total)).astype(BF))
                weights_low.append(jnp.concatenate(parts, 0))
            mixed = [dot_tn(weights_low[i], both_heads(value[i])) for i in range(pairs)]
            for i in range(pairs):
                probs[r, i] = weights_low[i]
                o[tok, cuts[i]] = mixed[i].astype(BF)

        row_blocks(attend)
        wait_weight(layer, OUT, 1)
        x1[...] = dot_nn(o[...], block_of(weights, OUT))
        b_out = refs.b_out[layer : layer + 1, :]

        def norm_two(at):
            tok = pl.ds(at, chunk)
            resid = h[tok, :].astype(F32) + x1[tok, :] + b_out
            x1[tok, :] = resid
            normed, hat, inverse = norm_chunk(resid, gain2, bias2)
            normal[tok, :] = normed.astype(BF)
            hat2[tok, :] = hat.astype(BF)
            inv2[tok, :] = lane_wide(inverse)

        chunks(norm_two)
        wait_weight(layer, UP, ff // BLOCK)
        b_up = refs.b_up

        for j in range(ff // BLOCK):
            at = slice(j * BLOCK, (j + 1) * BLOCK)
            u = dot_nn(normal[...], block_of(weights, UP + j)) + b_up[layer : layer + 1, at]
            hidden, bent = gelu_both(u)
            m[:, at] = hidden.astype(BF)
            slope[:, at] = bent.astype(BF)

        b_down = refs.b_down[layer : layer + 1, :]
        wait_weight(layer, DOWN, ff // BLOCK)
        w_down = weights[DOWN * BLOCK : DOWN * BLOCK + ff, :]
        h[...] = (x1[...] + dot_nn(m[...], w_down) + b_down).astype(BF)

    gain, bias_f = refs.lnf_gain[...], refs.lnf_bias[...]
    f, hatf, invf, dz = refs.dx1r, refs.x1, refs.invf, refs.dz
    sums = refs.sums
    sums[...] = jnp.zeros_like(sums)

    def add_row(row, value, width_at=0):
        sums[row : row + 1, width_at : width_at + value.shape[1]] += value

    def norm_final(at):
        tok = pl.ds(at, chunk)
        normed, hat, inverse = norm_chunk(h[tok, :].astype(F32), gain, bias_f)
        f[tok, :] = normed.astype(BF)
        hatf[tok, :] = hat
        invf[tok, :] = lane_wide(inverse)

    chunks(norm_final)
    refs.wait_head()
    w_head = refs.w_head
    phase_one = iota((slots, 1), 0) - STEP_LEN * step_of(iota((slots, 1), 0))
    for r in range(rows):
        tok = slice(r * slots, (r + 1) * slots)
        logits = [
            dot_nn(f[tok, :], w_head[j * width : (j + 1) * width, :])
            for j in range(classes // BLOCK)
        ]
        logits = jnp.concatenate(logits, 1) + refs.b_head[...]
        top = jnp.max(logits, -1, keepdims=True)
        expo = jnp.exp(logits - top)
        total = jnp.sum(expo, -1, keepdims=True)
        chosen = (
            (int_cols[:, rows + r : rows + r + 1] != 0.0) & (phase_one >= 1) & (phase_one <= 4)
        )
        weight = jnp.where(chosen, 1.0 / (4 * STEPS), 0.0)
        wanted = int_cols[:, 2 * rows + r : 2 * rows + r + 1]
        hit = wanted == iota((slots, classes), 1).astype(F32)
        delta = expo * (weight / total) - jnp.where(hit, weight, 0.0)
        low = delta.astype(BF)
        dz[tok, :] = low
        part = jnp.sum(low.astype(F32), 0, keepdims=True)
        for block in range(classes // BLOCK):
            add_row(VECTOR_ROWS - 2 + block, part[:, block * BLOCK : (block + 1) * BLOCK])
    for block in range(classes // BLOCK):
        at = slice(block * BLOCK, (block + 1) * BLOCK)
        put(dot_tn(f[...], dz[:, at]))
        tick()
    back_through(dz, w_head, 0, classes // BLOCK)
    dy = h

    def final_back(at):
        tok = pl.ds(at, chunk)
        back, gain_sum, bias_sum = norm_back_chunk(
            big[tok, :], hatf[tok, :], invf[tok, :], gain
        )
        dy[tok, :] = back.astype(BF)
        add_row(VECTOR_ROWS - 4, gain_sum)
        add_row(VECTOR_ROWS - 3, bias_sum)

    chunks(final_back)
    tick()

    for layer in reversed(range(layers)):
        qkv, probs, o = (k.at[layer] for k in (refs.qkv, refs.probs, refs.o))
        hat1, inv1, hat2, inv2 = (
            k.at[layer] for k in (refs.hat1, refs.inv1, refs.hat2, refs.inv2)
        )
        m, slope = (k.at[layer] for k in (refs.m, refs.slope))
        weights = refs.weights[layer]
        gain1, gain2 = refs.ln1_gain[layer : layer + 1, :], refs.ln2_gain[layer : layer + 1, :]
        du = slope
        base = layer * 10
        dsum = jnp.zeros((1, width), F32)
        for i in range(tokens // chunk):
            dsum = dsum + jnp.sum(dy[i * chunk : (i + 1) * chunk, :].astype(F32), 0, keepdims=True)
        add_row(base + 5, dsum)

        for j in range(ff // BLOCK):
            at = slice(j * BLOCK, (j + 1) * BLOCK)
            put(dot_tn(m[:, at], dy[...]))
            tick()
        bias1, bias2 = refs.ln1_bias[layer : layer + 1, :], refs.ln2_bias[layer : layer + 1, :]

        def normal_again(hat, gain, bias):
            def one(at):
                tok = pl.ds(at, chunk)
                normal[tok, :] = (hat[tok, :].astype(F32) * gain + bias).astype(BF)

            chunks(one)

        normal_again(hat2, gain2, bias2)
        for j in range(ff // BLOCK):
            at = slice(j * BLOCK, (j + 1) * BLOCK)
            low = (dot_nt(dy[...], block_of(weights, DOWN + j)) * slope[:, at].astype(F32)).astype(BF)
            du[:, at] = low
            add_row(base + 6 + j, jnp.sum(low.astype(F32), 0, keepdims=True))
            put(dot_tn(normal[...], low))
            tick()
        back_through(du, weights, UP, ff // BLOCK)
        tick()

        dx1, dx1r = refs.x1, refs.dx1r

        def second_back(at):
            tok = pl.ds(at, chunk)
            back, gain_sum, bias_sum = norm_back_chunk(
                big[tok, :], hat2[tok, :].astype(F32), inv2[tok, :], gain2
            )
            total = dy[tok, :].astype(F32) + back
            dx1[tok, :] = total
            low = total.astype(BF)
            dx1r[tok, :] = low
            add_row(base + 3, gain_sum)
            add_row(base + 4, bias_sum)
            add_row(base + 2, jnp.sum(low.astype(F32), 0, keepdims=True))

        chunks(second_back)
        put(dot_tn(o[...], dx1r[...]))
        do = o
        do[...] = dot_nt(dx1r[...], block_of(weights, OUT)).astype(BF)
        tick()
        dqkv = qkv

        def attend_back(r, at):
            tok = pl.ds(at, slots)
            cuts = [slice(pair * LANES, (pair + 1) * LANES) for pair in range(pairs)]
            query, key, value = (
                [qkv[tok, part * width + cut.start : part * width + cut.stop] for cut in cuts]
                for part in range(3)
            )
            given = [do[tok, cut] for cut in cuts]
            dp = [dot_nt(both_heads(value[i]), given[i]) for i in range(pairs)]
            p = [probs[r, i] for i in range(pairs)]
            dv = [dot_nn(p[i], given[i]) for i in range(pairs)]
            ds = []
            for i in range(pairs):
                parts = []
                for cut in (slice(0, slots), slice(slots, 2 * slots)):
                    p_f = p[i][cut].astype(F32)
                    prod = p_f * dp[i][cut]
                    total = jnp.sum(prod, 0, keepdims=True)
                    parts.append((prod - p_f * total).astype(BF))
                ds.append(jnp.concatenate(parts, 0))
            scale = HEAD_DIM ** (-0.5)
            dq = [dot_tn(ds[i], both_heads(key[i])) for i in range(pairs)]
            dk = [dot_nn(ds[i], query[i]) for i in range(pairs)]
            for i in range(pairs):
                at_q, at_k, at_v = (
                    slice(part * width + cuts[i].start, part * width + cuts[i].stop)
                    for part in range(3)
                )
                dqkv[tok, at_q] = (dq[i] * scale).astype(BF)
                dqkv[tok, at_k] = (pick_heads(dk[i]) * scale).astype(BF)
                dqkv[tok, at_v] = pick_heads(dv[i]).astype(BF)

        half_rows = rows // 2
        for start in (0, half_rows):

            def some(r, carry):
                attend_back(r, pl.multiple_of(r * slots, slots))
                return carry

            lax.fori_loop(start, start + half_rows, some, 0)
            tick()
        normal_again(hat1, gain1, bias1)
        for j in range(3 * width // BLOCK):
            at = slice(j * BLOCK, (j + 1) * BLOCK)
            put(dot_tn(normal[...], dqkv[:, at]))
            tick()
        back_through(dqkv, weights, QKV, 3)
        tick()

        def first_back(at):
            tok = pl.ds(at, chunk)
            back, gain_sum, bias_sum = norm_back_chunk(
                big[tok, :], hat1[tok, :].astype(F32), inv1[tok, :], gain1
            )
            dy[tok, :] = (dx1[tok, :] + back).astype(BF)
            add_row(base + 0, gain_sum)
            add_row(base + 1, bias_sum)

        chunks(first_back)
        if layer == layers - 1:
            refs.layer_done()
        tick()

    refs.send_back()
    index_rows = jnp.concatenate([int_rows[r : r + 1, :] for r in range(rows)], 1)
    half = n_codes // 2
    for block in range(2):
        one = (index_rows == (iota((half, tokens), 0) + block * half).astype(F32)).astype(BF)
        put(dot_nn(one, dy[...]))
        tick()
    token = iota((8, tokens), 1)
    slot = token & (slots - 1)
    slot_hit = (slot - STEP_LEN * step_of(slot) == iota((8, tokens), 0)).astype(BF)
    one = (index_rows == (iota((ACTION_ROWS, tokens), 0) + n_codes).astype(F32)).astype(BF)
    sums[VECTOR_ROWS : VECTOR_ROWS + 8, :] = dot_nn(slot_hit, dy[...])
    rest = jnp.zeros((SMALL_BLOCK - SMALL_ROWS, width), F32)
    put(jnp.concatenate([dot_nn(one, dy[...]), sums[...], rest], 0))


class Exchange:
    def __init__(self, total, result, send_sems, recv_sems, own_sems, line):
        self.total, self.result = total, result
        self.own_sems, self.send_sems, self.recv_sems = own_sems, send_sems, recv_sems
        self.line = line
        dp, section = lax.axis_index("dp"), lax.axis_index("section")
        self.z, self.y = dp // 2, dp % 2
        self.x, self.core = section // 2, section % 2
        self.bit = (
            self.x + self.core * (self.y - self.x),
            self.y + self.core * (self.x - self.y),
        )
        flip_x, flip_y = 1 - 2 * self.x, 1 - 2 * self.y
        self.near = (
            self.device(self.x + (1 - self.core) * flip_x, self.y + self.core * flip_y),
            self.device(self.x + self.core * flip_x, self.y + (1 - self.core) * flip_y),
        )
        self.twin = (dp, section + 1 - 2 * self.core)
        self.corner = (dp, 3 - section)
        self.above = (dp + 2, section)
        self.below = (dp - 2, section)
        self.side = self.z // (line // 2)
        self.inner = (dp + 2 - 4 * self.side, section)
        self.outer = (dp - 2 + 4 * self.side, section)

    def device(self, x, y):
        return (self.z * 2 + y, x * 2 + self.core)

    def neighbours(self):
        last = self.line - 1
        lines = (self.z + last - 1) // last + (2 * last - 1 - self.z) // last
        return 4 + lines

    def signal_all(self, semaphore):
        for other in (self.twin, *self.near, self.corner):
            pl.semaphore_signal(semaphore, inc=1, device_id=other, device_id_type=MESH)

        @pl.when(self.z < self.line - 1)
        def _():
            pl.semaphore_signal(semaphore, inc=1, device_id=self.above, device_id_type=MESH)

        @pl.when(self.z > 0)
        def _():
            pl.semaphore_signal(semaphore, inc=1, device_id=self.below, device_id_type=MESH)

    @staticmethod
    def landing_rows(size, kind):
        half = size // 2
        return (2 * half + half // 8, 2 * half, 2 * half + 3 * half // 4 + half // 8)[kind]

    def rows(self, ref, at, count):
        return ref.at[pl.ds(pl.multiple_of(at, 16), count)]

    def add(self, at, landing, landed, count):
        step = next(rows for rows in (64, 48, 32, 16) if count % rows == 0)

        def one(i, carry):
            here = pl.ds(pl.multiple_of(at + i * step, 16), step)
            there = pl.ds(pl.multiple_of(landed + i * step, 16), step)
            self.total[here, :] = (
                self.total[here, :].astype(F32) + landing[there, :].astype(F32)
            ).astype(BF)
            return carry

        if count == step:
            one(0, 0)
        else:
            lax.fori_loop(0, count // step, one, 0)

    def stages(self, i, start, size, kind, landing, landing_at, middle):
        z, last, side = self.z, self.line - 1, self.side
        total, result = self.total, self.result
        own_sem, send_sem = self.own_sems.at[i], self.send_sems.at[i]
        first_sem = 9 * i
        half = size // 2
        own = start + self.core * half
        end = not middle

        def when(condition):
            if isinstance(condition, bool):
                return lambda body: body() if condition else None
            return lambda body: pl.when(condition)(body)

        def copy(k, source, target, other):
            return lambda: pltpu.make_async_remote_copy(
                src_ref=source,
                dst_ref=target,
                send_sem=send_sem,
                recv_sem=self.recv_sems.at[first_sem + k],
                device_id=other,
                device_id_type=MESH,
            )

        def send(*copies):
            for make in copies:
                make().start()

        def wait(*copies):
            for make in copies:
                make().wait_recv()

        def give(k, at, count, landed, other):
            return copy(k, self.rows(total, at, count), self.rows(landing, landed, count), other)

        def back(k, at, count, other, source=result):
            return copy(k, self.rows(source, at, count), self.rows(result, at, count), other)

        def keep(at, count):
            return lambda: pltpu.make_async_copy(
                self.rows(total, at, count), self.rows(result, at, count), own_sem
            )

        twin = give(0, start + (1 - self.core) * half, half, landing_at, self.twin)
        twin_back = back(8, own, half, self.twin)
        free = landing_at + half

        def twin_done():
            wait(twin)
            self.add(own, landing, landing_at, half)

        def swaps(base, count, free):
            part, bit = count // 2, self.bit
            base1 = base + bit[0] * part
            first = give(1, base + (1 - bit[0]) * part, part, free, self.near[0])
            base2 = base1 + bit[1] * (part // 2)
            second = give(
                2, base1 + (1 - bit[1]) * (part // 2), part // 2, free + part, self.near[1]
            )

            def first_done():
                wait(first)
                self.add(base1, landing, free, part)

            def second_done():
                wait(second)
                self.add(base2, landing, free + part, part // 2)

            return first, first_done, base1, second, second_done, base2

        def middle_line(base, count, free, source):
            part = count // 2
            mine, other = base + side * part, base + (1 - side) * part
            inward = give(3, base, count, free, self.inner)
            across = give(4, other, part, free + count, self.inner)
            out_mine = back(3, mine, part, self.outer, source)
            across_back = back(5, mine, part, self.inner, source)
            out_other = back(4, other, part, self.outer)

            def start_line():
                when(end)(lambda: send(inward))

            def hop():
                @when(middle)
                def _():
                    wait(inward)
                    self.add(base, landing, free, count)
                    send(across)

            def hop_done():
                wait(across)
                self.add(mine, landing, free + count, part)

            def start_back():
                send(across_back, out_mine)

            def hop_back():
                wait(across_back)
                send(out_other)

            def ends_done():
                wait(out_mine, out_other)

            return mine, start_line, hop, hop_done, start_back, hop_back, ends_done

        def line_rows(ends, others):
            def all_sent(count):
                whole = self.rows(total, 0, count)
                return lambda: pltpu.make_async_copy(whole, whole, send_sem).wait()

            def finish():
                when(end)(all_sent(ends))
                when(middle)(all_sent(others))

            return finish

        if kind == 0:
            first, first_done, base1, second, second_done, base2 = swaps(own, half, free)
            rest = half // 4
            free += half // 2 + rest
            mine, start_line, hop, hop_done, start_back, hop_back, ends_done = middle_line(
                base2, rest, free, total
            )
            mine_kept = keep(mine, rest // 2)
            second_back = back(6, base2, rest, self.near[1])
            first_back = back(7, base1, half // 2, self.near[0])

            def s1():
                twin_done()
                send(first)

            def s2():
                first_done()
                send(second)

            def s3():
                second_done()
                start_line()

            def s5():
                @when(middle)
                def _():
                    hop_done()
                    start_back()
                    mine_kept().start()

            def s6():
                @when(middle)
                def _():
                    hop_back()
                    mine_kept().wait()
                    send(second_back)

            def s7():
                @when(end)
                def _():
                    ends_done()
                    send(second_back)

            def s8():
                wait(second_back)
                send(first_back)

            def s9():
                wait(first_back)
                send(twin_back)

            def s10():
                wait(twin_back)

            finish = line_rows(3 * half + 3 * half // 4, 4 * half)
            return [lambda: send(twin), s1, s2, s3, hop, s5, s6, s7, s8, s9, s10, finish]

        if kind == 2:
            mine, start_line, hop, hop_done, start_back, hop_back, ends_done = middle_line(
                own, half, free, result
            )
            first, first_done, base1, second, second_done, base2 = swaps(
                mine, half // 2, free + half + half // 2
            )
            mine_kept = keep(base2, half // 8)
            second_back = back(6, base2, half // 8, self.near[1], total)
            first_back = back(7, base1, half // 4, self.near[0])

            def s1():
                twin_done()
                start_line()

            def s3():
                @when(middle)
                def _():
                    hop_done()
                    send(first)

            def s4():
                @when(middle)
                def _():
                    first_done()
                    send(second)

            def s5():
                @when(middle)
                def _():
                    second_done()
                    send(second_back)
                    mine_kept().start()

            def s6():
                @when(middle)
                def _():
                    wait(second_back)
                    mine_kept().wait()
                    send(first_back)

            def s7():
                @when(middle)
                def _():
                    wait(first_back)
                    start_back()

            def s8():
                @when(middle)
                def _():
                    hop_back()
                    send(twin_back)

            def s9():
                @when(end)
                def _():
                    ends_done()
                    send(twin_back)

            def s10():
                wait(twin_back)

            finish = line_rows(3 * half, 4 * half + 3 * half // 4)
            return [lambda: send(twin), s1, hop, s3, s4, s5, s6, s7, s8, s9, s10, finish]

        part = half // 2
        low, high = own, own + part
        up = give(3, high, part, free, self.above)
        down = give(4, low, part, free + part, self.below)
        up_back = back(5, low, part, self.above)
        down_back = back(3, high, part, self.below)
        first, first_done, base1, second, second_done, base2 = swaps(
            own + side * part, part, free + side * part
        )
        mine_kept = keep(base2, half // 8)
        second_back = back(6, base2, half // 8, self.near[1], total)
        first_back = back(7, base1, half // 4, self.near[0])

        def up_hop(k):
            @when((z == k) if middle == (0 < k < last) else False)
            def _():
                wait(up)
                self.add(high, landing, free, part)
                if k < last:
                    send(up)

            @when((z == last - k) if middle == (0 < k < last) else False)
            def _():
                wait(down)
                self.add(low, landing, free + part, part)
                if k < last:
                    send(down)

            if k == last:
                when(end)(lambda: send(first))

        def back_hop(k):
            @when((z == k) if middle == (0 < k < last) else False)
            def _():
                wait(up_back)
                if k < last:
                    send(up_back)

            @when((z == last - k) if middle == (0 < k < last) else False)
            def _():
                wait(down_back)
                if k < last:
                    send(down_back)

            if k == last:
                send(twin_back)

        def s1():
            twin_done()
            when((z == 0) if end else False)(lambda: send(up))
            when((z == last) if end else False)(lambda: send(down))

        def t1():
            @when(end)
            def _():
                first_done()
                send(second)

        def t2():
            @when(end)
            def _():
                second_done()
                send(second_back)
                mine_kept().start()

        def t3():
            @when(end)
            def _():
                wait(second_back)
                mine_kept().wait()
                send(first_back)

        def t4():
            when(end)(lambda: wait(first_back))
            when((z == 0) if end else False)(lambda: send(up_back))
            when((z == last) if end else False)(lambda: send(down_back))

        def t5():
            wait(twin_back)

        hops = [functools.partial(up_hop, k) for k in range(1, last + 1)]
        hops_back = [functools.partial(back_hop, k) for k in range(1, last + 1)]
        finish = line_rows(3 * half + 3 * half // 4, 4 * half)
        return [lambda: send(twin), s1, *hops, t1, t2, t3, t4, *hops_back, t5, finish]


SIZES = (1024, 1024, 1024, 1024, 512, 512, 512, 1536, 1024, 1024, 512, 512, 512, 512, 512, 512, 512, 512, 512, 512, 256)
KINDS = (0, 1, 0, 0, 0, 2, 1, 0, 0, 0, 0, 0, 0, 2, 0, 0, 2, 0, 0, 0, 0)
PLAN_ENDS = (
    (),
    (),
    (0,),
    (),
    (),
    (16,),
    (),
    (32, 1,),
    (),
    (17, 18, 19,),
    (33, 48,),
    (64,),
    (80,),
    (49, 65,),
    (2,),
    (81, 82, 83, 84, 85, 86, 96,),
    (),
    (),
    (),
    (),
    (),
    (34, 87, 88,),
    (97, 98, 99,),
    (),
    (112,),
    (50,),
    (128,),
    (66, 113,),
    (144, 3, 4,),
    (129, 160, 35, 36,),
    (145, 176,),
    (51, 52, 53, 54, 161, 192,),
    (177, 208,),
    (),
    (),
    (193,),
    (),
    (209, 210, 211, 212, 213, 214, 224,),
    (67, 68, 114,),
    (20,),
    (
        225, 130, 215, 216, 240, 256, 272, 146, 241, 257, 258, 259, 260, 261, 262, 100, 162,
        273, 178, 288, 194, 304, 289, 320, 305, 21, 115, 116, 117, 118, 321, 226, 131, 132, 133,
        134, 263, 264, 55, 147, 148, 149, 150, 101, 242, 5, 6, 163, 164, 274, 179, 180, 195,
        196, 197, 198, 290, 37, 38, 69, 70, 306, 22, 322, 227, 228, 229, 230, 56, 102, 243, 244,
        245, 246, 275, 276, 277, 278, 7, 291, 292, 293, 294, 23, 307, 308, 309, 310, 323, 324,
        325, 326, 181, 182, 165, 166, 57, 39, 103, 8, 58, 71, 24, 25, 26, 119, 40, 135, 104,
        105, 106, 9, 72, 120, 151, 10, 167, 183, 136, 199, 231, 41, 247, 121, 42, 89, 152, 73,
        279, 168, 122, 295, 90, 311, 74, 184, 200, 327, 137, 232, 248, 138, 27, 153, 28, 280,
        107, 169, 154, 296, 108, 170, 312, 185, 201, 328, 186, 233, 202, 217, 249, 234, 218,
        281, 250, 297, 265, 282, 313, 298, 329, 266, 314, 330,
    ),
)
PLAN_MIDDLE = (
    (),
    (),
    (0,),
    (),
    (),
    (16,),
    (),
    (32, 1,),
    (),
    (17,),
    (33, 48,),
    (64,),
    (80,),
    (49, 65,),
    (2, 81,),
    (96,),
    (),
    (),
    (),
    (),
    (),
    (),
    (34, 97,),
    (),
    (112, 18,),
    (50,),
    (128,),
    (66, 113,),
    (144, 3,),
    (129, 160,),
    (35, 82, 145, 176,),
    (19, 20, 21, 22, 23, 51, 161, 192,),
    (),
    (177, 98, 208,),
    (),
    (),
    (193,),
    (4, 83, 67, 209,),
    (114, 224,),
    (99, 100, 101, 102, 103, 104,),
    (
        36, 130, 225, 240, 256, 52, 146, 272, 241, 257, 162, 273, 24, 53, 178, 288, 194, 84,
        304, 68, 115, 210, 289, 320, 305, 54, 55, 321, 131, 226, 147, 211, 258, 163, 242, 274,
        5, 179, 195, 85, 116, 259, 37, 290, 132, 6, 7, 69, 306, 56, 117, 322, 148, 212, 227,
        243, 164, 38, 39, 275, 180, 260, 86, 133, 196, 70, 71, 118, 119, 228, 291, 149, 244,
        165, 8, 181, 276, 57, 307, 134, 135, 213, 323, 292, 197, 58, 229, 308, 324, 150, 151,
        245, 40, 166, 167, 87, 261, 182, 183, 72, 120, 277, 293, 198, 199, 230, 231, 9, 309,
        136, 214, 10, 325, 246, 247, 25, 88, 89, 278, 279, 294, 295, 90, 152, 105, 310, 311,
        262, 326, 327, 41, 168, 184, 26, 27, 42, 73, 121, 200, 28, 232, 106, 107, 74, 122, 108,
        137, 215, 248, 138, 280, 153, 296, 216, 217, 312, 154, 263, 169, 218, 185, 328, 170,
        201, 186, 233, 264, 265, 202, 249, 234, 266, 281, 250, 297, 282, 313, 298, 329, 314,
        330,
    ),
)


def make_units(layers, ff, classes, n_codes):
    count = classes // BLOCK + layers * (2 * ff // BLOCK + 4) + n_codes // BLOCK
    units = [(i * BLOCK, BLOCK) for i in range(count)]
    units.append((count * BLOCK, SMALL_BLOCK))
    return units


def make_parts(early_rows):
    parts = []
    start = 0
    for size in SIZES:
        parts.append((start, size))
        start += size
    return parts, sum(1 for start, size in parts if start < early_rows)


def gradient_kernel(small, names, units, line, rows, *args):
    count = len(small)
    refs = SimpleNamespace(**dict(zip(names, args[count:])))
    small_copies = []
    for i, (name, source, target) in enumerate(zip(small, args[:count], args[-count:])):
        setattr(refs, name, target)
        small_copies.append(pltpu.make_async_copy(source, target, refs.small_sems.at[i]))
        small_copies[-1].start()
    layers, width, ff = refs.w_up.shape
    classes, n_codes = refs.w_head.shape[1], refs.codebook.shape[0]
    layer_blocks = 4 + 2 * ff // BLOCK
    early_units = classes // BLOCK + layer_blocks
    dp, section = lax.axis_index("dp"), lax.axis_index("section")
    sections = lax.axis_size("section")

    exchange = None
    barrier = pltpu.get_barrier_semaphore()
    if line:
        exchange = Exchange(
            refs.total, refs.result, refs.send_sems, refs.recv_sems, refs.own_sems, line
        )
        exchange.signal_all(barrier)
    else:
        for step in range(1, sections):
            other = (dp, lax.rem(section + step, sections))
            pl.semaphore_signal(barrier, inc=1, device_id=other, device_id_type=MESH)

    sems = iter(range(refs.weight_sems.shape[0]))

    def load(source, target):
        copy = pltpu.make_async_copy(source, target, refs.weight_sems.at[next(sems)])
        copy.start()
        return copy

    spare = layer_blocks * BLOCK
    v_codebook = refs.late.at[spare : spare + n_codes]
    codebook_copy = load(refs.codebook, v_codebook)
    block_copies = {}
    layer_weights = [refs.first_weights, refs.late]
    for layer in range(layers):
        target = layer_weights[layer]
        for first, count, whole in (
            (QKV, 3, refs.w_qkv),
            (OUT, 1, refs.w_out),
            (UP, ff // BLOCK, refs.w_up),
        ):
            for j in range(count):
                block_copies[layer, first + j] = load(
                    whole.at[layer, :, pl.ds(j * BLOCK, BLOCK)],
                    target.at[pl.ds((first + j) * BLOCK, BLOCK)],
                )
        for j in range(ff // BLOCK):
            block_copies[layer, DOWN + j] = load(
                refs.w_down.at[layer, pl.ds(j * BLOCK, BLOCK)],
                target.at[pl.ds((DOWN + j) * BLOCK, BLOCK)],
            )
    head_place = refs.late.at[spare : spare + classes // BLOCK * width]
    head_sems = [next(sems) for _ in range(classes // BLOCK)]
    head_copies = [
        pltpu.make_async_copy(
            refs.w_head.at[:, pl.ds(j * BLOCK, BLOCK)],
            head_place.at[pl.ds(j * width, width)],
            refs.weight_sems.at[head_sems[j]],
        )
        for j in range(classes // BLOCK)
    ]

    def load_head():
        for copy in head_copies:
            copy.start()

    def wait_head():
        for copy in head_copies:
            copy.wait()


    def wait_weight(layer, first, count):
        for j in range(count):
            block_copies[layer, first + j].wait()

    frame_copies = []
    for step in range(1, sections):
        other = lax.rem(section + step, sections)
        frame_copies.append(
            pltpu.make_async_remote_copy(
                src_ref=refs.sent_frames.at[other],
                dst_ref=refs.frames.at[section],
                send_sem=refs.frame_sems.at[0, step - 1],
                recv_sem=refs.frame_sems.at[1, step - 1],
                device_id=(dp, other),
                device_id_type=MESH,
            )
        )

    def send_frames():
        steps, rows_dev, frame_width = refs.held_frames.shape
        n_all = steps * rows_dev
        flat = refs.held_frames[...].reshape(n_all, frame_width)
        place = iota((rows * STEP_PLACES, n_all), 0)
        row = (place * 43) >> 10
        step = place - row * STEP_PLACES
        column = iota((rows * STEP_PLACES, n_all), 1)
        for other in range(sections):
            hit = (column == step * rows_dev + row + other * rows) & (step < steps)
            refs.sent_frames[other] = dot_nn(hit.astype(BF), flat).astype(BF)
        refs.frames[section] = refs.sent_frames[section]
        if exchange is not None:
            pl.semaphore_wait(barrier, exchange.neighbours())
        else:
            pl.semaphore_wait(barrier, sections - 1)
        for copy in frame_copies:
            copy.start()

    def wait_frames():
        for copy in frame_copies:
            copy.wait()

    def wait_small():
        for copy in small_copies:
            copy.wait()

    back_copies = []

    def send_back():
        for step in range(1, sections):
            other = lax.rem(section + step, sections)
            at = pl.ds(pl.multiple_of(other * LANES, LANES), LANES)
            back_copies.append(
                pltpu.make_async_remote_copy(
                    src_ref=refs.h.at[:, at],
                    dst_ref=refs.back.at[section],
                    send_sem=refs.frame_sems.at[3, step - 1],
                    recv_sem=refs.frame_sems.at[4, step - 1],
                    device_id=(dp, other),
                    device_id_type=MESH,
                )
            )
        at = pl.ds(pl.multiple_of(section * LANES, LANES), LANES)
        back_copies.append(
            pltpu.make_async_copy(refs.h.at[:, at], refs.back.at[section], refs.frame_sems.at[2, 0])
        )
        for copy in back_copies:
            copy.start()

    stages = {False: [], True: []}
    if exchange is not None:
        parts, early_parts = make_parts(early_units * BLOCK)
        for middle in stages:
            offsets = [0, 0]
            for i, (start, size) in enumerate(parts):
                late = i >= early_parts
                landing = refs.late if late else refs.early
                stages[middle].append(
                    exchange.stages(i, start, size, KINDS[i], landing, offsets[late], middle)
                )
                offsets[late] += exchange.landing_rows(size, KINDS[i])
    ticks = iter(range(10**6))
    ready = []
    freed = []
    at_end = (exchange.z == 0) | (exchange.z == line - 1) if line else None

    def run(k):
        events = PLAN_ENDS[k] + PLAN_MIDDLE[k]
        if not freed and any(event // 16 >= early_parts for event in events):
            pl.semaphore_wait(refs.free_sem, exchange.neighbours())
            freed.append(True)

        @pl.when(at_end)
        def _():
            for event in PLAN_ENDS[k]:
                stages[False][event // 16][event % 16]()

        @pl.when(jnp.logical_not(at_end))
        def _():
            for event in PLAN_MIDDLE[k]:
                stages[True][event // 16][event % 16]()

    def tick():
        if exchange is not None:
            run(next(ticks))

    def put(value):
        start, size = units[len(ready)]
        refs.total[start : start + size, :] = value.astype(BF)
        ready.append(start)

    def layer_done():
        if exchange is not None:
            exchange.signal_all(refs.free_sem)

    view = SimpleNamespace(**vars(refs))
    view.codebook, view.w_head = v_codebook, head_place
    view.weights = layer_weights
    view.own, view.rows, view.width, view.layers = section, rows, width, layers
    view.ff, view.classes, view.n_codes = ff, classes, n_codes
    view.wait_weight, view.wait_frames = wait_weight, wait_frames
    view.send_frames, view.wait_small = send_frames, wait_small
    view.wait_codebook, view.wait_head = codebook_copy.wait, wait_head
    view.load_head = load_head
    view.tick, view.put, view.layer_done, view.send_back = tick, put, layer_done, send_back
    compute(view)
    if exchange is not None:
        for k in range(next(ticks), len(PLAN_ENDS)):
            run(k)

        @pl.when(at_end)
        def _():
            for stage in stages[False]:
                stage[-1]()

        @pl.when(jnp.logical_not(at_end))
        def _():
            for stage in stages[True]:
                stage[-1]()

    else:
        keep = pltpu.make_async_copy(refs.total, refs.result, refs.own_sems.at[0])
        keep.start()
        keep.wait()
    for copy in back_copies:
        copy.wait()


def convert_kernel(names, units, layers, ff, classes, n_codes, *args):
    refs = SimpleNamespace(**dict(zip(names, args)))
    depth = refs.narrow.shape[0]
    width = refs.narrow.shape[2]
    targets = []
    for j in range(classes // BLOCK):
        targets.append(refs.head.at[:, pl.ds(j * BLOCK, BLOCK)])
    for layer in reversed(range(layers)):
        for j in range(ff // BLOCK):
            targets.append(refs.down.at[layer, pl.ds(j * BLOCK, BLOCK)])
        for j in range(ff // BLOCK):
            targets.append(refs.up.at[layer, :, pl.ds(j * BLOCK, BLOCK)])
        targets.append(refs.out.at[layer])
        for j in range(3):
            targets.append(refs.qkv.at[layer, :, pl.ds(j * BLOCK, BLOCK)])
    for j in range(n_codes // BLOCK):
        targets.append(refs.table.at[pl.ds(j * BLOCK, BLOCK)])
    count = len(targets)
    loads, stores = [], []
    for i in range(count):
        start, size = units[i]
        loads.append(
            pltpu.make_async_copy(
                refs.result.at[pl.ds(start, size)], refs.narrow.at[i % depth], refs.load_sems.at[i]
            )
        )
        stores.append(
            pltpu.make_async_copy(refs.wide.at[i % depth], targets[i], refs.store_sems.at[i])
        )
    small_load = pltpu.make_async_copy(
        refs.result.at[pl.ds(units[count][0], SMALL_ROWS)], refs.tiny, refs.load_sems.at[count]
    )
    small_load.start()
    back_load = pltpu.make_async_copy(refs.back, refs.v_back, refs.load_sems.at[count + 1])
    back_load.start()
    for i in range(depth):
        loads[i].start()
    small_load.wait()
    small = refs.tiny[...].astype(F32)
    refs.action_table[...] = small[: refs.action_table.shape[0]]
    vectors = small[ACTION_ROWS:]
    refs.slot_table[...] = vectors[VECTOR_ROWS : VECTOR_ROWS + STEP_LEN]
    for layer in range(layers):
        at = slice(layer, layer + 1)
        row = layer * 10
        for k, ref in enumerate(
            (refs.ln1_gain, refs.ln1_bias, refs.b_out, refs.ln2_gain, refs.ln2_bias, refs.b_down)
        ):
            ref[at, :] = vectors[row + k : row + k + 1]
        for j in range(ff // BLOCK):
            refs.b_up[at, j * BLOCK : (j + 1) * BLOCK] = vectors[row + 6 + j : row + 7 + j]
    refs.lnf_gain[...] = vectors[VECTOR_ROWS - 4 : VECTOR_ROWS - 3]
    refs.lnf_bias[...] = vectors[VECTOR_ROWS - 3 : VECTOR_ROWS - 2]
    for j in range(classes // BLOCK):
        refs.b_head[:, j * BLOCK : (j + 1) * BLOCK] = vectors[
            VECTOR_ROWS - 2 + j : VECTOR_ROWS - 1 + j
        ]
    for i in range(count):
        loads[i].wait()
        if i >= depth:
            stores[i - depth].wait()

        def one(k, carry, slot=i % depth):
            at = pl.ds(pl.multiple_of(k * 64, 64), 64)
            refs.wide[slot, at, :] = refs.narrow[slot, at, :].astype(F32)
            return carry

        lax.fori_loop(0, BLOCK // 64, one, 0)
        stores[i].start()
        if i + depth < count:
            loads[i + depth].start()
    back_load.wait()
    sections, tokens, lanes = refs.v_back.shape
    steps, rows_dev, _ = refs.frames.shape
    rows = rows_dev // sections
    slots = tokens // rows
    total = None
    for s in range(sections):
        token = iota((steps * rows_dev, tokens), 1)
        where = iota((steps * rows_dev, tokens), 0)
        step, row = where // rows_dev, where % rows_dev
        wanted = (row - s * rows) * slots + STEP_LEN * step + 1
        mine = (row >= s * rows) & (row < (s + 1) * rows)
        hit = ((token == wanted) & mine).astype(BF)
        part = dot_nn(hit, refs.v_back[s])
        total = part if total is None else total + part
    refs.frames[...] = total.reshape(steps, rows_dev, lanes)
    for i in range(count - depth, count):
        stores[i].wait()


def body(
    codes,
    actions,
    frames,
    segment_ids,
    targets,
    codebook,
    action_table,
    slot_table,
    ln1_gain,
    ln1_bias,
    w_qkv,
    w_out,
    b_out,
    ln2_gain,
    ln2_bias,
    w_up,
    b_up,
    w_down,
    b_down,
    lnf_gain,
    lnf_bias,
    w_head,
    b_head,
):
    layers, width, ff = w_up.shape
    classes, n_codes = w_head.shape[1], codebook.shape[0]
    sections, dp_count = lax.axis_size("section"), lax.axis_size("dp")
    rows_dev, slots = codes.shape
    rows = rows_dev // sections
    tokens = rows * slots
    frames_t = jnp.transpose(frames, (1, 0, 2))
    units = make_units(layers, ff, classes, n_codes)
    line = dp_count // 2
    if sections != 4 or dp_count != 2 * line or line != 4 or units[-1][0] + units[-1][1] != sum(SIZES):
        line = 0

    vmem, hbm = pl.BlockSpec(memory_space=pltpu.VMEM), pl.BlockSpec(memory_space=pl.ANY)
    small = dict(
        codes=codes,
        actions=actions,
        segs=segment_ids,
        targets=targets,
        action_table=action_table,
        slot_table=slot_table,
        ln1_gain=ln1_gain,
        ln1_bias=ln1_bias,
        b_out=b_out,
        ln2_gain=ln2_gain,
        ln2_bias=ln2_bias,
        b_down=b_down,
        b_up=b_up,
        lnf_gain=lnf_gain[None],
        lnf_bias=lnf_bias[None],
        b_head=b_head[None],
        held_frames=frames_t,
    )
    large = dict(
        codebook=codebook, w_qkv=w_qkv, w_out=w_out, w_up=w_up, w_down=w_down, w_head=w_head
    )
    total_rows = units[-1][0] + units[-1][1]
    layer_blocks = 4 + 2 * ff // BLOCK
    early_units = classes // BLOCK + layer_blocks
    early_rows, late_rows = 0, 0
    parts, early_parts = make_parts(early_units * BLOCK)
    for i, (start, size) in enumerate(parts):
        taken = Exchange.landing_rows(size, KINDS[i])
        early_rows, late_rows = (
            early_rows + taken * (i < early_parts),
            late_rows + taken * (i >= early_parts),
        )
    outs = dict(
        result=jax.ShapeDtypeStruct((total_rows, width), BF),
        back=jax.ShapeDtypeStruct((sections, tokens, frames.shape[2]), BF),
    )
    buffers = dict(
        qkv=((layers, tokens, 3 * width), BF),
        probs=((layers, rows, HEADS // 2, 2 * slots, slots), BF),
        o=((layers, tokens, width), BF),
        hat1=((layers, tokens, width), BF),
        inv1=((layers, tokens, LANES), F32),
        hat2=((layers, tokens, width), BF),
        inv2=((layers, tokens, LANES), F32),
        m=((layers, tokens, ff), BF),
        slope=((layers, tokens, ff), BF),
        int_rows=((slots, slots), F32),
        int_cols=((slots, slots), F32),
        bias=((rows, slots, slots), F32),
        h=((tokens, width), BF),
        x1=((tokens, width), F32),
        invf=((tokens, LANES), F32),
        dz=((tokens, classes), BF),
        sums=((ACTION_ROWS, width), F32),
        big=((tokens, width), F32),
        dx1r=((tokens, width), BF),
        frames=((sections, rows * STEP_PLACES, frames.shape[2]), BF),
        sent_frames=((sections, rows * STEP_PLACES, frames.shape[2]), BF),
        first_weights=((layer_blocks * BLOCK, width), BF),
        late=((max(late_rows, layer_blocks * BLOCK + n_codes), width), BF),
        early=((early_rows, width), BF),
        total=((total_rows, width), BF),
    )
    scratch = {name: pltpu.VMEM(*what) for name, what in buffers.items()}
    held = {name: pltpu.VMEM(array.shape, array.dtype) for name, array in small.items()}
    scratch.update(
        weight_sems=pltpu.SemaphoreType.DMA((1 + classes // BLOCK + layers * layer_blocks,)),
        frame_sems=pltpu.SemaphoreType.DMA((5, sections)),
        own_sems=pltpu.SemaphoreType.DMA((len(parts),)),
        send_sems=pltpu.SemaphoreType.DMA((len(parts),)),
        recv_sems=pltpu.SemaphoreType.DMA((9 * len(parts),)),
        free_sem=pltpu.SemaphoreType.REGULAR,
        small_sems=pltpu.SemaphoreType.DMA((len(small),)),
    )
    names = tuple(large) + tuple(outs) + tuple(scratch)
    result, back = pl.pallas_call(
        functools.partial(gradient_kernel, tuple(small), names, units, line, rows),
        out_shape=tuple(outs.values()),
        in_specs=[hbm] * (len(small) + len(large)),
        out_specs=(hbm, hbm),
        scratch_shapes=list(scratch.values()) + list(held.values()),
        compiler_params=pltpu.CompilerParams(
            collective_id=0, has_side_effects=True, vmem_limit_bytes=VMEM_LIMIT
        ),
    )(*small.values(), *large.values())
    if not line:
        result = lax.psum(result, ("dp", "section"))

    depth = 12
    sources = dict(result=result, back=back)
    wide = dict(
        head=(width, classes),
        down=(layers, ff, width),
        up=(layers, width, ff),
        out=(layers, width, width),
        qkv=(layers, width, 3 * width),
        table=(n_codes, width),
        action_table=action_table.shape,
        slot_table=slot_table.shape,
        ln1_gain=(layers, width),
        ln1_bias=(layers, width),
        b_out=(layers, width),
        ln2_gain=(layers, width),
        ln2_bias=(layers, width),
        b_down=(layers, width),
        b_up=(layers, ff),
        lnf_gain=(1, width),
        lnf_bias=(1, width),
        b_head=(1, classes),
        frames=frames_t.shape,
    )
    count = len(units)
    held = dict(
        narrow=pltpu.VMEM((depth, BLOCK, width), BF),
        wide=pltpu.VMEM((depth, BLOCK, width), F32),
        tiny=pltpu.VMEM((SMALL_ROWS, width), BF),
        v_back=pltpu.VMEM(back.shape, BF),
        load_sems=pltpu.SemaphoreType.DMA((count + 2,)),
        store_sems=pltpu.SemaphoreType.DMA((count,)),
    )
    names = tuple(sources) + tuple(wide) + tuple(held)
    converted = pl.pallas_call(
        functools.partial(convert_kernel, names, units, layers, ff, classes, n_codes),
        out_shape=tuple(jax.ShapeDtypeStruct(shape, F32) for shape in wide.values()),
        in_specs=[hbm, hbm],
        out_specs=(hbm,) * 6 + (vmem,) * (len(wide) - 6),
        scratch_shapes=list(held.values()),
        compiler_params=pltpu.CompilerParams(vmem_limit_bytes=VMEM_LIMIT),
    )(result, back)

    by_name = SimpleNamespace(**dict(zip(wide, converted)))
    return (
        by_name.table,
        by_name.action_table,
        by_name.slot_table,
        by_name.ln1_gain,
        by_name.ln1_bias,
        by_name.qkv,
        by_name.out,
        by_name.b_out,
        by_name.ln2_gain,
        by_name.ln2_bias,
        by_name.up,
        by_name.b_up,
        by_name.down,
        by_name.b_down,
        by_name.lnf_gain.reshape(-1),
        by_name.lnf_bias.reshape(-1),
        by_name.head,
        by_name.b_head.reshape(-1),
        jnp.transpose(by_name.frames, (1, 0, 2)),
    )


def solution(mesh):
    placed = (
        P("dp", None),
        P("dp", None),
        P("dp", None, "section"),
        P("dp", None),
        P("dp", None),
        P(),
        P(),
        P(),
        P(),
        P(),
        P(),
        P(),
        P(),
        P(),
        P(),
        P(),
        P(),
        P(),
        P(),
        P(),
        P(),
        P(),
        P(),
    )
    return jax.shard_map(
        body,
        mesh=mesh,
        in_specs=placed,
        out_specs=(
            P(),
            P(),
            P(),
            P(),
            P(),
            P(),
            P(),
            P(),
            P(),
            P(),
            P(),
            P(),
            P(),
            P(),
            P(),
            P(),
            P(),
            P(),
            P("dp", None, "section"),
        ),
        check_vma=False,
    )
```
